32 devices in a mesh: seq: 8 (over z, y), item: 4 (over x, core).
Axes of the slice: x: 2, y: 2, z: 4, core: 2. Of those that a mesh axis runs over, the one named last changes fastest.
Arguments:
- inputs: float32 [1024, 24, 768], P('seq', 'item'), may hold values from -6 to 6
- w_in: float32 [768, 3072], replicated, may hold values from -0.21875 to 0.21875
- c_in: float32 [3072], replicated, may hold values from -3 to 3
- w_out: float32 [3072, 768], replicated, may hold values from -0.109375 to 0.109375
- c_out: float32 [768], replicated, may hold values from -3 to 3
- gain_mix: float32 [768], replicated, may hold values from 0.5 to 1.5
- bias_mix: float32 [768], replicated, may hold values from -3 to 3
- gain_out: float32 [768], replicated, may hold values from 0.5 to 1.5
- bias_out: float32 [768], replicated, may hold values from -3 to 3
- cotangent: float32 [1024, 24, 768], P('seq', 'item'), may hold values from -6 to 6
Outputs:
- output: float32 [1024, 24, 768], P('seq', 'item')
- grad_inputs: float32 [1024, 24, 768], P('seq', 'item')
- grad_w_in: float32 [768, 3072], P('seq')
- grad_c_in: float32 [3072], P('seq')
- grad_w_out: float32 [3072, 768], P('seq')
- grad_c_out: float32 [768], P('seq')
- grad_gain_mix: float32 [768], P('seq')
- grad_bias_mix: float32 [768], P('seq')
- grad_gain_out: float32 [768], P('seq')
- grad_bias_out: float32 [768], P('seq')
The draws below stay inside these ranges and needn't reach their ends.
All inputs are finite; a program needn't handle non-finite values.
Results may differ from the reference program's by a relative error of at most 0.015.
Values may be sent and summed in bfloat16 or wider, within the bound.
A program may use at most 256 MiB of HBM per device.

```python
import math
import jax
import jax.numpy as jnp
from jax import lax

D = 768
FF = 3072
LENGTH = 1024
SEQUENCES = 24


def strengthened(drawn, rng, source, target, parts, factor):
    def block_of(axis_at):
        return (jnp.arange(drawn.shape[axis_at]) // (drawn.shape[axis_at] // parts)).reshape((-1,) + (1,) * (drawn.ndim - 1 - axis_at))

    near = jax.random.permutation(rng, parts)[block_of(target)]
    other_side = (block_of(target) + parts // 2) % parts
    return jnp.where((block_of(source) == near) | (block_of(source) == other_side), factor * drawn, drawn)


def shard_levels(stream_key, extent, pieces, least, top_value):
    def one(position, blocks):
        steps = jax.random.uniform(jax.random.fold_in(jax.random.fold_in(stream_key, 6), position), (blocks,), jnp.float32, least / len(pieces), top_value / len(pieces))
        return jnp.repeat(jnp.exp(steps), extent[position] // blocks).reshape((-1,) + (1,) * (len(extent) - position - 1))

    gain = one(*pieces[0])
    for cut in pieces[1:]:
        gain = gain * one(*cut)
    return gain


def bell_draw(key, shape, deviation, most, cuts=(), held_as=jnp.bfloat16):
    gain = shard_levels(key, shape, cuts, -0.22, 0.18) if cuts else 1.0
    drawn = jax.random.normal(key, shape, jnp.float32) * deviation * gain
    return jnp.minimum(jnp.maximum(drawn, -most), most).astype(held_as)


def gaussian_with(stream_key, shape, spread, bound, shards, heavy, kind=jnp.bfloat16):
    entries = spread * jax.random.normal(stream_key, shape, jnp.float32)
    if shards:
        entries = entries * shard_levels(stream_key, shape, shards, -0.22, 0.18)
    return jnp.clip(strengthened(entries, jax.random.fold_in(stream_key, 3), *heavy), -bound, bound).astype(kind)


def setup_inputs(seed: int = 0) -> dict:
    key_list = jax.random.split(jax.random.key(seed), 11)
    return {
        "inputs": bell_draw(key_list[0], (LENGTH, SEQUENCES, D), 1.0, 6.0, ((0, 8), (1, 4)), jnp.float32),
        "w_in": bell_draw(key_list[1], (D, FF), D ** -0.5, 0.21875, (), jnp.float32),
        "c_in": bell_draw(key_list[2], (FF,), 0.5, 3.0, (), jnp.float32),
        "w_out": bell_draw(key_list[3], (FF, D), FF ** -0.5, 0.109375, (), jnp.float32),
        "c_out": bell_draw(key_list[4], (D,), 0.5, 3.0, (), jnp.float32),
        "gain_mix": jnp.clip(1.0 + 0.1 * jax.random.normal(key_list[5], (D,), jnp.float32), 0.5, 1.5),
        "bias_mix": bell_draw(key_list[6], (D,), 0.5, 3.0, (), jnp.float32),
        "gain_out": jnp.clip(1.0 + 0.1 * jax.random.normal(key_list[7], (D,), jnp.float32), 0.5, 1.5),
        "bias_out": bell_draw(key_list[8], (D,), 0.5, 3.0, (), jnp.float32),
        "cotangent": gaussian_with(key_list[9], (LENGTH, SEQUENCES, D), 1.0, 6.0, ((0, 8), (1, 4)), (0, 2, 8, 2.0), jnp.float32),
    }


@jax.custom_vjp
def low(v):
    return lax.optimization_barrier(v.astype(jnp.bfloat16)).astype(jnp.float32)

@jax.custom_vjp
def low_back(v):
    return v

def low_keep(v):
    return (low(v), None)

def low_pass(kept, grad):
    return (grad,)

def back_keep(v):
    return (v, None)

def back_low(kept, grad):
    return (low(grad),)
low.defvjp(low_keep, low_pass)
low_back.defvjp(back_keep, back_low)

def tables(period):
    indices = jnp.arange(period, dtype=jnp.int32)
    products = indices[:, None] * indices[None, :] % period
    angles = products.astype(jnp.float32) * (2.0 * math.pi / period)
    return (low(jnp.cos(angles)), low(jnp.sin(angles)))

def layer_norm(values, scales, shifts):
    average = lax.optimization_barrier(jnp.mean(values, axis=-1, keepdims=True))
    centered = values - average
    variance = lax.optimization_barrier(jnp.mean(centered * centered, axis=-1, keepdims=True))
    return centered * lax.rsqrt(variance + 1e-05) * scales + shifts

def forward(piece, w_in, c_in, w_out, c_out, gain_mix, bias_mix, gain_out, bias_out, cos_hid, sin_hid, cos_seq, sin_seq):
    highest = lax.Precision.HIGHEST
    unit_scale = 1.0 / math.sqrt(LENGTH * D)
    piece_low = low(piece)
    cos_part = low_back(low(jnp.dot(piece_low, cos_hid, precision=highest)))
    sin_part = low_back(low(jnp.dot(piece_low, sin_hid, precision=highest)))
    mixed = (jnp.dot(cos_seq, cos_part, precision=highest) - jnp.dot(sin_seq, sin_part, precision=highest)) * unit_scale
    mixed = low_back(mixed)
    hidden = layer_norm(piece + mixed, gain_mix, bias_mix)
    pre = low_back(jnp.dot(low(hidden), low(w_in), precision=highest) + c_in)
    act = low(jax.nn.gelu(pre, approximate=False))
    branch = low_back(jnp.dot(act, low(w_out), precision=highest) + c_out)
    return layer_norm(hidden + branch, gain_out, bias_out)

def reference(inputs, w_in, c_in, w_out, c_out, gain_mix, bias_mix, gain_out, bias_out, cotangent):
    cos_hid, sin_hid = tables(D)
    cos_seq, sin_seq = tables(LENGTH)
    weights = (w_in, c_in, w_out, c_out, gain_mix, bias_mix, gain_out, bias_out)

    def per_sequence(totals, slices):
        piece, cot_piece = slices

        def layer(sequence, *params):
            return forward(sequence, *params, cos_hid, sin_hid, cos_seq, sin_seq)
        result, pullback = jax.vjp(layer, piece, *weights)
        gradients = pullback(cot_piece)
        totals = tuple((first + second for first, second in zip(totals, gradients[1:])))
        return (totals, (result, gradients[0]))
    initial = tuple((jnp.zeros_like(weight) for weight in weights))
    totals, (results, grad_pieces) = lax.scan(per_sequence, initial, (jnp.swapaxes(inputs, 0, 1), jnp.swapaxes(cotangent, 0, 1)))
    return (jnp.swapaxes(results, 0, 1), jnp.swapaxes(grad_pieces, 0, 1), totals[0], totals[1], totals[2], totals[3], totals[4], totals[5], totals[6], totals[7])
```

```python
import math

import jax
import jax.numpy as jnp
import numpy as np
from jax import lax
from jax.sharding import PartitionSpec as P


def table_block(row_ids, col_ids, period):
    products = row_ids[:, None] * col_ids[None, :] % period
    angles = products.astype(jnp.float32) * (2.0 * math.pi / period)
    return (jnp.cos(angles).astype(jnp.bfloat16), jnp.sin(angles).astype(jnp.bfloat16))


def plain_dot(left, right):
    return jnp.dot(left, right, preferred_element_type=jnp.float32)


def rows_dot(left, right):
    return lax.dot_general(
        left, right, (((0,), (0,)), ((), ())), preferred_element_type=jnp.float32
    )


def cols_dot(left, right):
    return lax.dot_general(
        left, right, (((1,), (1,)), ((), ())), preferred_element_type=jnp.float32
    )


def layer_norm(values, scales, shifts):
    average = jnp.mean(values, axis=-1, keepdims=True)
    centered = values - average
    variance = jnp.mean(centered * centered, axis=-1, keepdims=True)
    return centered * lax.rsqrt(variance + 1e-05) * scales + shifts


def gelu_exact(values):
    return jax.nn.gelu(values, approximate=False)


def gather_body(inputs, w_in, c_in, w_out, c_out, gain_mix, bias_mix, gain_out, bias_out, cotangent):
    local_len, per_dev, features = inputs.shape
    merged = per_dev * features
    period = local_len * lax.axis_size("seq")
    unit_scale = 1.0 / math.sqrt(period * features)
    own_rows = lax.axis_index("seq") * local_len + jnp.arange(local_len, dtype=jnp.int32)
    feat_ids = jnp.arange(features, dtype=jnp.int32)
    cos_hid, sin_hid = table_block(feat_ids, feat_ids, features)
    tokens = inputs.reshape(-1, features)
    tokens_low = tokens.astype(jnp.bfloat16)
    cos_part = (
        plain_dot(tokens_low, cos_hid).astype(jnp.bfloat16).reshape(local_len, per_dev, features)
    )
    sin_part = (
        plain_dot(tokens_low, sin_hid).astype(jnp.bfloat16).reshape(local_len, per_dev, features)
    )
    pieces = (
        lax.all_gather(cos_part, "seq", axis=0, tiled=True),
        lax.all_gather(sin_part, "seq", axis=0, tiled=True),
    )
    col_ids = jnp.arange(pieces[0].shape[0], dtype=jnp.int32)
    cos_blk, sin_blk = table_block(own_rows, col_ids, period)
    mixed = plain_dot(cos_blk, pieces[0].reshape(pieces[0].shape[0], -1)) - plain_dot(
        sin_blk, pieces[1].reshape(pieces[1].shape[0], -1)
    )
    mixed = (mixed * unit_scale).reshape(-1, features)
    hidden, pull_mix = jax.vjp(layer_norm, tokens + mixed, gain_mix, bias_mix)
    hidden_low = hidden.astype(jnp.bfloat16)
    w_in_low = w_in.astype(jnp.bfloat16)
    w_out_low = w_out.astype(jnp.bfloat16)
    pre = plain_dot(hidden_low, w_in_low) + c_in
    act, pull_gelu = jax.vjp(gelu_exact, pre)
    act_low = act.astype(jnp.bfloat16)
    branch = plain_dot(act_low, w_out_low) + c_out
    output, pull_out = jax.vjp(layer_norm, hidden + branch, gain_out, bias_out)
    g_sum2, grad_gain_out, grad_bias_out = pull_out(cotangent.reshape(-1, features))
    g_branch = g_sum2.astype(jnp.bfloat16)
    grad_c_out = jnp.sum(g_branch.astype(jnp.float32), axis=0)
    grad_w_out = rows_dot(act_low, g_branch)
    (g_act,) = pull_gelu(cols_dot(g_branch, w_out_low))
    g_pre = g_act.astype(jnp.bfloat16)
    grad_c_in = jnp.sum(g_pre.astype(jnp.float32), axis=0)
    grad_w_in = rows_dot(hidden_low, g_pre)
    g_hidden = g_sum2 + cols_dot(g_pre, w_in_low)
    g_sum1, grad_gain_mix, grad_bias_mix = pull_mix(g_hidden)
    g_mixed = g_sum1.astype(jnp.bfloat16).reshape(local_len, per_dev, features)
    empty = jnp.zeros((local_len, merged), jnp.float32)
    piece = lax.all_gather(g_mixed, "seq", axis=0, tiled=True)
    row_ids = jnp.arange(piece.shape[0], dtype=jnp.int32)
    cos_blk, sin_blk = table_block(row_ids, own_rows, period)
    flat = piece.reshape(piece.shape[0], -1)
    cycle_gc = rows_dot(cos_blk, flat)
    cycle_gs = (empty, empty)[1] - rows_dot(sin_blk, flat)
    g_cos = (cycle_gc * unit_scale).astype(jnp.bfloat16).reshape(-1, features)
    g_sin = (cycle_gs * unit_scale).astype(jnp.bfloat16).reshape(-1, features)
    grad_inputs = g_sum1 + cols_dot(g_cos, cos_hid) + cols_dot(g_sin, sin_hid)
    shards = (
        lax.psum_scatter(
            grad_w_in.astype(jnp.bfloat16), "seq", scatter_dimension=0, tiled=True
        ).astype(jnp.float32),
        lax.psum_scatter(
            grad_c_in.astype(jnp.bfloat16), "seq", scatter_dimension=0, tiled=True
        ).astype(jnp.float32),
        lax.psum_scatter(
            grad_w_out.astype(jnp.bfloat16), "seq", scatter_dimension=0, tiled=True
        ).astype(jnp.float32),
        lax.psum_scatter(
            grad_c_out.astype(jnp.bfloat16), "seq", scatter_dimension=0, tiled=True
        ).astype(jnp.float32),
        lax.psum_scatter(
            grad_gain_mix.astype(jnp.bfloat16), "seq", scatter_dimension=0, tiled=True
        ).astype(jnp.float32),
        lax.psum_scatter(
            grad_bias_mix.astype(jnp.bfloat16), "seq", scatter_dimension=0, tiled=True
        ).astype(jnp.float32),
        lax.psum_scatter(
            grad_gain_out.astype(jnp.bfloat16), "seq", scatter_dimension=0, tiled=True
        ).astype(jnp.float32),
        lax.psum_scatter(
            grad_bias_out.astype(jnp.bfloat16), "seq", scatter_dimension=0, tiled=True
        ).astype(jnp.float32),
    )
    summed = (
        lax.psum(shards[0].astype(jnp.bfloat16), "item").astype(jnp.float32),
        lax.psum(shards[1].astype(jnp.bfloat16), "item").astype(jnp.float32),
        lax.psum(shards[2].astype(jnp.bfloat16), "item").astype(jnp.float32),
        lax.psum(shards[3].astype(jnp.bfloat16), "item").astype(jnp.float32),
        lax.psum(shards[4].astype(jnp.bfloat16), "item").astype(jnp.float32),
        lax.psum(shards[5].astype(jnp.bfloat16), "item").astype(jnp.float32),
        lax.psum(shards[6].astype(jnp.bfloat16), "item").astype(jnp.float32),
        lax.psum(shards[7].astype(jnp.bfloat16), "item").astype(jnp.float32),
    )
    return (
        output.reshape(inputs.shape),
        grad_inputs.reshape(inputs.shape),
        summed[0],
        summed[1],
        summed[2],
        summed[3],
        summed[4],
        summed[5],
        summed[6],
        summed[7],
    )


def packed_tables(features, parts):
    half = features // 2
    share = half // parts
    index = np.arange(features)
    forward = np.zeros((features, features), np.float32)
    unpack = np.zeros((features, features), np.float32)
    for low in range(half):
        block, place = divmod(low, share)
        cos_slot = block * 2 * share + place
        sin_slot = cos_slot + share
        angles = (index * low % features).astype(np.float32) * np.float32(2.0 * math.pi / features)
        forward[cos_slot] = np.cos(angles)
        unpack[cos_slot, low] = 1.0
        if low:
            unpack[cos_slot, features - low] = 1.0
            forward[sin_slot] = np.sin(angles)
            unpack[sin_slot, low] = -1.0
            unpack[sin_slot, features - low] = 1.0
        else:
            forward[sin_slot] = 1.0 - 2.0 * (index % 2)
            unpack[sin_slot, half] = 1.0
    return forward.astype(jnp.bfloat16), unpack.astype(jnp.bfloat16)


def seq_tables(period):
    index = np.arange(period)
    angles = (index[:, None] * index[None, :] % period).astype(np.float32)
    angles = angles * np.float32(2.0 * math.pi / period)
    return np.cos(angles).astype(jnp.bfloat16), np.sin(angles).astype(jnp.bfloat16)


def mix(values, forward, unpack, cos_seq, sin_seq):
    features = values.shape[2]
    share = features // lax.axis_size("seq") // 2
    unit_scale = 1.0 / math.sqrt(cos_seq.shape[0] * features)
    packed = jnp.einsum("gf,spf->gsp", forward, values, preferred_element_type=jnp.float32)
    packed = packed.astype(jnp.bfloat16)
    packed = lax.all_to_all(packed, "seq", 0, 2, tiled=True)
    by_cos = plain_dot(packed[:share], cos_seq)
    by_sin = plain_dot(packed[share:], sin_seq)
    middle = plain_dot(packed[share], cos_seq)
    first = jnp.where(lax.axis_index("seq") == 0, middle, by_sin[0])
    turned = jnp.concatenate([by_cos, first[None], by_sin[1:]], axis=0) * unit_scale
    turned = lax.all_to_all(turned.astype(jnp.bfloat16), "seq", 2, 0, tiled=True)
    return jnp.einsum("gsp,gl->spl", turned, unpack, preferred_element_type=jnp.float32)


def exchange_body(inputs, w_in, c_in, w_out, c_out, gain_mix, bias_mix, gain_out, bias_out, cotangent):
    local_len, per_dev, features = inputs.shape
    shape = (per_dev, local_len, features)
    period = local_len * lax.axis_size("seq")
    forward, unpack = packed_tables(features, lax.axis_size("seq"))
    cos_seq, sin_seq = seq_tables(period)
    held = jnp.swapaxes(inputs, 0, 1)
    mixed = mix(held.astype(jnp.bfloat16), forward, unpack, cos_seq, sin_seq)
    tokens = held.reshape(-1, features)
    mixed = mixed.reshape(-1, features)
    hidden, pull_mix = jax.vjp(layer_norm, tokens + mixed, gain_mix, bias_mix)
    hidden_low = hidden.astype(jnp.bfloat16)
    w_in_low = w_in.astype(jnp.bfloat16)
    w_out_low = w_out.astype(jnp.bfloat16)
    pre = plain_dot(hidden_low, w_in_low) + c_in
    act, pull_gelu = jax.vjp(gelu_exact, pre)
    act_low = act.astype(jnp.bfloat16)
    branch = plain_dot(act_low, w_out_low) + c_out
    output, pull_out = jax.vjp(layer_norm, hidden + branch, gain_out, bias_out)
    cot = jnp.swapaxes(cotangent, 0, 1).reshape(-1, features)
    g_sum2, grad_gain_out, grad_bias_out = pull_out(cot)
    g_branch = g_sum2.astype(jnp.bfloat16)
    grad_c_out = jnp.sum(g_branch.astype(jnp.float32), axis=0)
    grad_w_out = rows_dot(act_low, g_branch)
    (g_act,) = pull_gelu(cols_dot(g_branch, w_out_low))
    g_pre = g_act.astype(jnp.bfloat16)
    grad_c_in = jnp.sum(g_pre.astype(jnp.float32), axis=0)
    grad_w_in = rows_dot(hidden_low, g_pre)
    g_hidden = g_sum2 + cols_dot(g_pre, w_in_low)
    g_sum1, grad_gain_mix, grad_bias_mix = pull_mix(g_hidden)
    back = mix(g_sum1.astype(jnp.bfloat16).reshape(shape), forward, unpack, cos_seq, sin_seq)
    grad_inputs = g_sum1.reshape(shape) + back

    def reduce_matrix(grad):
        cut = lax.psum_scatter(grad.astype(jnp.bfloat16), "item", scatter_dimension=1, tiled=True)
        cut = lax.psum_scatter(cut, "seq", scatter_dimension=0, tiled=True)
        return lax.all_gather(cut, "item", axis=1, tiled=True).astype(jnp.float32)

    parts = lax.axis_size("seq")
    vectors = (grad_c_in, grad_c_out, grad_gain_mix, grad_bias_mix, grad_gain_out, grad_bias_out)
    joined = jnp.concatenate([v.reshape(parts, -1) for v in vectors], axis=1)
    joined = lax.psum(joined, ("seq", "item"))[lax.axis_index("seq")]
    cuts, at = [], 0
    for v in vectors:
        cuts.append(joined[at : at + v.shape[0] // parts])
        at += v.shape[0] // parts
    return (
        jnp.swapaxes(output.reshape(shape), 0, 1),
        jnp.swapaxes(grad_inputs, 0, 1),
        reduce_matrix(grad_w_in),
        cuts[0],
        reduce_matrix(grad_w_out),
        *cuts[1:],
    )


def body(inputs, *rest):
    if inputs.shape[0] * lax.axis_size("seq") > 2048:
        return gather_body(inputs, *rest)
    return exchange_body(inputs, *rest)


def solution(mesh):
    placed = (
        P("seq", "item", None),
        P(),
        P(),
        P(),
        P(),
        P(),
        P(),
        P(),
        P(),
        P("seq", "item", None),
    )
    return jax.shard_map(
        body,
        mesh=mesh,
        in_specs=placed,
        out_specs=(
            P("seq", "item", None),
            P("seq", "item", None),
            P("seq", None),
            P("seq"),
            P("seq", None),
            P("seq"),
            P("seq"),
            P("seq"),
            P("seq"),
            P("seq"),
        ),
        check_vma=False,
    )
```

```python
import math

import jax
import jax.numpy as jnp
import numpy as np
from jax import lax
from jax.experimental import pallas as pl
from jax.experimental.pallas import tpu as pltpu
from jax.sharding import PartitionSpec as P


def table_block(row_ids, col_ids, period):
    products = row_ids[:, None] * col_ids[None, :] % period
    angles = products.astype(jnp.float32) * (2.0 * math.pi / period)
    return (jnp.cos(angles).astype(jnp.bfloat16), jnp.sin(angles).astype(jnp.bfloat16))


def plain_dot(left, right):
    return jnp.dot(left, right, preferred_element_type=jnp.float32)


def rows_dot(left, right):
    return lax.dot_general(
        left, right, (((0,), (0,)), ((), ())), preferred_element_type=jnp.float32
    )


def cols_dot(left, right):
    return lax.dot_general(
        left, right, (((1,), (1,)), ((), ())), preferred_element_type=jnp.float32
    )


def layer_norm(values, scales, shifts):
    average = jnp.mean(values, axis=-1, keepdims=True)
    centered = values - average
    variance = jnp.mean(centered * centered, axis=-1, keepdims=True)
    return centered * lax.rsqrt(variance + 1e-05) * scales + shifts


def gelu_exact(values):
    return jax.nn.gelu(values, approximate=False)


def gather_body(inputs, w_in, c_in, w_out, c_out, gain_mix, bias_mix, gain_out, bias_out, cotangent):
    local_len, per_dev, features = inputs.shape
    merged = per_dev * features
    period = local_len * lax.axis_size("seq")
    unit_scale = 1.0 / math.sqrt(period * features)
    own_rows = lax.axis_index("seq") * local_len + jnp.arange(local_len, dtype=jnp.int32)
    feat_ids = jnp.arange(features, dtype=jnp.int32)
    cos_hid, sin_hid = table_block(feat_ids, feat_ids, features)
    tokens = inputs.reshape(-1, features)
    tokens_low = tokens.astype(jnp.bfloat16)
    cos_part = (
        plain_dot(tokens_low, cos_hid).astype(jnp.bfloat16).reshape(local_len, per_dev, features)
    )
    sin_part = (
        plain_dot(tokens_low, sin_hid).astype(jnp.bfloat16).reshape(local_len, per_dev, features)
    )
    pieces = (
        lax.all_gather(cos_part, "seq", axis=0, tiled=True),
        lax.all_gather(sin_part, "seq", axis=0, tiled=True),
    )
    col_ids = jnp.arange(pieces[0].shape[0], dtype=jnp.int32)
    cos_blk, sin_blk = table_block(own_rows, col_ids, period)
    mixed = plain_dot(cos_blk, pieces[0].reshape(pieces[0].shape[0], -1)) - plain_dot(
        sin_blk, pieces[1].reshape(pieces[1].shape[0], -1)
    )
    mixed = (mixed * unit_scale).reshape(-1, features)
    hidden, pull_mix = jax.vjp(layer_norm, tokens + mixed, gain_mix, bias_mix)
    hidden_low = hidden.astype(jnp.bfloat16)
    w_in_low = w_in.astype(jnp.bfloat16)
    w_out_low = w_out.astype(jnp.bfloat16)
    pre = plain_dot(hidden_low, w_in_low) + c_in
    act, pull_gelu = jax.vjp(gelu_exact, pre)
    act_low = act.astype(jnp.bfloat16)
    branch = plain_dot(act_low, w_out_low) + c_out
    output, pull_out = jax.vjp(layer_norm, hidden + branch, gain_out, bias_out)
    g_sum2, grad_gain_out, grad_bias_out = pull_out(cotangent.reshape(-1, features))
    g_branch = g_sum2.astype(jnp.bfloat16)
    grad_c_out = jnp.sum(g_branch.astype(jnp.float32), axis=0)
    grad_w_out = rows_dot(act_low, g_branch)
    (g_act,) = pull_gelu(cols_dot(g_branch, w_out_low))
    g_pre = g_act.astype(jnp.bfloat16)
    grad_c_in = jnp.sum(g_pre.astype(jnp.float32), axis=0)
    grad_w_in = rows_dot(hidden_low, g_pre)
    g_hidden = g_sum2 + cols_dot(g_pre, w_in_low)
    g_sum1, grad_gain_mix, grad_bias_mix = pull_mix(g_hidden)
    g_mixed = g_sum1.astype(jnp.bfloat16).reshape(local_len, per_dev, features)
    empty = jnp.zeros((local_len, merged), jnp.float32)
    piece = lax.all_gather(g_mixed, "seq", axis=0, tiled=True)
    row_ids = jnp.arange(piece.shape[0], dtype=jnp.int32)
    cos_blk, sin_blk = table_block(row_ids, own_rows, period)
    flat = piece.reshape(piece.shape[0], -1)
    cycle_gc = rows_dot(cos_blk, flat)
    cycle_gs = (empty, empty)[1] - rows_dot(sin_blk, flat)
    g_cos = (cycle_gc * unit_scale).astype(jnp.bfloat16).reshape(-1, features)
    g_sin = (cycle_gs * unit_scale).astype(jnp.bfloat16).reshape(-1, features)
    grad_inputs = g_sum1 + cols_dot(g_cos, cos_hid) + cols_dot(g_sin, sin_hid)
    shards = (
        lax.psum_scatter(
            grad_w_in.astype(jnp.bfloat16), "seq", scatter_dimension=0, tiled=True
        ).astype(jnp.float32),
        lax.psum_scatter(
            grad_c_in.astype(jnp.bfloat16), "seq", scatter_dimension=0, tiled=True
        ).astype(jnp.float32),
        lax.psum_scatter(
            grad_w_out.astype(jnp.bfloat16), "seq", scatter_dimension=0, tiled=True
        ).astype(jnp.float32),
        lax.psum_scatter(
            grad_c_out.astype(jnp.bfloat16), "seq", scatter_dimension=0, tiled=True
        ).astype(jnp.float32),
        lax.psum_scatter(
            grad_gain_mix.astype(jnp.bfloat16), "seq", scatter_dimension=0, tiled=True
        ).astype(jnp.float32),
        lax.psum_scatter(
            grad_bias_mix.astype(jnp.bfloat16), "seq", scatter_dimension=0, tiled=True
        ).astype(jnp.float32),
        lax.psum_scatter(
            grad_gain_out.astype(jnp.bfloat16), "seq", scatter_dimension=0, tiled=True
        ).astype(jnp.float32),
        lax.psum_scatter(
            grad_bias_out.astype(jnp.bfloat16), "seq", scatter_dimension=0, tiled=True
        ).astype(jnp.float32),
    )
    summed = (
        lax.psum(shards[0].astype(jnp.bfloat16), "item").astype(jnp.float32),
        lax.psum(shards[1].astype(jnp.bfloat16), "item").astype(jnp.float32),
        lax.psum(shards[2].astype(jnp.bfloat16), "item").astype(jnp.float32),
        lax.psum(shards[3].astype(jnp.bfloat16), "item").astype(jnp.float32),
        lax.psum(shards[4].astype(jnp.bfloat16), "item").astype(jnp.float32),
        lax.psum(shards[5].astype(jnp.bfloat16), "item").astype(jnp.float32),
        lax.psum(shards[6].astype(jnp.bfloat16), "item").astype(jnp.float32),
        lax.psum(shards[7].astype(jnp.bfloat16), "item").astype(jnp.float32),
    )
    return (
        output.reshape(inputs.shape),
        grad_inputs.reshape(inputs.shape),
        summed[0],
        summed[1],
        summed[2],
        summed[3],
        summed[4],
        summed[5],
        summed[6],
        summed[7],
    )


def packed_tables(features, parts):
    half = features // 2
    share = half // parts
    index = np.arange(features)
    forward = np.zeros((features, features), np.float32)
    unpack = np.zeros((features, features), np.float32)
    for low in range(half):
        block, place = divmod(low, share)
        cos_slot = block * 2 * share + place
        sin_slot = cos_slot + share
        angles = (index * low % features).astype(np.float32) * np.float32(2.0 * math.pi / features)
        forward[cos_slot] = np.cos(angles)
        unpack[cos_slot, low] = 1.0
        if low:
            unpack[cos_slot, features - low] = 1.0
            forward[sin_slot] = np.sin(angles)
            unpack[sin_slot, low] = -1.0
            unpack[sin_slot, features - low] = 1.0
        else:
            forward[sin_slot] = 1.0 - 2.0 * (index % 2)
            unpack[sin_slot, half] = 1.0
    return forward.astype(jnp.bfloat16), unpack.astype(jnp.bfloat16)


def seq_tables(period):
    index = np.arange(period)
    angles = (index[:, None] * index[None, :] % period).astype(np.float32)
    angles = angles * np.float32(2.0 * math.pi / period)
    return np.cos(angles).astype(jnp.bfloat16), np.sin(angles).astype(jnp.bfloat16)


MESH = pl.DeviceIdType.MESH
CHUNKS = 3
BF16, F32 = jnp.bfloat16, jnp.float32


def dot(left, right, left_dim, right_dim):
    return lax.dot_general(
        left, right, (((left_dim,), (right_dim,)), ((), ())), preferred_element_type=F32
    )


def row_mean(values):
    return jnp.mean(values, axis=-1, keepdims=True)


def layer_kernel(
    x_hbm, cot_hbm, win_hbm, wout_hbm, prm_hbm, fwd_hbm, unp_hbm, cos_hbm, sin_hbm,
    out_hbm, gin_hbm, gmat_hbm, gvec_ref,
    fwd_v, unp_v, cos_v, sin_v, prm_v, xbuf, cotb, wbuf, stage,
    ysend, yrecv, zsend, zrecv, actb, gpb, hb, gbb, dgb, acc, r1b, ostage, vacc,
    recv1, recv2, recv3, recv4, recv5, recv6, vsend, vrecv, vmid, vlast,
    ld_sem, x_sem, cot_sem, stg_sem, a_send, a_recv, b_send, b_recv, out_sem,
    red_send, red_recv, gat_send, gat_recv, v_send, v_recv,
):
    chunks, rows, features = xbuf.shape
    per_chunk, share, period = yrecv.shape[2], yrecv.shape[3], yrecv.shape[4]
    own_len = period // 8
    half = share // 2
    unit_scale = 1.0 / math.sqrt(period * features)

    me, item = lax.axis_index("seq"), lax.axis_index("item")
    peers = [(lax.rem(me + k, 8), item) for k in range(1, 8)]
    z_lo, y_at = lax.rem(lax.div(me, 2), 2), lax.rem(me, 2)
    z_at, z_hi = lax.div(me, 2), lax.div(me, 4)
    core, x_at = lax.rem(item, 2), lax.div(item, 2)
    core_peer = (me, item + 1 - 2 * core)
    x_peer = (me, item + 2 - 4 * x_at)
    far_peer = (me, lax.rem(item + 2, 4) + 1 - 2 * core)
    y_peer = (me + 1 - 2 * y_at, item)
    za_peer = (me + 2 - 4 * z_lo, item)
    zb_peer = (me + 4 - 8 * z_hi, item)

    def remote(src, dst, send, recv, peer):
        return pltpu.make_async_remote_copy(
            src_ref=src, dst_ref=dst, send_sem=send, recv_sem=recv, device_id=peer, device_id_type=MESH
        )

    def wait_bytes(ref, sem):
        pltpu.make_async_copy(ref, ref, sem).wait()

    tables = [
        pltpu.make_async_copy(src, dst, ld_sem.at[i])
        for i, (src, dst) in enumerate(
            [(fwd_hbm, fwd_v), (prm_hbm, prm_v), (cos_hbm, cos_v), (sin_hbm, sin_v), (unp_hbm, unp_v)]
        )
    ]
    x_loads = [pltpu.make_async_copy(x_hbm.at[c], xbuf.at[c], x_sem.at[c]) for c in range(chunks)]
    cot_loads = [pltpu.make_async_copy(cot_hbm.at[c], cotb.at[c], cot_sem.at[c]) for c in range(chunks)]
    x_loads[0].start()
    tables[0].start()
    for load in x_loads[1:] + tables[1:]:
        load.start()

    barrier = pltpu.get_barrier_semaphore()
    everyone = peers + [core_peer, x_peer, far_peer]
    for peer in everyone:
        pl.semaphore_signal(barrier, inc=1, device_id=peer, device_id_type=MESH)

    slots, piece = stage.shape[0], stage.shape[1]
    per_block = features // piece
    steps = 8 * per_block

    def weight_load(step, part, slot):
        block, at = lax.div(step, per_block), lax.rem(step, per_block) * piece
        if part == 0:
            cols = pl.ds(pl.multiple_of(block * features, features), features)
            src = win_hbm.at[pl.ds(pl.multiple_of(at, piece), piece), cols]
        else:
            src = wout_hbm.at[pl.ds(pl.multiple_of(block * features + at, piece), piece), :]
        return pltpu.make_async_copy(src, stage.at[slot], stg_sem.at[slot])

    def cast_weights(part):
        total = 4 * per_block
        groups = piece // share

        def one(step, carry):
            slot = lax.rem(step, slots)
            weight_load(step, part, slot).wait()
            block, at = lax.div(step, per_block), lax.rem(step, per_block) * groups
            value = stage[slot].astype(BF16)
            for g in range(groups):
                where = at + g
                wbuf[4 * part + block, lax.div(where, 2), lax.rem(where, 2)] = value[g * share : (g + 1) * share]

            @pl.when(step + slots < total)
            def _():
                weight_load(step + slots, part, slot).start()

            return carry

        lax.fori_loop(0, total, one, 0)

    def first_loads(part):
        for slot in range(slots):
            weight_load(jnp.int32(slot), part, jnp.int32(slot)).start()

    def block_of(index):
        return wbuf[index].reshape(features, features)

    def to_owners(turn, c, low):
        packed = dot(fwd_v[...], low, 1, 1).astype(BF16)
        for s in range(per_chunk):
            ysend[c, s] = packed[:, s * own_len : (s + 1) * own_len]
        mine = pl.ds(pl.multiple_of(me * own_len, own_len), own_len)
        for peer in peers:
            to = pl.ds(pl.multiple_of(peer[0] * share, share), share)
            remote(
                ysend.at[c, :, to, :], yrecv.at[turn, c, :, :, mine], a_send.at[turn, c], a_recv.at[turn, c], peer
            ).start()
        own = pl.ds(pl.multiple_of(me * share, share), share)
        pltpu.make_async_copy(ysend.at[c, :, own, :], yrecv.at[turn, c, :, :, mine], a_recv.at[turn, c]).start()

    def owners_sent(turn, c):
        wait_bytes(ysend.at[c, :, pl.ds(0, 7 * share), :], a_send.at[turn, c])

    def turn_and_return(turn, c):
        wait_bytes(yrecv.at[turn, c], a_recv.at[turn, c])
        held = yrecv[turn, c]
        cos_rows = held[:, :half].reshape(per_chunk * half, period)
        sin_rows = held[:, half:].reshape(per_chunk * half, period)
        mid_rows = held[:, half : half + 16].reshape(per_chunk * 16, period)
        by_cos = dot(cos_rows, cos_v[...], 1, 0) * unit_scale
        by_sin = dot(sin_rows, sin_v[...], 1, 0) * unit_scale
        by_mid = dot(mid_rows, cos_v[...], 1, 0) * unit_scale
        top = lax.broadcasted_iota(jnp.int32, (16, period), 0) == 0
        top = jnp.logical_and(top, me == 0)
        for s in range(per_chunk):
            zsend[c, s, :half] = by_cos[s * half : (s + 1) * half].astype(BF16)
            sin_part = by_sin[s * half : (s + 1) * half]
            zsend[c, s, half : half + 16] = jnp.where(
                top, by_mid[s * 16 : (s + 1) * 16], sin_part[:16]
            ).astype(BF16)
            zsend[c, s, half + 16 :] = sin_part[16:].astype(BF16)
        mine = pl.ds(pl.multiple_of(me * share, share), share)
        for peer in peers:
            to = pl.ds(pl.multiple_of(peer[0] * own_len, own_len), own_len)
            remote(
                zsend.at[c, :, :, to], zrecv.at[turn, c, :, mine, :], b_send.at[turn, c], b_recv.at[turn, c], peer
            ).start()
        own = pl.ds(pl.multiple_of(me * own_len, own_len), own_len)
        pltpu.make_async_copy(zsend.at[c, :, :, own], zrecv.at[turn, c, :, mine, :], b_recv.at[turn, c]).start()

    def return_sent(turn, c):
        wait_bytes(zsend.at[c, :, :, pl.ds(0, 7 * own_len)], b_send.at[turn, c])

    def mixed_of(turn, c):
        wait_bytes(zrecv.at[turn, c], b_recv.at[turn, c])
        held = jnp.concatenate([zrecv[turn, c, s] for s in range(per_chunk)], axis=1)
        return dot(held, unp_v[...], 0, 0)

    tables[0].wait()
    for c in range(chunks):
        x_loads[c].wait()
        if c == 0:
            first_loads(0)
            pl.semaphore_wait(barrier, len(everyone))
        to_owners(0, c, xbuf[c].astype(BF16))
    for load in tables[1:]:
        load.wait()
    for load in cot_loads:
        load.start()
    vacc[...] = jnp.zeros_like(vacc)
    cast_weights(0)
    first_loads(1)
    for c in range(chunks):
        turn_and_return(0, c)
        if c == 0:
            cast_weights(1)
    for load in cot_loads:
        load.wait()
    for c in range(chunks):
        owners_sent(0, c)

    gain_mix, bias_mix = prm_v[5:6], prm_v[6:7]
    gain_out, bias_out, c_out = prm_v[7:8], prm_v[8:9], prm_v[4:5]

    def out_copy(c):
        return pltpu.make_async_copy(ostage, out_hbm.at[c], out_sem.at[0])

    def feed(c, carry):
        value = xbuf[c] + mixed_of(0, c)
        value = value - row_mean(value)
        scale = lax.rsqrt(row_mean(value * value) + 1e-05)
        normal = value * scale
        r1b[...] = jnp.broadcast_to(scale, r1b.shape)
        xbuf[c] = normal
        hidden = normal * gain_mix + bias_mix
        hb[c] = hidden.astype(BF16)
        acc[...] = hidden + c_out

        def up(j, carry):
            pre = dot(hb[c], block_of(j), 1, 0) + prm_v[pl.ds(j, 1)]
            prob = 0.5 + 0.5 * lax.erf(pre * math.sqrt(0.5))
            density = jnp.exp(-0.5 * pre * pre) * (1.0 / math.sqrt(2.0 * math.pi))
            act = (pre * prob).astype(BF16)
            dgb[j] = prob + pre * density
            actb[j, c] = act
            acc[...] += dot(act, block_of(4 + j), 1, 0)
            return carry

        lax.fori_loop(0, 4, up, 0)
        value = acc[...]
        value = value - row_mean(value)
        scale = lax.rsqrt(row_mean(value * value) + 1e-05)
        normal = value * scale

        @pl.when(c > 0)
        def _():
            out_copy(c).wait()

        ostage[...] = normal * gain_out + bias_out
        out_copy(c).start()
        cot = cotb[c]
        vacc[7:8] += jnp.sum(cot * normal, axis=0, keepdims=True)
        vacc[8:9] += jnp.sum(cot, axis=0, keepdims=True)
        scaled = cot * gain_out
        g_sum2 = scale * (scaled - row_mean(scaled) - normal * row_mean(scaled * normal))
        low = g_sum2.astype(BF16)
        gbb[c] = low
        vacc[4:5] += jnp.sum(low.astype(F32), axis=0, keepdims=True)
        acc[...] = g_sum2

        def down(j, carry):
            g_pre = (dot(gbb[c], block_of(4 + j), 1, 1) * dgb[j]).astype(BF16)
            gpb[j, c] = g_pre
            vacc[pl.ds(j, 1)] += jnp.sum(g_pre.astype(F32), axis=0, keepdims=True)
            acc[...] += dot(g_pre, block_of(j), 1, 1)
            return carry

        lax.fori_loop(0, 4, down, 0)
        g_hidden = acc[...]
        normal = xbuf[c]
        vacc[5:6] += jnp.sum(g_hidden * normal, axis=0, keepdims=True)
        vacc[6:7] += jnp.sum(g_hidden, axis=0, keepdims=True)
        scaled = g_hidden * gain_mix
        g_sum1 = r1b[:, :1] * (scaled - row_mean(scaled) - normal * row_mean(scaled * normal))
        xbuf[c] = g_sum1
        to_owners(1, c, g_sum1.astype(BF16))
        return carry

    lax.fori_loop(0, chunks, feed, 0)

    lanes = vsend.shape[2]
    vsend[...] = jnp.zeros_like(vsend)
    for d in range(8):
        at = d * (features // 2)
        for r in range(3):
            where = at + r * lanes
            vsend[d, r : r + 1, :] = vacc[where // features : where // features + 1, where % features : where % features + lanes]
        for r in range(5):
            vsend[d, 3 + r : 4 + r, :share] = vacc[4 + r : 5 + r, d * share : (d + 1) * share]
    for peer in peers:
        remote(vsend.at[peer[0]], vrecv.at[me], v_send.at[0], v_recv.at[0], peer).start()
    pltpu.make_async_copy(vsend.at[me], vrecv.at[me], v_recv.at[0]).start()

    def weight_products(kind):
        def one(j, carry):
            if kind == 0:
                grad = dot(hb[...].reshape(-1, features), gpb[j].reshape(-1, features), 0, 0)
                wbuf[j] = grad.astype(BF16).reshape(wbuf.shape[1:])
            else:
                grad = dot(actb[j].reshape(-1, features), gbb[...].reshape(-1, features), 0, 0).astype(BF16)
                for y in range(2):
                    for q in range(4):
                        at = (y * 4 + q) * share
                        wbuf[4 + q, j, y] = grad[at : at + share]
            return carry

        lax.fori_loop(0, 4, one, 0)

    def core_send(kind):
        for x in range(2):
            remote(
                wbuf.at[4 * kind + 2 * x + 1 - core], recv1.at[kind, x],
                red_send.at[0, kind], red_recv.at[0, kind], core_peer,
            ).start()

    def core_sum(kind):
        wait_bytes(recv1.at[kind], red_recv.at[0, kind])
        for x in range(2):
            wbuf[4 * kind + 2 * x + core] += recv1[kind, x]

    def second_send(kind):
        if kind == 0:
            remote(
                wbuf.at[2 * (1 - x_at) + core], recv2.at[0], red_send.at[1, 0], red_recv.at[1, 0], x_peer
            ).start()
        else:
            for x in range(2):
                remote(
                    wbuf.at[4 + 2 * x + core, :, 1 - y_at], recv2.at[1, :, x],
                    red_send.at[1, 1], red_recv.at[1, 1], y_peer,
                ).start()

    def second_sum(kind):
        wait_bytes(recv2.at[kind], red_recv.at[1, kind])
        if kind == 0:
            wbuf[2 * x_at + core] += recv2[0]
        else:
            for x in range(2):
                wbuf[4 + 2 * x + core, :, y_at] += recv2[1, :, x]

    own_block = [2 * x_at + core, 4 + 2 * x_at + core]

    def third_send(kind):
        if kind == 0:
            src, peer = wbuf.at[own_block[0], :, 1 - y_at], y_peer
        else:
            src, peer = wbuf.at[4 + 2 * (1 - x_at) + core, :, y_at], x_peer
        remote(src, recv3.at[kind], red_send.at[2, kind], red_recv.at[2, kind], peer).start()

    def third_sum(kind):
        wait_bytes(recv3.at[kind], red_recv.at[2, kind])
        wbuf[own_block[kind], :, y_at] += recv3[kind]

    z_pair = lax.rem(z_at + 2, 4)
    z_next = z_at + 1 - 2 * z_lo

    def fourth_send(kind):
        for slot, z in ((0, z_next), (1, lax.rem(z_next + 2, 4))):
            remote(
                wbuf.at[own_block[kind], z, y_at], recv4.at[kind, slot],
                red_send.at[3, kind], red_recv.at[3, kind], za_peer,
            ).start()

    def fourth_sum(kind):
        wait_bytes(recv4.at[kind], red_recv.at[3, kind])
        for slot, z in ((0, z_at), (1, z_pair)):
            wbuf[own_block[kind], z, y_at] += recv4[kind, slot]

    def fifth_send(kind):
        remote(
            wbuf.at[own_block[kind], z_pair, y_at], recv5.at[kind], red_send.at[4, kind], red_recv.at[4, kind], zb_peer
        ).start()

    def fifth_sum(kind):
        wait_bytes(recv5.at[kind], red_recv.at[4, kind])
        recv6[kind, item] = wbuf[own_block[kind], z_at, y_at] + recv5[kind]
        for peer in (x_peer, core_peer, far_peer):
            remote(
                recv6.at[kind, item], recv6.at[kind, item], gat_send.at[kind], gat_recv.at[kind], peer
            ).start()

    def mat_copy(kind):
        return pltpu.make_async_copy(recv6.at[kind], gmat_hbm.at[kind], out_sem.at[2])

    def gathered(kind):
        wait_bytes(recv6.at[kind, pl.ds(0, 3)], gat_recv.at[kind])

    def final(c):
        grad = xbuf[c] + mixed_of(1, c)
        xbuf[c] = grad
        pltpu.make_async_copy(xbuf.at[c], gin_hbm.at[c], out_sem.at[1]).start()

    weight_products(0)
    core_send(0)
    for c in range(chunks):
        return_sent(0, c)
    turn_and_return(1, 0)
    weight_products(1)
    core_send(1)
    core_sum(0)
    second_send(0)
    turn_and_return(1, 1)
    core_sum(1)
    second_send(1)
    turn_and_return(1, 2)

    wait_bytes(vrecv, v_recv.at[0])
    vmid[...] = jnp.sum(vrecv[...], axis=0)
    for peer in (x_peer, core_peer, far_peer):
        remote(vmid, vlast.at[item], v_send.at[1], v_recv.at[1], peer).start()
    pltpu.make_async_copy(vmid, vlast.at[item], v_recv.at[1]).start()

    second_sum(0)
    third_send(0)
    second_sum(1)
    third_send(1)
    final(0)
    third_sum(0)
    fourth_send(0)
    third_sum(1)
    fourth_send(1)
    final(1)
    fourth_sum(0)
    fifth_send(0)
    fourth_sum(1)
    fifth_send(1)
    fifth_sum(0)
    fifth_sum(1)
    wait_bytes(vlast, v_recv.at[1])
    gvec_ref[...] = jnp.sum(vlast[...], axis=0)
    final(2)
    for kind in range(2):
        gathered(kind)
        mat_copy(kind).start()

    out_copy(chunks - 1).wait()
    wait_bytes(xbuf, out_sem.at[1])
    wait_bytes(recv6, out_sem.at[2])
    for c in range(chunks):
        owners_sent(1, c)
        return_sent(1, c)
    for kind in range(2):
        wait_bytes(recv1.at[kind], red_send.at[0, kind])
        wait_bytes(recv2.at[kind], red_send.at[1, kind])
        wait_bytes(recv3.at[kind], red_send.at[2, kind])
        wait_bytes(recv4.at[kind], red_send.at[3, kind])
        wait_bytes(recv5.at[kind], red_send.at[4, kind])
        wait_bytes(recv6.at[kind, pl.ds(0, 3)], gat_send.at[kind])
    wait_bytes(vrecv.at[pl.ds(0, 7)], v_send.at[0])
    wait_bytes(vlast.at[pl.ds(0, 3)], v_send.at[1])


def exchange_body(inputs, w_in, c_in, w_out, c_out, gain_mix, bias_mix, gain_out, bias_out, cotangent):
    local_len, per_dev, features = inputs.shape
    parts = lax.axis_size("seq")
    period = local_len * parts
    share = features // parts
    per_chunk = per_dev // CHUNKS
    rows = per_chunk * local_len
    forward, unpack = packed_tables(features, parts)
    cos_seq, sin_seq = seq_tables(period)
    held = jnp.swapaxes(inputs, 0, 1).reshape(CHUNKS, rows, features)
    cot = jnp.swapaxes(cotangent, 0, 1).reshape(CHUNKS, rows, features)
    params = jnp.concatenate(
        [c_in.reshape(4, features)]
        + [v[None] for v in (c_out, gain_mix, bias_mix, gain_out, bias_out)]
        + [jnp.zeros((7, features), F32)],
        axis=0,
    )
    anywhere = pl.BlockSpec(memory_space=pl.ANY)
    whole = (CHUNKS, rows, features)
    vm, dma = pltpu.VMEM, pltpu.SemaphoreType.DMA
    output, grad_inputs, mats, vecs = pl.pallas_call(
        layer_kernel,
        out_shape=(
            jax.ShapeDtypeStruct(whole, F32),
            jax.ShapeDtypeStruct(whole, F32),
            jax.ShapeDtypeStruct((2, 4, share, features), BF16),
            jax.ShapeDtypeStruct((8, 128), F32),
        ),
        in_specs=[anywhere] * 9,
        out_specs=(anywhere, anywhere, anywhere, pl.BlockSpec(memory_space=pltpu.VMEM)),
        scratch_shapes=[
            vm((features, features), BF16),
            vm((features, features), BF16),
            vm((period, period), BF16),
            vm((period, period), BF16),
            vm((16, features), F32),
            vm(whole, F32),
            vm(whole, F32),
            vm((8, 4, 2, share, features), BF16),
            vm((4, 192, features), F32),
            vm((CHUNKS, per_chunk, features, local_len), BF16),
            vm((2, CHUNKS, per_chunk, share, period), BF16),
            vm((CHUNKS, per_chunk, share, period), BF16),
            vm((2, CHUNKS, per_chunk, features, local_len), BF16),
            vm((4,) + whole, BF16),
            vm((4,) + whole, BF16),
            vm(whole, BF16),
            vm(whole, BF16),
            vm((4, rows, features), F32),
            vm((rows, features), F32),
            vm((rows, 128), F32),
            vm((rows, features), F32),
            vm((16, features), F32),
            vm((2, 2, 4, 2, share, features), BF16),
            vm((2, 4, 2, share, features), BF16),
            vm((2, 4, share, features), BF16),
            vm((2, 2, share, features), BF16),
            vm((2, share, features), BF16),
            vm((2, 4, share, features), BF16),
            vm((8, 8, 128), F32),
            vm((8, 8, 128), F32),
            vm((8, 128), F32),
            vm((4, 8, 128), F32),
            dma((5,)),
            dma((CHUNKS,)),
            dma((CHUNKS,)),
            dma((4,)),
            dma((2, CHUNKS)),
            dma((2, CHUNKS)),
            dma((2, CHUNKS)),
            dma((2, CHUNKS)),
            dma((3,)),
            dma((5, 2)),
            dma((5, 2)),
            dma((2,)),
            dma((2,)),
            dma((2,)),
            dma((2,)),
        ],
        compiler_params=pltpu.CompilerParams(
            collective_id=0, has_side_effects=True, vmem_limit_bytes=62 * 1024 * 1024
        ),
    )(held, cot, w_in, w_out, params, forward, unpack, cos_seq, sin_seq)
    shape = (per_dev, local_len, features)
    grad_in = jnp.swapaxes(mats[0], 0, 1).reshape(share, 4 * features).astype(F32)
    grad_out = mats[1].reshape(4 * share, features).astype(F32)
    return (
        jnp.swapaxes(output.reshape(shape), 0, 1),
        jnp.swapaxes(grad_inputs.reshape(shape), 0, 1),
        grad_in,
        vecs[:3].reshape(-1),
        grad_out,
        vecs[3, :share],
        vecs[4, :share],
        vecs[5, :share],
        vecs[6, :share],
        vecs[7, :share],
    )


def body(inputs, *rest):
    if lax.axis_size("seq") != 8 or lax.axis_size("item") != 4:
        return gather_body(inputs, *rest)
    return exchange_body(inputs, *rest)


def solution(mesh):
    placed = (
        P("seq", "item", None),
        P(),
        P(),
        P(),
        P(),
        P(),
        P(),
        P(),
        P(),
        P("seq", "item", None),
    )
    return jax.shard_map(
        body,
        mesh=mesh,
        in_specs=placed,
        out_specs=(
            P("seq", "item", None),
            P("seq", "item", None),
            P("seq", None),
            P("seq"),
            P("seq", None),
            P("seq"),
            P("seq"),
            P("seq"),
            P("seq"),
            P("seq"),
        ),
        check_vma=False,
    )
```

```python
import math

import jax
import jax.numpy as jnp
import numpy as np
from jax import lax
from jax.experimental import pallas as pl
from jax.experimental.pallas import tpu as pltpu
from jax.sharding import PartitionSpec as P


def table_block(row_ids, col_ids, period):
    products = row_ids[:, None] * col_ids[None, :] % period
    angles = products.astype(jnp.float32) * (2.0 * math.pi / period)
    return (jnp.cos(angles).astype(jnp.bfloat16), jnp.sin(angles).astype(jnp.bfloat16))


def plain_dot(left, right):
    return jnp.dot(left, right, preferred_element_type=jnp.float32)


def rows_dot(left, right):
    return lax.dot_general(
        left, right, (((0,), (0,)), ((), ())), preferred_element_type=jnp.float32
    )


def cols_dot(left, right):
    return lax.dot_general(
        left, right, (((1,), (1,)), ((), ())), preferred_element_type=jnp.float32
    )


def layer_norm(values, scales, shifts):
    average = jnp.mean(values, axis=-1, keepdims=True)
    centered = values - average
    variance = jnp.mean(centered * centered, axis=-1, keepdims=True)
    return centered * lax.rsqrt(variance + 1e-05) * scales + shifts


def gelu_exact(values):
    return jax.nn.gelu(values, approximate=False)


def gather_body(inputs, w_in, c_in, w_out, c_out, gain_mix, bias_mix, gain_out, bias_out, cotangent):
    local_len, per_dev, features = inputs.shape
    merged = per_dev * features
    period = local_len * lax.axis_size("seq")
    unit_scale = 1.0 / math.sqrt(period * features)
    own_rows = lax.axis_index("seq") * local_len + jnp.arange(local_len, dtype=jnp.int32)
    feat_ids = jnp.arange(features, dtype=jnp.int32)
    cos_hid, sin_hid = table_block(feat_ids, feat_ids, features)
    tokens = inputs.reshape(-1, features)
    tokens_low = tokens.astype(jnp.bfloat16)
    cos_part = (
        plain_dot(tokens_low, cos_hid).astype(jnp.bfloat16).reshape(local_len, per_dev, features)
    )
    sin_part = (
        plain_dot(tokens_low, sin_hid).astype(jnp.bfloat16).reshape(local_len, per_dev, features)
    )
    pieces = (
        lax.all_gather(cos_part, "seq", axis=0, tiled=True),
        lax.all_gather(sin_part, "seq", axis=0, tiled=True),
    )
    col_ids = jnp.arange(pieces[0].shape[0], dtype=jnp.int32)
    cos_blk, sin_blk = table_block(own_rows, col_ids, period)
    mixed = plain_dot(cos_blk, pieces[0].reshape(pieces[0].shape[0], -1)) - plain_dot(
        sin_blk, pieces[1].reshape(pieces[1].shape[0], -1)
    )
    mixed = (mixed * unit_scale).reshape(-1, features)
    hidden, pull_mix = jax.vjp(layer_norm, tokens + mixed, gain_mix, bias_mix)
    hidden_low = hidden.astype(jnp.bfloat16)
    w_in_low = w_in.astype(jnp.bfloat16)
    w_out_low = w_out.astype(jnp.bfloat16)
    pre = plain_dot(hidden_low, w_in_low) + c_in
    act, pull_gelu = jax.vjp(gelu_exact, pre)
    act_low = act.astype(jnp.bfloat16)
    branch = plain_dot(act_low, w_out_low) + c_out
    output, pull_out = jax.vjp(layer_norm, hidden + branch, gain_out, bias_out)
    g_sum2, grad_gain_out, grad_bias_out = pull_out(cotangent.reshape(-1, features))
    g_branch = g_sum2.astype(jnp.bfloat16)
    grad_c_out = jnp.sum(g_branch.astype(jnp.float32), axis=0)
    grad_w_out = rows_dot(act_low, g_branch)
    (g_act,) = pull_gelu(cols_dot(g_branch, w_out_low))
    g_pre = g_act.astype(jnp.bfloat16)
    grad_c_in = jnp.sum(g_pre.astype(jnp.float32), axis=0)
    grad_w_in = rows_dot(hidden_low, g_pre)
    g_hidden = g_sum2 + cols_dot(g_pre, w_in_low)
    g_sum1, grad_gain_mix, grad_bias_mix = pull_mix(g_hidden)
    g_mixed = g_sum1.astype(jnp.bfloat16).reshape(local_len, per_dev, features)
    empty = jnp.zeros((local_len, merged), jnp.float32)
    piece = lax.all_gather(g_mixed, "seq", axis=0, tiled=True)
    row_ids = jnp.arange(piece.shape[0], dtype=jnp.int32)
    cos_blk, sin_blk = table_block(row_ids, own_rows, period)
    flat = piece.reshape(piece.shape[0], -1)
    cycle_gc = rows_dot(cos_blk, flat)
    cycle_gs = (empty, empty)[1] - rows_dot(sin_blk, flat)
    g_cos = (cycle_gc * unit_scale).astype(jnp.bfloat16).reshape(-1, features)
    g_sin = (cycle_gs * unit_scale).astype(jnp.bfloat16).reshape(-1, features)
    grad_inputs = g_sum1 + cols_dot(g_cos, cos_hid) + cols_dot(g_sin, sin_hid)
    shards = (
        lax.psum_scatter(
            grad_w_in.astype(jnp.bfloat16), "seq", scatter_dimension=0, tiled=True
        ).astype(jnp.float32),
        lax.psum_scatter(
            grad_c_in.astype(jnp.bfloat16), "seq", scatter_dimension=0, tiled=True
        ).astype(jnp.float32),
        lax.psum_scatter(
            grad_w_out.astype(jnp.bfloat16), "seq", scatter_dimension=0, tiled=True
        ).astype(jnp.float32),
        lax.psum_scatter(
            grad_c_out.astype(jnp.bfloat16), "seq", scatter_dimension=0, tiled=True
        ).astype(jnp.float32),
        lax.psum_scatter(
            grad_gain_mix.astype(jnp.bfloat16), "seq", scatter_dimension=0, tiled=True
        ).astype(jnp.float32),
        lax.psum_scatter(
            grad_bias_mix.astype(jnp.bfloat16), "seq", scatter_dimension=0, tiled=True
        ).astype(jnp.float32),
        lax.psum_scatter(
            grad_gain_out.astype(jnp.bfloat16), "seq", scatter_dimension=0, tiled=True
        ).astype(jnp.float32),
        lax.psum_scatter(
            grad_bias_out.astype(jnp.bfloat16), "seq", scatter_dimension=0, tiled=True
        ).astype(jnp.float32),
    )
    summed = (
        lax.psum(shards[0].astype(jnp.bfloat16), "item").astype(jnp.float32),
        lax.psum(shards[1].astype(jnp.bfloat16), "item").astype(jnp.float32),
        lax.psum(shards[2].astype(jnp.bfloat16), "item").astype(jnp.float32),
        lax.psum(shards[3].astype(jnp.bfloat16), "item").astype(jnp.float32),
        lax.psum(shards[4].astype(jnp.bfloat16), "item").astype(jnp.float32),
        lax.psum(shards[5].astype(jnp.bfloat16), "item").astype(jnp.float32),
        lax.psum(shards[6].astype(jnp.bfloat16), "item").astype(jnp.float32),
        lax.psum(shards[7].astype(jnp.bfloat16), "item").astype(jnp.float32),
    )
    return (
        output.reshape(inputs.shape),
        grad_inputs.reshape(inputs.shape),
        summed[0],
        summed[1],
        summed[2],
        summed[3],
        summed[4],
        summed[5],
        summed[6],
        summed[7],
    )


def packed_tables(features, parts):
    half = features // 2
    share = half // parts
    index = np.arange(features)
    forward = np.zeros((features, features), np.float32)
    unpack = np.zeros((features, features), np.float32)
    for low in range(half):
        block, place = divmod(low, share)
        cos_slot = block * 2 * share + place
        sin_slot = cos_slot + share
        angles = (index * low % features).astype(np.float32) * np.float32(2.0 * math.pi / features)
        forward[cos_slot] = np.cos(angles)
        unpack[cos_slot, low] = 1.0
        if low:
            unpack[cos_slot, features - low] = 1.0
            forward[sin_slot] = np.sin(angles)
            unpack[sin_slot, low] = -1.0
            unpack[sin_slot, features - low] = 1.0
        else:
            forward[sin_slot] = 1.0 - 2.0 * (index % 2)
            unpack[sin_slot, half] = 1.0
    return forward.astype(jnp.bfloat16), unpack.astype(jnp.bfloat16)


def seq_tables(period):
    index = np.arange(period)
    angles = (index[:, None] * index[None, :] % period).astype(np.float32)
    angles = angles * np.float32(2.0 * math.pi / period)
    return np.cos(angles).astype(jnp.bfloat16), np.sin(angles).astype(jnp.bfloat16)


MESH = pl.DeviceIdType.MESH
CHUNKS = 3
BF16, F32 = jnp.bfloat16, jnp.float32


def dot(left, right, left_dim, right_dim):
    return lax.dot_general(
        left, right, (((left_dim,), (right_dim,)), ((), ())), preferred_element_type=F32
    )


def row_mean(values):
    return jnp.mean(values, axis=-1, keepdims=True)


def layer_kernel(
    x_hbm, cot_hbm, win_hbm, wout_hbm, cin_ref, cout_ref, gmix_ref, bmix_ref, gout_ref, bout_ref,
    fwd_hbm, unp_hbm, cos_hbm, sin_hbm,
    out_hbm, gsum_hbm, zback_hbm, gmat_ref, gvec_ref,
    fwd_v, unp_v, cos_v, sin_v, prm_v, xbuf, cotb, win_v, wout_v, stage,
    ysend, yrecv, zsend, zrecv, actb, gpb, hb, gbb, dgb, acc, r1b, ostage, vacc,
    recv1, hop0, hop1, hop2, hop3, vsend, vrecv, vmid, vlast,
    ld_sem, x_sem, cot_sem, stg_sem, a_send, a_recv, b_send, b_recv, out_sem,
    core_send, core_recv, red_send, red_recv, gat_send, gat_recv, v_send, v_recv,
):
    chunks, rows, features = xbuf.shape
    per_chunk, share, period = yrecv.shape[2], yrecv.shape[3], yrecv.shape[4]
    own_len = period // 8
    half = share // 2
    unit_scale = 1.0 / math.sqrt(period * features)

    me, item = lax.axis_index("seq"), lax.axis_index("item")
    peers = [(lax.rem(me + k, 8), item) for k in range(1, 8)]
    z_lo, y_at = lax.rem(lax.div(me, 2), 2), lax.rem(me, 2)
    z_at, z_hi = lax.div(me, 2), lax.div(me, 4)
    core, x_at = lax.rem(item, 2), lax.div(item, 2)
    core_peer = (me, item + 1 - 2 * core)
    x_peer = (me, item + 2 - 4 * x_at)
    far_peer = (me, lax.rem(item + 2, 4) + 1 - 2 * core)
    y_peer = (me + 1 - 2 * y_at, item)
    za_peer = (me + 2 - 4 * z_lo, item)
    zb_peer = (me + 4 - 8 * z_hi, item)

    def remote(src, dst, send, recv, peer):
        return pltpu.make_async_remote_copy(
            src_ref=src, dst_ref=dst, send_sem=send, recv_sem=recv, device_id=peer, device_id_type=MESH
        )

    def wait_bytes(ref, sem):
        pltpu.make_async_copy(ref, ref, sem).wait()

    tables = [
        pltpu.make_async_copy(src, dst, ld_sem.at[i])
        for i, (src, dst) in enumerate(
            [(fwd_hbm, fwd_v), (cos_hbm, cos_v), (sin_hbm, sin_v), (unp_hbm, unp_v)]
        )
    ]
    x_loads = [pltpu.make_async_copy(x_hbm.at[c], xbuf.at[c], x_sem.at[c]) for c in range(chunks)]
    cot_loads = [pltpu.make_async_copy(cot_hbm.at[c], cotb.at[c], cot_sem.at[c]) for c in range(chunks)]
    x_loads[0].start()
    tables[0].start()
    for load in x_loads[1:] + tables[1:]:
        load.start()

    barrier = pltpu.get_barrier_semaphore()
    everyone = peers + [core_peer, x_peer, far_peer]
    for peer in everyone:
        pl.semaphore_signal(barrier, inc=1, device_id=peer, device_id_type=MESH)

    slots, piece = stage.shape[0], stage.shape[1]
    per_block = features // piece
    steps = 8 * per_block

    def weight_load(step, part, slot):
        block, at = lax.div(step, per_block), lax.rem(step, per_block) * piece
        if part == 0:
            cols = pl.ds(pl.multiple_of(block * features, features), features)
            src = win_hbm.at[pl.ds(pl.multiple_of(at, piece), piece), cols]
        else:
            src = wout_hbm.at[pl.ds(pl.multiple_of(block * features + at, piece), piece), :]
        return pltpu.make_async_copy(src, stage.at[slot], stg_sem.at[slot])

    def cast_weights(part):
        total = 4 * per_block
        groups = piece // share

        def one(step, carry):
            slot = lax.rem(step, slots)
            weight_load(step, part, slot).wait()
            block, at = lax.div(step, per_block), lax.rem(step, per_block) * groups
            value = stage[slot].astype(BF16)
            for g in range(groups):
                where = at + g
                rows_of = value[g * share : (g + 1) * share]
                if part == 0:
                    win_v[block, lax.div(where, 2), lax.rem(where, 2)] = rows_of
                else:
                    wout_v[block, lax.div(where, 4), lax.rem(lax.div(where, 2), 2), lax.rem(where, 2)] = rows_of

            @pl.when(step + slots < total)
            def _():
                weight_load(step + slots, part, slot).start()

            return carry

        lax.fori_loop(0, total, one, 0)

    def first_loads(part):
        for slot in range(slots):
            weight_load(jnp.int32(slot), part, jnp.int32(slot)).start()

    def in_block(j):
        return win_v[j].reshape(features, features)

    def out_block(j):
        return wout_v[j].reshape(features, features)

    def pack(c, low):
        packed = dot(fwd_v[...], low, 1, 1).astype(BF16)
        for s in range(per_chunk):
            ysend[c, s] = packed[:, s * own_len : (s + 1) * own_len]

    def send_owners(way, c):
        mine = pl.ds(pl.multiple_of(me * own_len, own_len), own_len)
        for peer in peers:
            to = pl.ds(pl.multiple_of(peer[0] * share, share), share)
            remote(
                ysend.at[c, :, to, :], yrecv.at[way, c, :, :, mine], a_send.at[way, c], a_recv.at[way, c], peer
            ).start()
        own = pl.ds(pl.multiple_of(me * share, share), share)
        pltpu.make_async_copy(ysend.at[c, :, own, :], yrecv.at[way, c, :, :, mine], a_recv.at[way, c]).start()

    def owners_sent(way, c):
        wait_bytes(ysend.at[c, :, pl.ds(0, 7 * share), :], a_send.at[way, c])

    def turn(way, c):
        wait_bytes(yrecv.at[way, c], a_recv.at[way, c])
        held = yrecv[way, c]
        cos_rows = held[:, :half].reshape(per_chunk * half, period)
        sin_rows = held[:, half:].reshape(per_chunk * half, period)
        mid_rows = held[:, half : half + 16].reshape(per_chunk * 16, period)
        by_cos = dot(cos_rows, cos_v[...], 1, 0) * unit_scale
        by_sin = dot(sin_rows, sin_v[...], 1, 0) * unit_scale
        by_mid = dot(mid_rows, cos_v[...], 1, 0) * unit_scale
        top = lax.broadcasted_iota(jnp.int32, (16, period), 0) == 0
        top = jnp.logical_and(top, me == 0)
        for s in range(per_chunk):
            zsend[c, s, :half] = by_cos[s * half : (s + 1) * half].astype(BF16)
            sin_part = by_sin[s * half : (s + 1) * half]
            zsend[c, s, half : half + 16] = jnp.where(
                top, by_mid[s * 16 : (s + 1) * 16], sin_part[:16]
            ).astype(BF16)
            zsend[c, s, half + 16 :] = sin_part[16:].astype(BF16)

    def send_back(way, c):
        mine = pl.ds(pl.multiple_of(me * share, share), share)
        landing = zrecv if way == 0 else zback_hbm
        for peer in peers:
            to = pl.ds(pl.multiple_of(peer[0] * own_len, own_len), own_len)
            remote(
                zsend.at[c, :, :, to], landing.at[c, :, mine, :], b_send.at[way, c], b_recv.at[way, c], peer
            ).start()
        own = pl.ds(pl.multiple_of(me * own_len, own_len), own_len)
        pltpu.make_async_copy(zsend.at[c, :, :, own], landing.at[c, :, mine, :], b_recv.at[way, c]).start()

    def return_sent(way, c):
        wait_bytes(zsend.at[c, :, :, pl.ds(0, 7 * own_len)], b_send.at[way, c])

    def mixed_of(c):
        wait_bytes(zrecv.at[c], b_recv.at[0, c])
        held = jnp.concatenate([zrecv[c, s] for s in range(per_chunk)], axis=1)
        return dot(held, unp_v[...], 0, 0)

    tables[0].wait()
    x_loads[0].wait()
    first_loads(0)
    pack(0, xbuf[0].astype(BF16))
    pl.semaphore_wait(barrier, len(everyone))
    send_owners(0, 0)
    x_loads[1].wait()
    pack(1, xbuf[1].astype(BF16))
    for load in cot_loads:
        load.start()
    vacc[...] = jnp.zeros_like(vacc)
    for j in range(4):
        prm_v[j : j + 1] = cin_ref[j * features : (j + 1) * features].reshape(1, features)
    for r, ref in enumerate((cout_ref, gmix_ref, bmix_ref, gout_ref, bout_ref)):
        prm_v[4 + r : 5 + r] = ref[...].reshape(1, features)
    cast_weights(0)
    first_loads(1)
    send_owners(0, 1)
    x_loads[2].wait()
    pack(2, xbuf[2].astype(BF16))
    cast_weights(1)
    for load in tables[1:]:
        load.wait()
    turn(0, 0)
    send_back(0, 0)
    owners_sent(0, 0)
    owners_sent(0, 1)
    send_owners(0, 2)
    turn(0, 1)

    gain_mix, bias_mix = prm_v[5:6], prm_v[6:7]
    gain_out, bias_out, c_out = prm_v[7:8], prm_v[8:9], prm_v[4:5]

    def out_copy(c):
        return pltpu.make_async_copy(ostage, out_hbm.at[c], out_sem.at[0])

    def sum_copy(c):
        return pltpu.make_async_copy(xbuf.at[c], gsum_hbm.at[c], out_sem.at[1])

    def feed_up(c, mixed=None):
        value = xbuf[c] + (mixed_of(c) if mixed is None else mixed)
        value = value - row_mean(value)
        scale = lax.rsqrt(row_mean(value * value) + 1e-05)
        normal = value * scale
        r1b[...] = jnp.broadcast_to(scale, r1b.shape)
        xbuf[c] = normal
        hidden = normal * gain_mix + bias_mix
        hb[c] = hidden.astype(BF16)
        acc[...] = hidden + c_out

        def up(j, carry):
            pre = dot(hb[c], in_block(j), 1, 0) + prm_v[pl.ds(j, 1)]
            prob = 0.5 + 0.5 * lax.erf(pre * math.sqrt(0.5))
            density = jnp.exp(-0.5 * pre * pre) * (1.0 / math.sqrt(2.0 * math.pi))
            act = (pre * prob).astype(BF16)
            dgb[j] = prob + pre * density
            actb[j, c] = act
            acc[...] += dot(act, out_block(j), 1, 0)
            return carry

        lax.fori_loop(0, 4, up, 0, unroll=True)

    def feed_mid(c):
        value = acc[...]
        value = value - row_mean(value)
        scale = lax.rsqrt(row_mean(value * value) + 1e-05)
        normal = value * scale

        if c > 0:
            out_copy(c - 1).wait()
        ostage[...] = normal * gain_out + bias_out
        out_copy(c).start()
        cot_loads[c].wait()
        cot = cotb[c]
        vacc[7:8] += jnp.sum(cot * normal, axis=0, keepdims=True)
        vacc[8:9] += jnp.sum(cot, axis=0, keepdims=True)
        scaled = cot * gain_out
        g_sum2 = scale * (scaled - row_mean(scaled) - normal * row_mean(scaled * normal))
        low = g_sum2.astype(BF16)
        gbb[c] = low
        vacc[4:5] += jnp.sum(low.astype(F32), axis=0, keepdims=True)
        acc[...] = g_sum2

    def feed_down(c):
        for j in range(4):
            g_pre = (dot(gbb[c], out_block(j), 1, 1) * dgb[j]).astype(BF16)
            gpb[j, c] = g_pre
            vacc[j : j + 1] += jnp.sum(g_pre.astype(F32), axis=0, keepdims=True)

    def feed_end(c):
        for j in range(4):
            acc[...] += dot(gpb[j, c], in_block(j), 1, 1)
        g_hidden = acc[...]
        normal = xbuf[c]
        vacc[5:6] += jnp.sum(g_hidden * normal, axis=0, keepdims=True)
        vacc[6:7] += jnp.sum(g_hidden, axis=0, keepdims=True)
        scaled = g_hidden * gain_mix
        g_sum1 = r1b[:, :1] * (scaled - row_mean(scaled) - normal * row_mean(scaled * normal))
        xbuf[c] = g_sum1
        sum_copy(c).start()
        pack(c, g_sum1.astype(BF16))

    cut = hop3.shape[2]
    routes = ('xyz', 'xyz', 'xyz', 'xyz', 'yxz', 'zxy')
    z_pair = lax.rem(z_at + 2, 4)
    z_next = z_at + 1 - 2 * z_lo
    z_far = lax.rem(z_next + 2, 4)

    def part(p):
        return pl.ds((p % 3) * cut, cut)

    def add(*terms):
        total = terms[0].astype(F32)
        for term in terms[1:]:
            total = total + term.astype(F32)
        return total.astype(BF16)

    def product(p):
        kind, h, at = p // 3, p % 3, part(p)
        if kind == 0:
            for away in (1, 0):
                for x in range(2):
                    q = 2 * x + (1 - core if away else core)
                    grad = dot(hb[...].reshape(-1, features), gpb[q, :, :, at].reshape(-1, cut), 0, 0)
                    win_v[q, :, :, :, at] = grad.astype(BF16).reshape(4, 2, share, cut)
                    if away:
                        remote(
                            win_v.at[q, :, :, :, at], recv1.at[0, h, x], core_send.at[0, h], core_recv.at[0, h], core_peer
                        ).start()
        else:
            for j in range(4):
                grad = dot(actb[j].reshape(-1, features), gbb[:, :, at].reshape(-1, cut), 0, 0)
                wout_v[j, :, :, :, :, at] = grad.astype(BF16).reshape(2, 2, 2, share, cut)
            for x in range(2):
                remote(
                    wout_v.at[:, :, x, 1 - core, :, at], recv1.at[1, h, x], core_send.at[1, h], core_recv.at[1, h], core_peer
                ).start()

    def hop(p, step):
        kind, h, at, route = p // 3, p % 3, part(p), routes[p]
        if step == 0:
            wait_bytes(recv1.at[kind, h], core_recv.at[kind, h])

        def place(x, z, y):
            return (2 * x + core, z, y, slice(None), at) if kind == 0 else (z, y, x, core, slice(None), at)

        grads = (win_v, wout_v)[kind]

        def put(x, z, y, got):
            where = place(x, z, y)
            grads[where] = add(grads[where], got)

        def send(x, z, y, dst, peer):
            remote(grads.at[place(x, z, y)], dst, red_send.at[step, p], red_recv.at[step, p], peer).start()

        landing = (hop0, hop1, hop2, hop3)
        every = slice(None)
        if step:
            wait_bytes(landing[step - 1].at[p], red_recv.at[step - 1, p])
        if route == "xyz":
            if step == 0:
                put(1 - x_at, every, every, recv1[kind, h, 1 - x_at])
                send(1 - x_at, every, every, hop0.at[p], x_peer)
                put(x_at, every, every, recv1[kind, h, x_at])
            elif step == 1:
                put(x_at, every, 1 - y_at, hop0[p, :, 1 - y_at])
                send(x_at, every, 1 - y_at, hop1.at[p], y_peer)
                put(x_at, every, y_at, hop0[p, :, y_at])
        elif route == "yxz":
            if step == 0:
                for x in range(2):
                    put(x, every, 1 - y_at, recv1[kind, h, x, :, 1 - y_at])
                    send(x, every, 1 - y_at, hop0.at[p, :, x], y_peer)
                for x in range(2):
                    put(x, every, y_at, recv1[kind, h, x, :, y_at])
            elif step == 1:
                put(1 - x_at, every, y_at, hop0[p, :, 1 - x_at])
                send(1 - x_at, every, y_at, hop1.at[p], x_peer)
                put(x_at, every, y_at, hop0[p, :, x_at])
        if route != "zxy":
            if step == 2:
                for z in (z_next, z_far, z_pair, z_at):
                    put(x_at, z, y_at, hop1[p, z])
                send(x_at, z_next, y_at, hop2.at[p, 0], za_peer)
                send(x_at, z_far, y_at, hop2.at[p, 1], za_peer)
            elif step == 3:
                put(x_at, z_pair, y_at, hop2[p, 1])
                send(x_at, z_pair, y_at, hop3.at[p], zb_peer)
            elif step == 4:
                finish(p, add(grads[place(x_at, z_at, y_at)], hop2[p, 0], hop3[p]))
            return
        if step == 0:
            for x in range(2):
                for z in (z_next, z_far):
                    put(x, z, every, recv1[kind, h, x, z])
            for x in range(2):
                send(x, z_next, every, hop0.at[p, 2 * x], za_peer)
                send(x, z_far, every, hop0.at[p, 2 * x + 1], za_peer)
            for x in range(2):
                for z in (z_pair, z_at):
                    put(x, z, every, recv1[kind, h, x, z])
        elif step == 1:
            for x in range(2):
                put(x, z_pair, every, hop0[p, 2 * x + 1])
                send(x, z_pair, every, hop1.at[p, pl.ds(2 * x, 2)], zb_peer)
                put(x, z_at, every, hop0[p, 2 * x])
        elif step == 2:
            put(1 - x_at, z_at, every, hop1[p, pl.ds(2 * (1 - x_at), 2)])
            send(1 - x_at, z_at, every, hop2.at[p], x_peer)
            put(x_at, z_at, every, hop1[p, pl.ds(2 * x_at, 2)])
        elif step == 3:
            put(x_at, z_at, 1 - y_at, hop2[p, 1 - y_at])
            send(x_at, z_at, 1 - y_at, hop3.at[p], y_peer)
        elif step == 4:
            finish(p, add(grads[place(x_at, z_at, y_at)], hop2[p, y_at], hop3[p]))

    def finish(p, total):
        kind, at = p // 3, part(p)
        gmat_ref[kind, item, :, at] = total
        here = gmat_ref.at[kind, item, :, at]
        remote(here, here, gat_send.at[1, p], gat_recv.at[1, p], x_peer).start()
        remote(here, here, gat_send.at[0, p], gat_recv.at[0, p], core_peer).start()
        if p in (2,):
            remote(here, here, gat_send.at[2, p], gat_recv.at[2, p], far_peer).start()

    def forward_on(p):
        there = gmat_ref.at[p // 3, x_peer[1], :, part(p)]
        wait_bytes(there, gat_recv.at[1, p])
        if p not in (2,):
            remote(there, there, gat_send.at[2, p], gat_recv.at[2, p], core_peer).start()

    def vectors_out():
        lanes = vsend.shape[2]
        vsend[...] = jnp.zeros_like(vsend)
        for d in range(8):
            at = d * (features // 2)
            for r in range(3):
                where = at + r * lanes
                vsend[d, r : r + 1, :] = vacc[where // features : where // features + 1, where % features : where % features + lanes]
            for r in range(5):
                vsend[d, 3 + r : 4 + r, :share] = vacc[4 + r : 5 + r, d * share : (d + 1) * share]
        for peer in peers:
            remote(vsend.at[peer[0]], vrecv.at[me], v_send.at[0], v_recv.at[0], peer).start()
        pltpu.make_async_copy(vsend.at[me], vrecv.at[me], v_recv.at[0]).start()

    def vectors_on():
        wait_bytes(vrecv, v_recv.at[0])
        vmid[...] = jnp.sum(vrecv[...], axis=0)
        remote(vmid, vlast.at[0], v_send.at[1], v_recv.at[1], core_peer).start()

    def vectors_over():
        wait_bytes(vlast.at[0], v_recv.at[1])
        vlast[1] = vmid[...] + vlast[0]
        remote(vlast.at[1], vlast.at[2], v_send.at[2], v_recv.at[2], x_peer).start()

    def vectors_end():
        wait_bytes(vlast.at[2], v_recv.at[2])
        gvec_ref[...] = vlast[1] + vlast[2]

    feed_up(0)
    owners_sent(0, 2)
    send_back(0, 1)
    feed_mid(0)
    feed_down(0)
    feed_end(0)
    turn(0, 2)
    send_back(0, 2)
    feed_up(1)
    feed_mid(1)
    feed_down(1)
    feed_end(1)
    mixed = mixed_of(2)
    send_owners(1, 0)
    feed_up(2, mixed)
    send_owners(1, 1)
    feed_mid(2)
    feed_down(2)
    product(3)
    product(4)
    feed_end(2)
    hop(3, 0)
    send_owners(1, 2)
    product(5)
    hop(4, 0)
    for c in range(chunks):
        return_sent(0, c)
    turn(1, 0)
    send_back(1, 0)
    product(0)
    hop(5, 0)
    vectors_out()
    product(1)
    hop(0, 0)
    hop(3, 1)
    product(2)
    turn(1, 1)
    send_back(1, 1)
    hop(4, 1)
    hop(1, 0)
    hop(3, 2)
    hop(5, 1)
    vectors_on()
    turn(1, 2)
    send_back(1, 2)
    hop(0, 1)
    hop(2, 0)
    hop(4, 2)
    hop(3, 3)
    hop(5, 2)
    vectors_over()
    hop(1, 1)
    hop(0, 2)
    hop(3, 4)
    hop(4, 3)
    hop(5, 3)
    vectors_end()
    hop(2, 1)
    hop(1, 2)
    hop(0, 3)
    forward_on(3)
    hop(4, 4)
    hop(5, 4)
    hop(2, 2)
    hop(1, 3)
    hop(0, 4)
    forward_on(4)
    forward_on(5)
    hop(2, 3)
    hop(1, 4)
    forward_on(0)
    hop(2, 4)
    forward_on(1)
    forward_on(2)

    out_copy(chunks - 1).wait()
    wait_bytes(xbuf, out_sem.at[1])
    for c in range(chunks):
        owners_sent(1, c)
        return_sent(1, c)
    for kind in range(2):
        for h in range(3):
            wait_bytes(recv1.at[kind, h], core_send.at[kind, h])
    for p in range(6):
        for step, ref in enumerate((hop0, hop1, hop2, hop3)):
            wait_bytes(ref.at[p], red_send.at[step, p])
        for leg in range(3):
            wait_bytes(hop3.at[p], gat_send.at[leg, p])
        wait_bytes(hop3.at[p], gat_recv.at[0, p])
        wait_bytes(hop3.at[p], gat_recv.at[2, p])
    wait_bytes(vrecv.at[pl.ds(0, 7)], v_send.at[0])
    wait_bytes(vlast.at[1], v_send.at[1])
    wait_bytes(vlast.at[1], v_send.at[2])
    for c in range(chunks):
        wait_bytes(zback_hbm.at[c], b_recv.at[1, c])


def finish_kernel(
    out_in, gsum_in, zback_in, gmat_in, gvec_in, unp_in,
    out_ref, gin_ref, gwi_ref, gwo_ref, gci_ref, gco_ref, ggm_ref, gbm_ref, ggo_ref, gbo_ref,
    unp_v, zv, gv, ov, mv, res, wi, wo, sem_in, sem_out,
):
    chunks, per_chunk, features = zv.shape[0], zv.shape[1], zv.shape[2]
    share = mv.shape[2]
    loads = [pltpu.make_async_copy(unp_in, unp_v, sem_in.at[0]), pltpu.make_async_copy(gmat_in, mv, sem_in.at[1])]
    for c in range(chunks):
        loads.append(pltpu.make_async_copy(zback_in.at[c], zv.at[c], sem_in.at[2 + 2 * c]))
        loads.append(pltpu.make_async_copy(gsum_in.at[c], gv.at[c], sem_in.at[3 + 2 * c]))
    passing = [pltpu.make_async_copy(out_in.at[c], ov.at[c], sem_in.at[2 + 2 * chunks + c]) for c in range(chunks)]
    for load in loads + passing:
        load.start()
    stores = []

    def put(src, dst):
        copy = pltpu.make_async_copy(src, dst, sem_out.at[len(stores)])
        copy.start()
        stores.append(copy)

    loads[0].wait()
    loads[1].wait()
    for q in range(4):
        wi[:, q * features : (q + 1) * features] = mv[0, q].astype(F32)
        wo[q * share : (q + 1) * share] = mv[1, q].astype(F32)
    put(wi, gwi_ref)
    put(wo, gwo_ref)
    for c in range(chunks):
        loads[2 + 2 * c].wait()
        loads[3 + 2 * c].wait()
        held = jnp.concatenate([zv[c, s] for s in range(per_chunk)], axis=1)
        res[c] = gv[c] + dot(held, unp_v[...], 0, 0)
        put(res.at[c], gin_ref.at[c])
        passing[c].wait()
        put(ov.at[c], out_ref.at[c])
    lanes = gvec_in.shape[1]
    for r in range(3):
        gci_ref[r * lanes : (r + 1) * lanes] = gvec_in[r]
    for r, ref in enumerate((gco_ref, ggm_ref, gbm_ref, ggo_ref, gbo_ref)):
        ref[...] = gvec_in[3 + r, :share]
    for copy in stores:
        copy.wait()


def exchange_body(inputs, w_in, c_in, w_out, c_out, gain_mix, bias_mix, gain_out, bias_out, cotangent):
    local_len, per_dev, features = inputs.shape
    parts = lax.axis_size("seq")
    period = local_len * parts
    share = features // parts
    per_chunk = per_dev // CHUNKS
    rows = per_chunk * local_len
    forward, unpack = packed_tables(features, parts)
    cos_seq, sin_seq = seq_tables(period)
    held = jnp.swapaxes(inputs, 0, 1).reshape(CHUNKS, rows, features)
    cot = jnp.swapaxes(cotangent, 0, 1).reshape(CHUNKS, rows, features)
    anywhere = pl.BlockSpec(memory_space=pl.ANY)
    whole = (CHUNKS, rows, features)
    vm, dma = pltpu.VMEM, pltpu.SemaphoreType.DMA
    inside = pl.BlockSpec(memory_space=pltpu.VMEM)
    out_tmp, g_sum, z_back, mats, vecs = pl.pallas_call(
        layer_kernel,
        out_shape=(
            jax.ShapeDtypeStruct(whole, F32),
            jax.ShapeDtypeStruct(whole, F32),
            jax.ShapeDtypeStruct((CHUNKS, per_chunk, features, local_len), BF16),
            jax.ShapeDtypeStruct((2, 4, share, features), BF16),
            jax.ShapeDtypeStruct((8, 128), F32),
        ),
        in_specs=[anywhere] * 4 + [inside] * 6 + [anywhere] * 4,
        out_specs=(anywhere, anywhere, anywhere, inside, inside),
        scratch_shapes=[
            vm((features, features), BF16),
            vm((features, features), BF16),
            vm((period, period), BF16),
            vm((period, period), BF16),
            vm((16, features), F32),
            vm(whole, F32),
            vm(whole, F32),
            vm((4, 4, 2, share, features), BF16),
            vm((4, 2, 2, 2, share, features), BF16),
            vm((4, 192, features), F32),
            vm((CHUNKS, per_chunk, features, local_len), BF16),
            vm((2, CHUNKS, per_chunk, share, period), BF16),
            vm((CHUNKS, per_chunk, share, period), BF16),
            vm((CHUNKS, per_chunk, features, local_len), BF16),
            vm((4,) + whole, BF16),
            vm((4,) + whole, BF16),
            vm(whole, BF16),
            vm(whole, BF16),
            vm((4, rows, features), F32),
            vm((rows, features), F32),
            vm((rows, 128), F32),
            vm((rows, features), F32),
            vm((16, features), F32),
            vm((2, 3, 2, 4, 2, share, features // 3), BF16),
            vm((6, 4, 2, share, features // 3), BF16),
            vm((6, 4, share, features // 3), BF16),
            vm((6, 2, share, features // 3), BF16),
            vm((6, share, features // 3), BF16),
            vm((8, 8, 128), F32),
            vm((8, 8, 128), F32),
            vm((8, 128), F32),
            vm((3, 8, 128), F32),
            dma((4,)),
            dma((CHUNKS,)),
            dma((CHUNKS,)),
            dma((4,)),
            dma((2, CHUNKS)),
            dma((2, CHUNKS)),
            dma((2, CHUNKS)),
            dma((2, CHUNKS)),
            dma((2,)),
            dma((2, 3)),
            dma((2, 3)),
            dma((4, 6)),
            dma((4, 6)),
            dma((3, 6)),
            dma((3, 6)),
            dma((3,)),
            dma((3,)),
        ],
        compiler_params=pltpu.CompilerParams(
            collective_id=0, has_side_effects=True, vmem_limit_bytes=62 * 1024 * 1024
        ),
    )(held, cot, w_in, w_out, c_in, c_out, gain_mix, bias_mix, gain_out, bias_out, forward, unpack, cos_seq, sin_seq)
    shape = (per_dev, local_len, features)
    vec = lambda n: jax.ShapeDtypeStruct((n,), F32)
    output, grad_inputs, grad_in, grad_out, grad_c_in, *others = pl.pallas_call(
        finish_kernel,
        in_specs=[anywhere] * 4 + [inside, anywhere],
        out_specs=(anywhere,) * 4 + (inside,) * 6,
        out_shape=(
            jax.ShapeDtypeStruct(whole, F32),
            jax.ShapeDtypeStruct(whole, F32),
            jax.ShapeDtypeStruct((share, 4 * features), F32),
            jax.ShapeDtypeStruct((4 * share, features), F32),
            vec(4 * share),
        )
        + (vec(share),) * 5,
        scratch_shapes=[
            vm((features, features), BF16),
            vm((CHUNKS, per_chunk, features, local_len), BF16),
            vm(whole, F32),
            vm(whole, F32),
            vm((2, 4, share, features), BF16),
            vm(whole, F32),
            vm((share, 4 * features), F32),
            vm((4 * share, features), F32),
            dma((2 + 3 * CHUNKS,)),
            dma((2 + 2 * CHUNKS,)),
        ],
        compiler_params=pltpu.CompilerParams(vmem_limit_bytes=60 * 1024 * 1024),
    )(out_tmp, g_sum, z_back, mats, vecs, unpack)
    output = jnp.swapaxes(output.reshape(shape), 0, 1)
    grad_inputs = jnp.swapaxes(grad_inputs.reshape(shape), 0, 1)
    return (output, grad_inputs, grad_in, grad_c_in, grad_out, *others)


def body(inputs, *rest):
    if lax.axis_size("seq") != 8 or lax.axis_size("item") != 4:
        return gather_body(inputs, *rest)
    return exchange_body(inputs, *rest)


def solution(mesh):
    placed = (
        P("seq", "item", None),
        P(),
        P(),
        P(),
        P(),
        P(),
        P(),
        P(),
        P(),
        P("seq", "item", None),
    )
    return jax.shard_map(
        body,
        mesh=mesh,
        in_specs=placed,
        out_specs=(
            P("seq", "item", None),
            P("seq", "item", None),
            P("seq", None),
            P("seq"),
            P("seq", None),
            P("seq"),
            P("seq"),
            P("seq"),
            P("seq"),
            P("seq"),
        ),
        check_vma=False,
    )
```

```python
import math

import jax
import jax.numpy as jnp
import numpy as np
from jax import lax
from jax.experimental import pallas as pl
from jax.experimental.pallas import tpu as pltpu
from jax.sharding import PartitionSpec as P


def table_block(row_ids, col_ids, period):
    products = row_ids[:, None] * col_ids[None, :] % period
    angles = products.astype(jnp.float32) * (2.0 * math.pi / period)
    return (jnp.cos(angles).astype(jnp.bfloat16), jnp.sin(angles).astype(jnp.bfloat16))


def plain_dot(left, right):
    return jnp.dot(left, right, preferred_element_type=jnp.float32)


def rows_dot(left, right):
    return lax.dot_general(
        left, right, (((0,), (0,)), ((), ())), preferred_element_type=jnp.float32
    )


def cols_dot(left, right):
    return lax.dot_general(
        left, right, (((1,), (1,)), ((), ())), preferred_element_type=jnp.float32
    )


def layer_norm(values, scales, shifts):
    average = jnp.mean(values, axis=-1, keepdims=True)
    centered = values - average
    variance = jnp.mean(centered * centered, axis=-1, keepdims=True)
    return centered * lax.rsqrt(variance + 1e-05) * scales + shifts


def gelu_exact(values):
    return jax.nn.gelu(values, approximate=False)


def gather_body(inputs, w_in, c_in, w_out, c_out, gain_mix, bias_mix, gain_out, bias_out, cotangent):
    local_len, per_dev, features = inputs.shape
    merged = per_dev * features
    period = local_len * lax.axis_size("seq")
    unit_scale = 1.0 / math.sqrt(period * features)
    own_rows = lax.axis_index("seq") * local_len + jnp.arange(local_len, dtype=jnp.int32)
    feat_ids = jnp.arange(features, dtype=jnp.int32)
    cos_hid, sin_hid = table_block(feat_ids, feat_ids, features)
    tokens = inputs.reshape(-1, features)
    tokens_low = tokens.astype(jnp.bfloat16)
    cos_part = (
        plain_dot(tokens_low, cos_hid).astype(jnp.bfloat16).reshape(local_len, per_dev, features)
    )
    sin_part = (
        plain_dot(tokens_low, sin_hid).astype(jnp.bfloat16).reshape(local_len, per_dev, features)
    )
    pieces = (
        lax.all_gather(cos_part, "seq", axis=0, tiled=True),
        lax.all_gather(sin_part, "seq", axis=0, tiled=True),
    )
    col_ids = jnp.arange(pieces[0].shape[0], dtype=jnp.int32)
    cos_blk, sin_blk = table_block(own_rows, col_ids, period)
    mixed = plain_dot(cos_blk, pieces[0].reshape(pieces[0].shape[0], -1)) - plain_dot(
        sin_blk, pieces[1].reshape(pieces[1].shape[0], -1)
    )
    mixed = (mixed * unit_scale).reshape(-1, features)
    hidden, pull_mix = jax.vjp(layer_norm, tokens + mixed, gain_mix, bias_mix)
    hidden_low = hidden.astype(jnp.bfloat16)
    w_in_low = w_in.astype(jnp.bfloat16)
    w_out_low = w_out.astype(jnp.bfloat16)
    pre = plain_dot(hidden_low, w_in_low) + c_in
    act, pull_gelu = jax.vjp(gelu_exact, pre)
    act_low = act.astype(jnp.bfloat16)
    branch = plain_dot(act_low, w_out_low) + c_out
    output, pull_out = jax.vjp(layer_norm, hidden + branch, gain_out, bias_out)
    g_sum2, grad_gain_out, grad_bias_out = pull_out(cotangent.reshape(-1, features))
    g_branch = g_sum2.astype(jnp.bfloat16)
    grad_c_out = jnp.sum(g_branch.astype(jnp.float32), axis=0)
    grad_w_out = rows_dot(act_low, g_branch)
    (g_act,) = pull_gelu(cols_dot(g_branch, w_out_low))
    g_pre = g_act.astype(jnp.bfloat16)
    grad_c_in = jnp.sum(g_pre.astype(jnp.float32), axis=0)
    grad_w_in = rows_dot(hidden_low, g_pre)
    g_hidden = g_sum2 + cols_dot(g_pre, w_in_low)
    g_sum1, grad_gain_mix, grad_bias_mix = pull_mix(g_hidden)
    g_mixed = g_sum1.astype(jnp.bfloat16).reshape(local_len, per_dev, features)
    empty = jnp.zeros((local_len, merged), jnp.float32)
    piece = lax.all_gather(g_mixed, "seq", axis=0, tiled=True)
    row_ids = jnp.arange(piece.shape[0], dtype=jnp.int32)
    cos_blk, sin_blk = table_block(row_ids, own_rows, period)
    flat = piece.reshape(piece.shape[0], -1)
    cycle_gc = rows_dot(cos_blk, flat)
    cycle_gs = (empty, empty)[1] - rows_dot(sin_blk, flat)
    g_cos = (cycle_gc * unit_scale).astype(jnp.bfloat16).reshape(-1, features)
    g_sin = (cycle_gs * unit_scale).astype(jnp.bfloat16).reshape(-1, features)
    grad_inputs = g_sum1 + cols_dot(g_cos, cos_hid) + cols_dot(g_sin, sin_hid)
    shards = (
        lax.psum_scatter(
            grad_w_in.astype(jnp.bfloat16), "seq", scatter_dimension=0, tiled=True
        ).astype(jnp.float32),
        lax.psum_scatter(
            grad_c_in.astype(jnp.bfloat16), "seq", scatter_dimension=0, tiled=True
        ).astype(jnp.float32),
        lax.psum_scatter(
            grad_w_out.astype(jnp.bfloat16), "seq", scatter_dimension=0, tiled=True
        ).astype(jnp.float32),
        lax.psum_scatter(
            grad_c_out.astype(jnp.bfloat16), "seq", scatter_dimension=0, tiled=True
        ).astype(jnp.float32),
        lax.psum_scatter(
            grad_gain_mix.astype(jnp.bfloat16), "seq", scatter_dimension=0, tiled=True
        ).astype(jnp.float32),
        lax.psum_scatter(
            grad_bias_mix.astype(jnp.bfloat16), "seq", scatter_dimension=0, tiled=True
        ).astype(jnp.float32),
        lax.psum_scatter(
            grad_gain_out.astype(jnp.bfloat16), "seq", scatter_dimension=0, tiled=True
        ).astype(jnp.float32),
        lax.psum_scatter(
            grad_bias_out.astype(jnp.bfloat16), "seq", scatter_dimension=0, tiled=True
        ).astype(jnp.float32),
    )
    summed = (
        lax.psum(shards[0].astype(jnp.bfloat16), "item").astype(jnp.float32),
        lax.psum(shards[1].astype(jnp.bfloat16), "item").astype(jnp.float32),
        lax.psum(shards[2].astype(jnp.bfloat16), "item").astype(jnp.float32),
        lax.psum(shards[3].astype(jnp.bfloat16), "item").astype(jnp.float32),
        lax.psum(shards[4].astype(jnp.bfloat16), "item").astype(jnp.float32),
        lax.psum(shards[5].astype(jnp.bfloat16), "item").astype(jnp.float32),
        lax.psum(shards[6].astype(jnp.bfloat16), "item").astype(jnp.float32),
        lax.psum(shards[7].astype(jnp.bfloat16), "item").astype(jnp.float32),
    )
    return (
        output.reshape(inputs.shape),
        grad_inputs.reshape(inputs.shape),
        summed[0],
        summed[1],
        summed[2],
        summed[3],
        summed[4],
        summed[5],
        summed[6],
        summed[7],
    )


def packed_tables(features, parts):
    half = features // 2
    share = half // parts
    index = np.arange(features)
    forward = np.zeros((features, features), np.float32)
    unpack = np.zeros((features, features), np.float32)
    for low in range(half):
        block, place = divmod(low, share)
        cos_slot = block * 2 * share + place
        sin_slot = cos_slot + share
        angles = (index * low % features).astype(np.float32) * np.float32(2.0 * math.pi / features)
        forward[cos_slot] = np.cos(angles)
        unpack[cos_slot, low] = 1.0
        if low:
            unpack[cos_slot, features - low] = 1.0
            forward[sin_slot] = np.sin(angles)
            unpack[sin_slot, low] = -1.0
            unpack[sin_slot, features - low] = 1.0
        else:
            forward[sin_slot] = 1.0 - 2.0 * (index % 2)
            unpack[sin_slot, half] = 1.0
    return forward.astype(jnp.bfloat16), unpack.astype(jnp.bfloat16)


def seq_tables(period):
    index = np.arange(period)
    angles = (index[:, None] * index[None, :] % period).astype(np.float32)
    angles = angles * np.float32(2.0 * math.pi / period)
    return np.cos(angles).astype(jnp.bfloat16), np.sin(angles).astype(jnp.bfloat16)


MESH = pl.DeviceIdType.MESH
CHUNKS = 3
BF16, F32 = jnp.bfloat16, jnp.float32


def dot(left, right, left_dim, right_dim):
    return lax.dot_general(
        left, right, (((left_dim,), (right_dim,)), ((), ())), preferred_element_type=F32
    )


def row_mean(values):
    return jnp.mean(values, axis=-1, keepdims=True)


def layer_kernel(
    x_hbm, cot_hbm, win_hbm, wout_hbm, cin_ref, cout_ref, gmix_ref, bmix_ref, gout_ref, bout_ref,
    fwd_hbm, unp_hbm, cos_hbm, sin_hbm,
    out_hbm, gin_hbm, gmat_ref, gvec_ref,
    fwd_v, unp_v, cos_v, sin_v, prm_v, xbuf, cotb, win_v, wout_v, stage,
    ysend, yrecv, zsend, zrecv, actb, gpb, hb, gbb, dgb, acc, r1b, ostage, vacc,
    recv1, hop0, hop1, hop2, hop3, vsend, vrecv, vmid, vlast,
    ld_sem, x_sem, cot_sem, stg_sem, a_send, a_recv, b_send, b_recv, out_sem,
    core_send, core_recv, red_send, red_recv, gat_send, gat_recv, v_send, v_recv,
):
    chunks, rows, features = xbuf.shape
    per_chunk, share, period = yrecv.shape[2], yrecv.shape[3], yrecv.shape[4]
    own_len = period // 8
    half = share // 2
    unit_scale = 1.0 / math.sqrt(period * features)

    me, item = lax.axis_index("seq"), lax.axis_index("item")
    peers = [(lax.rem(me + k, 8), item) for k in range(1, 8)]
    z_lo, y_at = lax.rem(lax.div(me, 2), 2), lax.rem(me, 2)
    z_at, z_hi = lax.div(me, 2), lax.div(me, 4)
    core, x_at = lax.rem(item, 2), lax.div(item, 2)
    core_peer = (me, item + 1 - 2 * core)
    x_peer = (me, item + 2 - 4 * x_at)
    far_peer = (me, lax.rem(item + 2, 4) + 1 - 2 * core)
    y_peer = (me + 1 - 2 * y_at, item)
    za_peer = (me + 2 - 4 * z_lo, item)
    zb_peer = (me + 4 - 8 * z_hi, item)

    def remote(src, dst, send, recv, peer):
        return pltpu.make_async_remote_copy(
            src_ref=src, dst_ref=dst, send_sem=send, recv_sem=recv, device_id=peer, device_id_type=MESH
        )

    def wait_bytes(ref, sem):
        pltpu.make_async_copy(ref, ref, sem).wait()

    tables = [
        pltpu.make_async_copy(src, dst, ld_sem.at[i])
        for i, (src, dst) in enumerate(
            [(fwd_hbm, fwd_v), (cos_hbm, cos_v), (sin_hbm, sin_v), (unp_hbm, unp_v)]
        )
    ]
    x_loads = [pltpu.make_async_copy(x_hbm.at[c], xbuf.at[c], x_sem.at[c]) for c in range(chunks)]
    cot_loads = [pltpu.make_async_copy(cot_hbm.at[c], cotb.at[c], cot_sem.at[c]) for c in range(chunks)]
    x_loads[0].start()
    tables[0].start()
    for load in x_loads[1:] + tables[1:]:
        load.start()

    barrier = pltpu.get_barrier_semaphore()
    everyone = peers + [core_peer, x_peer, far_peer]
    for peer in everyone:
        pl.semaphore_signal(barrier, inc=1, device_id=peer, device_id_type=MESH)

    slots, piece = stage.shape[0], stage.shape[1]
    per_block = features // piece
    steps = 8 * per_block

    def weight_load(step, part, slot):
        block, at = lax.div(step, per_block), lax.rem(step, per_block) * piece
        if part == 0:
            cols = pl.ds(pl.multiple_of(block * features, features), features)
            src = win_hbm.at[pl.ds(pl.multiple_of(at, piece), piece), cols]
        else:
            src = wout_hbm.at[pl.ds(pl.multiple_of(block * features + at, piece), piece), :]
        return pltpu.make_async_copy(src, stage.at[slot], stg_sem.at[slot])

    def cast_weights(part):
        total = 4 * per_block
        groups = piece // share

        def one(step, carry):
            slot = lax.rem(step, slots)
            weight_load(step, part, slot).wait()
            block, at = lax.div(step, per_block), lax.rem(step, per_block) * groups
            value = stage[slot].astype(BF16)
            for g in range(groups):
                where = at + g
                rows_of = value[g * share : (g + 1) * share]
                if part == 0:
                    win_v[block, lax.div(where, 2), lax.rem(where, 2)] = rows_of
                else:
                    wout_v[block, lax.div(where, 4), lax.rem(lax.div(where, 2), 2), lax.rem(where, 2)] = rows_of

            @pl.when(step + slots < total)
            def _():
                weight_load(step + slots, part, slot).start()

            return carry

        lax.fori_loop(0, total, one, 0)

    def first_loads(part):
        for slot in range(slots):
            weight_load(jnp.int32(slot), part, jnp.int32(slot)).start()

    def in_block(j):
        return win_v[j].reshape(features, features)

    def out_block(j):
        return wout_v[j].reshape(features, features)

    def pack(c, low):
        packed = dot(fwd_v[...], low, 1, 1).astype(BF16)
        for s in range(per_chunk):
            ysend[c, s] = packed[:, s * own_len : (s + 1) * own_len]

    def send_owners(way, c):
        mine = pl.ds(pl.multiple_of(me * own_len, own_len), own_len)
        for peer in peers:
            to = pl.ds(pl.multiple_of(peer[0] * share, share), share)
            remote(
                ysend.at[c, :, to, :], yrecv.at[way, c, :, :, mine], a_send.at[way, c], a_recv.at[way, c], peer
            ).start()
        own = pl.ds(pl.multiple_of(me * share, share), share)
        pltpu.make_async_copy(ysend.at[c, :, own, :], yrecv.at[way, c, :, :, mine], a_recv.at[way, c]).start()

    def owners_sent(way, c):
        wait_bytes(ysend.at[c, :, pl.ds(0, 7 * share), :], a_send.at[way, c])

    def turn(way, c):
        wait_bytes(yrecv.at[way, c], a_recv.at[way, c])
        held = yrecv[way, c]
        cos_rows = held[:, :half].reshape(per_chunk * half, period)
        sin_rows = held[:, half:].reshape(per_chunk * half, period)
        mid_rows = held[:, half : half + 16].reshape(per_chunk * 16, period)
        by_cos = dot(cos_rows, cos_v[...], 1, 0) * unit_scale
        by_sin = dot(sin_rows, sin_v[...], 1, 0) * unit_scale
        by_mid = dot(mid_rows, cos_v[...], 1, 0) * unit_scale
        top = lax.broadcasted_iota(jnp.int32, (16, period), 0) == 0
        top = jnp.logical_and(top, me == 0)
        for s in range(per_chunk):
            zsend[c, s, :half] = by_cos[s * half : (s + 1) * half].astype(BF16)
            sin_part = by_sin[s * half : (s + 1) * half]
            zsend[c, s, half : half + 16] = jnp.where(
                top, by_mid[s * 16 : (s + 1) * 16], sin_part[:16]
            ).astype(BF16)
            zsend[c, s, half + 16 :] = sin_part[16:].astype(BF16)

    def send_back(way, c):
        mine = pl.ds(pl.multiple_of(me * share, share), share)
        for peer in peers:
            to = pl.ds(pl.multiple_of(peer[0] * own_len, own_len), own_len)
            remote(
                zsend.at[c, :, :, to], zrecv.at[c, :, mine, :], b_send.at[way, c], b_recv.at[way, c], peer
            ).start()
        own = pl.ds(pl.multiple_of(me * own_len, own_len), own_len)
        pltpu.make_async_copy(zsend.at[c, :, :, own], zrecv.at[c, :, mine, :], b_recv.at[way, c]).start()

    def return_sent(way, c):
        wait_bytes(zsend.at[c, :, :, pl.ds(0, 7 * own_len)], b_send.at[way, c])

    def mixed_of(c, way=0):
        wait_bytes(zrecv.at[c], b_recv.at[way, c])
        held = jnp.concatenate([zrecv[c, s] for s in range(per_chunk)], axis=1)
        return dot(held, unp_v[...], 0, 0)

    tables[0].wait()
    x_loads[0].wait()
    first_loads(0)
    pack(0, xbuf[0].astype(BF16))
    pl.semaphore_wait(barrier, len(everyone))
    send_owners(0, 0)
    x_loads[1].wait()
    pack(1, xbuf[1].astype(BF16))
    for load in cot_loads:
        load.start()
    vacc[...] = jnp.zeros_like(vacc)
    for j in range(4):
        prm_v[j : j + 1] = cin_ref[j * features : (j + 1) * features].reshape(1, features)
    for r, ref in enumerate((cout_ref, gmix_ref, bmix_ref, gout_ref, bout_ref)):
        prm_v[4 + r : 5 + r] = ref[...].reshape(1, features)
    cast_weights(0)
    first_loads(1)
    send_owners(0, 1)
    x_loads[2].wait()
    pack(2, xbuf[2].astype(BF16))
    cast_weights(1)
    for load in tables[1:]:
        load.wait()
    turn(0, 0)
    send_back(0, 0)
    owners_sent(0, 0)
    owners_sent(0, 1)
    send_owners(0, 2)
    turn(0, 1)

    gain_mix, bias_mix = prm_v[5:6], prm_v[6:7]
    gain_out, bias_out, c_out = prm_v[7:8], prm_v[8:9], prm_v[4:5]

    def out_copy(c):
        return pltpu.make_async_copy(ostage, out_hbm.at[c], out_sem.at[0])

    def feed_up(c, mixed=None):
        value = xbuf[c] + (mixed_of(c) if mixed is None else mixed)
        value = value - row_mean(value)
        scale = lax.rsqrt(row_mean(value * value) + 1e-05)
        normal = value * scale
        r1b[...] = jnp.broadcast_to(scale, r1b.shape)
        xbuf[c] = normal
        hidden = normal * gain_mix + bias_mix
        hb[c] = hidden.astype(BF16)
        acc[...] = hidden + c_out

        def up(j, carry):
            pre = dot(hb[c], in_block(j), 1, 0) + prm_v[pl.ds(j, 1)]
            prob = 0.5 + 0.5 * lax.erf(pre * math.sqrt(0.5))
            density = jnp.exp(-0.5 * pre * pre) * (1.0 / math.sqrt(2.0 * math.pi))
            act = (pre * prob).astype(BF16)
            dgb[j] = prob + pre * density
            actb[j, c] = act
            acc[...] += dot(act, out_block(j), 1, 0)
            return carry

        lax.fori_loop(0, 4, up, 0, unroll=True)

    def feed_mid(c):
        value = acc[...]
        value = value - row_mean(value)
        scale = lax.rsqrt(row_mean(value * value) + 1e-05)
        normal = value * scale

        if c > 0:
            out_copy(c - 1).wait()
        ostage[...] = (normal * gain_out + bias_out).astype(BF16)
        out_copy(c).start()
        cot_loads[c].wait()
        cot = cotb[c]
        vacc[7:8] += jnp.sum(cot * normal, axis=0, keepdims=True)
        vacc[8:9] += jnp.sum(cot, axis=0, keepdims=True)
        scaled = cot * gain_out
        g_sum2 = scale * (scaled - row_mean(scaled) - normal * row_mean(scaled * normal))
        low = g_sum2.astype(BF16)
        gbb[c] = low
        vacc[4:5] += jnp.sum(low.astype(F32), axis=0, keepdims=True)
        acc[...] = g_sum2

    def feed_down(c):
        for j in range(4):
            g_pre = (dot(gbb[c], out_block(j), 1, 1) * dgb[j]).astype(BF16)
            gpb[j, c] = g_pre
            vacc[j : j + 1] += jnp.sum(g_pre.astype(F32), axis=0, keepdims=True)

    def feed_end(c):
        for j in range(4):
            acc[...] += dot(gpb[j, c], in_block(j), 1, 1)
        g_hidden = acc[...]
        normal = xbuf[c]
        vacc[5:6] += jnp.sum(g_hidden * normal, axis=0, keepdims=True)
        vacc[6:7] += jnp.sum(g_hidden, axis=0, keepdims=True)
        scaled = g_hidden * gain_mix
        g_sum1 = r1b[:, :1] * (scaled - row_mean(scaled) - normal * row_mean(scaled * normal))
        xbuf[c] = g_sum1
        pack(c, g_sum1.astype(BF16))

    cut = hop3.shape[3]
    routes = ('xyz', 'xyz', 'yxz', 'xzy', 'yxz', 'xzy')
    z_pair = lax.rem(z_at + 2, 4)
    z_next = z_at + 1 - 2 * z_lo
    z_far = lax.rem(z_next + 2, 4)

    def part(p):
        return pl.ds((p % 3) * cut, cut)

    def add(*terms):
        total = terms[0].astype(F32)
        for term in terms[1:]:
            total = total + term.astype(F32)
        return total.astype(BF16)

    def product(p):
        kind, h, at = p // 3, p % 3, part(p)
        if kind == 0:
            for away in (1, 0):
                for x in range(2):
                    q = 2 * x + (1 - core if away else core)
                    grad = dot(hb[...].reshape(-1, features), gpb[q, :, :, at].reshape(-1, cut), 0, 0)
                    win_v[q, :, :, :, at] = grad.astype(BF16).reshape(4, 2, share, cut)
                    if away:
                        remote(
                            win_v.at[q, :, :, :, at], recv1.at[0, h, x], core_send.at[0, h], core_recv.at[0, h], core_peer
                        ).start()
        else:
            for j in range(4):
                grad = dot(actb[j].reshape(-1, features), gbb[:, :, at].reshape(-1, cut), 0, 0)
                wout_v[j, :, :, :, :, at] = grad.astype(BF16).reshape(2, 2, 2, share, cut)
            for x in range(2):
                remote(
                    wout_v.at[:, :, x, 1 - core, :, at], recv1.at[1, h, x], core_send.at[1, h], core_recv.at[1, h], core_peer
                ).start()

    def hop(p, step):
        kind, h, at = p // 3, p % 3, part(p)
        legs = routes[p].replace("z", "ab")
        past = legs[:step]
        grads = (win_v, wout_v)[kind]
        landing = (hop0, hop1, hop2, hop3)
        if step == 0:
            wait_bytes(recv1.at[kind, h], core_recv.at[kind, h])
        else:
            wait_bytes(landing[step - 1].at[p], red_recv.at[step - 1, p])

        def place(x, z, y):
            return (2 * x + core, z, y, slice(None), at) if kind == 0 else (z, y, x, core, slice(None), at)

        def arrived(x, z, y):
            if step == 0:
                return recv1[kind, h, x, z, y]
            count_z = 1 if "b" in past else 2 if "a" in past else 4
            count_y = 1 if "y" in past else 2
            slot = (0 if "x" in past else x * count_z) + zslot(z)
            if isinstance(y, slice):
                return landing[step - 1][p, pl.ds(slot * 2, 2)]
            return landing[step - 1][p, slot * count_y + (0 if count_y == 1 else y)]

        def zslot(z):
            if "a" not in past:
                return z
            return 0 if z is z_at else 1

        both_y = slice(None)
        xs = (x_at,) if "x" in past else (0, 1)
        ys = (y_at,) if "y" in past else (both_y,)
        zs = (z_at,) if "b" in past else (z_at, z_pair) if "a" in past else tuple(range(4))

        def put(x, z, y):
            where = place(x, z, y)
            grads[where] = add(grads[where], arrived(x, z, y))

        if step == 4:
            where = place(x_at, z_at, y_at)
            finish(p, add(grads[where], arrived(x_at, z_at, y_at)))
            return
        leg = legs[step]
        if leg == "x":
            away, keep, peer = [(1 - x_at, z, y) for z in zs for y in ys], [(x_at, z, y) for z in zs for y in ys], x_peer
        elif leg == "y":
            away, keep, peer = [(x, z, 1 - y_at) for x in xs for z in zs], [(x, z, y_at) for x in xs for z in zs], y_peer
        elif leg == "a":
            away = [(x, z, y) for x in xs for z in (z_next, z_far) for y in ys]
            keep, peer = [(x, z, y) for x in xs for z in (z_at, z_pair) for y in ys], za_peer
        else:
            away, keep, peer = [(x, z_pair, y) for x in xs for y in ys], [(x, z_at, y) for x in xs for y in ys], zb_peer
        for x, z, y in away:
            put(x, z, y)
        for count, (x, z, y) in enumerate(away):
            width = 2 if isinstance(y, slice) else 1
            dst = landing[step].at[p, pl.ds(count * 2, 2)] if width == 2 else landing[step].at[p, count]
            remote(grads.at[place(x, z, y)], dst, red_send.at[step, p], red_recv.at[step, p], peer).start()
        for x, z, y in keep:
            put(x, z, y)

    def finish(p, total):
        kind, at = p // 3, part(p)
        gmat_ref[kind, item, :, at] = total
        here = gmat_ref.at[kind, item, :, at]
        remote(here, here, gat_send.at[1, p], gat_recv.at[1, p], x_peer).start()
        remote(here, here, gat_send.at[0, p], gat_recv.at[0, p], core_peer).start()
        if p in (2, 3):
            remote(here, here, gat_send.at[2, p], gat_recv.at[2, p], far_peer).start()

    def forward_on(p):
        there = gmat_ref.at[p // 3, x_peer[1], :, part(p)]
        wait_bytes(there, gat_recv.at[1, p])
        if p not in (2, 3):
            remote(there, there, gat_send.at[2, p], gat_recv.at[2, p], core_peer).start()

    def final(c):
        hb[c] = (xbuf[c] + mixed_of(c, 1)).astype(BF16)
        pltpu.make_async_copy(hb.at[c], gin_hbm.at[c], out_sem.at[1]).start()

    def vectors_out():
        lanes = vsend.shape[2]
        vsend[...] = jnp.zeros_like(vsend)
        for d in range(8):
            at = d * (features // 2)
            for r in range(3):
                where = at + r * lanes
                vsend[d, r : r + 1, :] = vacc[where // features : where // features + 1, where % features : where % features + lanes]
            for r in range(5):
                vsend[d, 3 + r : 4 + r, :share] = vacc[4 + r : 5 + r, d * share : (d + 1) * share]
        for peer in peers:
            remote(vsend.at[peer[0]], vrecv.at[me], v_send.at[0], v_recv.at[0], peer).start()
        pltpu.make_async_copy(vsend.at[me], vrecv.at[me], v_recv.at[0]).start()

    def vectors_on():
        wait_bytes(vrecv, v_recv.at[0])
        vmid[...] = jnp.sum(vrecv[...], axis=0)
        remote(vmid, vlast.at[0], v_send.at[1], v_recv.at[1], core_peer).start()

    def vectors_over():
        wait_bytes(vlast.at[0], v_recv.at[1])
        vlast[1] = vmid[...] + vlast[0]
        remote(vlast.at[1], vlast.at[2], v_send.at[2], v_recv.at[2], x_peer).start()

    def vectors_end():
        wait_bytes(vlast.at[2], v_recv.at[2])
        gvec_ref[...] = vlast[1] + vlast[2]

    feed_up(0)
    send_back(0, 1)
    owners_sent(0, 2)
    feed_mid(0)
    turn(0, 2)
    send_back(0, 2)
    feed_down(0)
    feed_end(0)
    feed_up(1)
    send_owners(1, 0)
    feed_mid(1)
    feed_down(1)
    feed_end(1)
    send_owners(1, 1)
    feed_up(2)
    feed_mid(2)
    feed_down(2)
    product(3)
    return_sent(0, 0)
    turn(1, 0)
    send_back(1, 0)
    hop(3, 0)
    feed_end(2)
    send_owners(1, 2)
    product(4)
    product(5)
    hop(4, 0)
    hop(5, 0)
    return_sent(0, 1)
    turn(1, 1)
    send_back(1, 1)
    product(1)
    product(0)
    hop(3, 1)
    vectors_out()
    product(2)
    hop(0, 0)
    hop(2, 0)
    hop(5, 1)
    hop(1, 0)
    hop(3, 2)
    hop(0, 1)
    hop(5, 2)
    hop(4, 1)
    return_sent(0, 2)
    turn(1, 2)
    send_back(1, 2)
    final(0)
    hop(2, 1)
    hop(0, 2)
    vectors_on()
    hop(1, 1)
    hop(3, 3)
    hop(4, 2)
    hop(0, 3)
    vectors_over()
    hop(5, 3)
    final(1)
    hop(1, 2)
    hop(3, 4)
    hop(2, 2)
    hop(4, 3)
    hop(5, 4)
    hop(1, 3)
    hop(2, 3)
    hop(0, 4)
    hop(1, 4)
    final(2)
    hop(4, 4)
    hop(2, 4)
    forward_on(0)
    vectors_end()
    forward_on(4)
    forward_on(1)
    forward_on(5)
    forward_on(2)
    forward_on(3)

    out_copy(chunks - 1).wait()
    wait_bytes(hb, out_sem.at[1])
    for c in range(chunks):
        owners_sent(1, c)
        return_sent(1, c)
    for kind in range(2):
        for h in range(3):
            wait_bytes(recv1.at[kind, h], core_send.at[kind, h])
    for p in range(6):
        for step, ref in enumerate((hop0, hop1, hop2, hop3)):
            wait_bytes(ref.at[p], red_send.at[step, p])
        for leg in range(3):
            wait_bytes(hop3.at[p], gat_send.at[leg, p])
        wait_bytes(hop3.at[p], gat_recv.at[0, p])
        wait_bytes(hop3.at[p], gat_recv.at[2, p])
    wait_bytes(vrecv.at[pl.ds(0, 7)], v_send.at[0])
    wait_bytes(vlast.at[1], v_send.at[1])
    wait_bytes(vlast.at[1], v_send.at[2])


def finish_kernel(
    out_in, gin_in, gmat_in, gvec_in,
    out_ref, gin_ref, gwi_ref, gwo_ref, gci_ref, gco_ref, ggm_ref, gbm_ref, ggo_ref, gbo_ref,
    low, mv, res, wi, wo, sem_in, sem_out,
):
    chunks, features, share = low.shape[1], low.shape[3], mv.shape[2]
    loads = [pltpu.make_async_copy(gmat_in, mv, sem_in.at[0])]
    for k, src in enumerate((out_in, gin_in)):
        for c in range(chunks):
            loads.append(pltpu.make_async_copy(src.at[c], low.at[k, c], sem_in.at[len(loads)]))
    for load in loads:
        load.start()
    stores = []

    def put(src, dst):
        copy = pltpu.make_async_copy(src, dst, sem_out.at[len(stores)])
        copy.start()
        stores.append(copy)

    loads[0].wait()
    for q in range(4):
        wi[:, q * features : (q + 1) * features] = mv[0, q].astype(F32)
        wo[q * share : (q + 1) * share] = mv[1, q].astype(F32)
    put(wi, gwi_ref)
    put(wo, gwo_ref)
    for k, dst in enumerate((out_ref, gin_ref)):
        for c in range(chunks):
            loads[1 + k * chunks + c].wait()
            res[k, c] = low[k, c].astype(F32)
            put(res.at[k, c], dst.at[c])
    lanes = gvec_in.shape[1]
    for r in range(3):
        gci_ref[r * lanes : (r + 1) * lanes] = gvec_in[r]
    for r, ref in enumerate((gco_ref, ggm_ref, gbm_ref, ggo_ref, gbo_ref)):
        ref[...] = gvec_in[3 + r, :share]
    for copy in stores:
        copy.wait()


def exchange_body(inputs, w_in, c_in, w_out, c_out, gain_mix, bias_mix, gain_out, bias_out, cotangent):
    local_len, per_dev, features = inputs.shape
    parts = lax.axis_size("seq")
    period = local_len * parts
    share = features // parts
    per_chunk = per_dev // CHUNKS
    rows = per_chunk * local_len
    forward, unpack = packed_tables(features, parts)
    cos_seq, sin_seq = seq_tables(period)
    held = jnp.swapaxes(inputs, 0, 1).reshape(CHUNKS, rows, features)
    cot = jnp.swapaxes(cotangent, 0, 1).reshape(CHUNKS, rows, features)
    anywhere = pl.BlockSpec(memory_space=pl.ANY)
    whole = (CHUNKS, rows, features)
    vm, dma = pltpu.VMEM, pltpu.SemaphoreType.DMA
    inside = pl.BlockSpec(memory_space=pltpu.VMEM)
    out_low, gin_low, mats, vecs = pl.pallas_call(
        layer_kernel,
        out_shape=(
            jax.ShapeDtypeStruct(whole, BF16),
            jax.ShapeDtypeStruct(whole, BF16),
            jax.ShapeDtypeStruct((2, 4, share, features), BF16),
            jax.ShapeDtypeStruct((8, 128), F32),
        ),
        in_specs=[anywhere] * 4 + [inside] * 6 + [anywhere] * 4,
        out_specs=(anywhere, anywhere, inside, inside),
        scratch_shapes=[
            vm((features, features), BF16),
            vm((features, features), BF16),
            vm((period, period), BF16),
            vm((period, period), BF16),
            vm((16, features), F32),
            vm(whole, F32),
            vm(whole, F32),
            vm((4, 4, 2, share, features), BF16),
            vm((4, 2, 2, 2, share, features), BF16),
            vm((4, 192, features), F32),
            vm((CHUNKS, per_chunk, features, local_len), BF16),
            vm((2, CHUNKS, per_chunk, share, period), BF16),
            vm((CHUNKS, per_chunk, share, period), BF16),
            vm((CHUNKS, per_chunk, features, local_len), BF16),
            vm((4,) + whole, BF16),
            vm((4,) + whole, BF16),
            vm(whole, BF16),
            vm(whole, BF16),
            vm((4, rows, features), F32),
            vm((rows, features), F32),
            vm((rows, 128), F32),
            vm((rows, features), BF16),
            vm((16, features), F32),
            vm((2, 3, 2, 4, 2, share, features // 3), BF16),
            vm((6, 8, share, features // 3), BF16),
            vm((6, 4, share, features // 3), BF16),
            vm((6, 2, share, features // 3), BF16),
            vm((6, 1, share, features // 3), BF16),
            vm((8, 8, 128), F32),
            vm((8, 8, 128), F32),
            vm((8, 128), F32),
            vm((3, 8, 128), F32),
            dma((4,)),
            dma((CHUNKS,)),
            dma((CHUNKS,)),
            dma((4,)),
            dma((2, CHUNKS)),
            dma((2, CHUNKS)),
            dma((2, CHUNKS)),
            dma((2, CHUNKS)),
            dma((2,)),
            dma((2, 3)),
            dma((2, 3)),
            dma((4, 6)),
            dma((4, 6)),
            dma((3, 6)),
            dma((3, 6)),
            dma((3,)),
            dma((3,)),
        ],
        compiler_params=pltpu.CompilerParams(
            collective_id=0, has_side_effects=True, vmem_limit_bytes=62 * 1024 * 1024
        ),
    )(held, cot, w_in, w_out, c_in, c_out, gain_mix, bias_mix, gain_out, bias_out, forward, unpack, cos_seq, sin_seq)
    shape = (per_dev, local_len, features)
    vec = lambda n: jax.ShapeDtypeStruct((n,), F32)
    output, grad_inputs, grad_in, grad_out, grad_c_in, *others = pl.pallas_call(
        finish_kernel,
        in_specs=[anywhere] * 3 + [inside],
        out_specs=(anywhere,) * 4 + (inside,) * 6,
        out_shape=(
            jax.ShapeDtypeStruct(whole, F32),
            jax.ShapeDtypeStruct(whole, F32),
            jax.ShapeDtypeStruct((share, 4 * features), F32),
            jax.ShapeDtypeStruct((4 * share, features), F32),
            vec(4 * share),
        )
        + (vec(share),) * 5,
        scratch_shapes=[
            vm((2,) + whole, BF16),
            vm((2, 4, share, features), BF16),
            vm((2,) + whole, F32),
            vm((share, 4 * features), F32),
            vm((4 * share, features), F32),
            dma((1 + 2 * CHUNKS,)),
            dma((2 + 2 * CHUNKS,)),
        ],
        compiler_params=pltpu.CompilerParams(vmem_limit_bytes=60 * 1024 * 1024),
    )(out_low, gin_low, mats, vecs)
    output = jnp.swapaxes(output.reshape(shape), 0, 1)
    grad_inputs = jnp.swapaxes(grad_inputs.reshape(shape), 0, 1)
    return (output, grad_inputs, grad_in, grad_c_in, grad_out, *others)


def body(inputs, *rest):
    if lax.axis_size("seq") != 8 or lax.axis_size("item") != 4:
        return gather_body(inputs, *rest)
    return exchange_body(inputs, *rest)


def solution(mesh):
    placed = (
        P("seq", "item", None),
        P(),
        P(),
        P(),
        P(),
        P(),
        P(),
        P(),
        P(),
        P("seq", "item", None),
    )
    return jax.shard_map(
        body,
        mesh=mesh,
        in_specs=placed,
        out_specs=(
            P("seq", "item", None),
            P("seq", "item", None),
            P("seq", None),
            P("seq"),
            P("seq", None),
            P("seq"),
            P("seq"),
            P("seq"),
            P("seq"),
            P("seq"),
        ),
        check_vma=False,
    )
```

```python
import math

import jax
import jax.numpy as jnp
import numpy as np
from jax import lax
from jax.experimental import pallas as pl
from jax.experimental.pallas import tpu as pltpu
from jax.sharding import PartitionSpec as P


def table_block(row_ids, col_ids, period):
    products = row_ids[:, None] * col_ids[None, :] % period
    angles = products.astype(jnp.float32) * (2.0 * math.pi / period)
    return (jnp.cos(angles).astype(jnp.bfloat16), jnp.sin(angles).astype(jnp.bfloat16))


def plain_dot(left, right):
    return jnp.dot(left, right, preferred_element_type=jnp.float32)


def rows_dot(left, right):
    return lax.dot_general(
        left, right, (((0,), (0,)), ((), ())), preferred_element_type=jnp.float32
    )


def cols_dot(left, right):
    return lax.dot_general(
        left, right, (((1,), (1,)), ((), ())), preferred_element_type=jnp.float32
    )


def layer_norm(values, scales, shifts):
    average = jnp.mean(values, axis=-1, keepdims=True)
    centered = values - average
    variance = jnp.mean(centered * centered, axis=-1, keepdims=True)
    return centered * lax.rsqrt(variance + 1e-05) * scales + shifts


def gelu_exact(values):
    return jax.nn.gelu(values, approximate=False)


def gather_body(inputs, w_in, c_in, w_out, c_out, gain_mix, bias_mix, gain_out, bias_out, cotangent):
    local_len, per_dev, features = inputs.shape
    merged = per_dev * features
    period = local_len * lax.axis_size("seq")
    unit_scale = 1.0 / math.sqrt(period * features)
    own_rows = lax.axis_index("seq") * local_len + jnp.arange(local_len, dtype=jnp.int32)
    feat_ids = jnp.arange(features, dtype=jnp.int32)
    cos_hid, sin_hid = table_block(feat_ids, feat_ids, features)
    tokens = inputs.reshape(-1, features)
    tokens_low = tokens.astype(jnp.bfloat16)
    cos_part = (
        plain_dot(tokens_low, cos_hid).astype(jnp.bfloat16).reshape(local_len, per_dev, features)
    )
    sin_part = (
        plain_dot(tokens_low, sin_hid).astype(jnp.bfloat16).reshape(local_len, per_dev, features)
    )
    pieces = (
        lax.all_gather(cos_part, "seq", axis=0, tiled=True),
        lax.all_gather(sin_part, "seq", axis=0, tiled=True),
    )
    col_ids = jnp.arange(pieces[0].shape[0], dtype=jnp.int32)
    cos_blk, sin_blk = table_block(own_rows, col_ids, period)
    mixed = plain_dot(cos_blk, pieces[0].reshape(pieces[0].shape[0], -1)) - plain_dot(
        sin_blk, pieces[1].reshape(pieces[1].shape[0], -1)
    )
    mixed = (mixed * unit_scale).reshape(-1, features)
    hidden, pull_mix = jax.vjp(layer_norm, tokens + mixed, gain_mix, bias_mix)
    hidden_low = hidden.astype(jnp.bfloat16)
    w_in_low = w_in.astype(jnp.bfloat16)
    w_out_low = w_out.astype(jnp.bfloat16)
    pre = plain_dot(hidden_low, w_in_low) + c_in
    act, pull_gelu = jax.vjp(gelu_exact, pre)
    act_low = act.astype(jnp.bfloat16)
    branch = plain_dot(act_low, w_out_low) + c_out
    output, pull_out = jax.vjp(layer_norm, hidden + branch, gain_out, bias_out)
    g_sum2, grad_gain_out, grad_bias_out = pull_out(cotangent.reshape(-1, features))
    g_branch = g_sum2.astype(jnp.bfloat16)
    grad_c_out = jnp.sum(g_branch.astype(jnp.float32), axis=0)
    grad_w_out = rows_dot(act_low, g_branch)
    (g_act,) = pull_gelu(cols_dot(g_branch, w_out_low))
    g_pre = g_act.astype(jnp.bfloat16)
    grad_c_in = jnp.sum(g_pre.astype(jnp.float32), axis=0)
    grad_w_in = rows_dot(hidden_low, g_pre)
    g_hidden = g_sum2 + cols_dot(g_pre, w_in_low)
    g_sum1, grad_gain_mix, grad_bias_mix = pull_mix(g_hidden)
    g_mixed = g_sum1.astype(jnp.bfloat16).reshape(local_len, per_dev, features)
    empty = jnp.zeros((local_len, merged), jnp.float32)
    piece = lax.all_gather(g_mixed, "seq", axis=0, tiled=True)
    row_ids = jnp.arange(piece.shape[0], dtype=jnp.int32)
    cos_blk, sin_blk = table_block(row_ids, own_rows, period)
    flat = piece.reshape(piece.shape[0], -1)
    cycle_gc = rows_dot(cos_blk, flat)
    cycle_gs = (empty, empty)[1] - rows_dot(sin_blk, flat)
    g_cos = (cycle_gc * unit_scale).astype(jnp.bfloat16).reshape(-1, features)
    g_sin = (cycle_gs * unit_scale).astype(jnp.bfloat16).reshape(-1, features)
    grad_inputs = g_sum1 + cols_dot(g_cos, cos_hid) + cols_dot(g_sin, sin_hid)
    shards = (
        lax.psum_scatter(
            grad_w_in.astype(jnp.bfloat16), "seq", scatter_dimension=0, tiled=True
        ).astype(jnp.float32),
        lax.psum_scatter(
            grad_c_in.astype(jnp.bfloat16), "seq", scatter_dimension=0, tiled=True
        ).astype(jnp.float32),
        lax.psum_scatter(
            grad_w_out.astype(jnp.bfloat16), "seq", scatter_dimension=0, tiled=True
        ).astype(jnp.float32),
        lax.psum_scatter(
            grad_c_out.astype(jnp.bfloat16), "seq", scatter_dimension=0, tiled=True
        ).astype(jnp.float32),
        lax.psum_scatter(
            grad_gain_mix.astype(jnp.bfloat16), "seq", scatter_dimension=0, tiled=True
        ).astype(jnp.float32),
        lax.psum_scatter(
            grad_bias_mix.astype(jnp.bfloat16), "seq", scatter_dimension=0, tiled=True
        ).astype(jnp.float32),
        lax.psum_scatter(
            grad_gain_out.astype(jnp.bfloat16), "seq", scatter_dimension=0, tiled=True
        ).astype(jnp.float32),
        lax.psum_scatter(
            grad_bias_out.astype(jnp.bfloat16), "seq", scatter_dimension=0, tiled=True
        ).astype(jnp.float32),
    )
    summed = (
        lax.psum(shards[0].astype(jnp.bfloat16), "item").astype(jnp.float32),
        lax.psum(shards[1].astype(jnp.bfloat16), "item").astype(jnp.float32),
        lax.psum(shards[2].astype(jnp.bfloat16), "item").astype(jnp.float32),
        lax.psum(shards[3].astype(jnp.bfloat16), "item").astype(jnp.float32),
        lax.psum(shards[4].astype(jnp.bfloat16), "item").astype(jnp.float32),
        lax.psum(shards[5].astype(jnp.bfloat16), "item").astype(jnp.float32),
        lax.psum(shards[6].astype(jnp.bfloat16), "item").astype(jnp.float32),
        lax.psum(shards[7].astype(jnp.bfloat16), "item").astype(jnp.float32),
    )
    return (
        output.reshape(inputs.shape),
        grad_inputs.reshape(inputs.shape),
        summed[0],
        summed[1],
        summed[2],
        summed[3],
        summed[4],
        summed[5],
        summed[6],
        summed[7],
    )


def packed_tables(features, parts):
    half = features // 2
    share = half // parts
    index = np.arange(features)
    forward = np.zeros((features, features), np.float32)
    unpack = np.zeros((features, features), np.float32)
    for low in range(half):
        block, place = divmod(low, share)
        cos_slot = block * 2 * share + place
        sin_slot = cos_slot + share
        angles = (index * low % features).astype(np.float32) * np.float32(2.0 * math.pi / features)
        forward[cos_slot] = np.cos(angles)
        unpack[cos_slot, low] = 1.0
        if low:
            unpack[cos_slot, features - low] = 1.0
            forward[sin_slot] = np.sin(angles)
            unpack[sin_slot, low] = -1.0
            unpack[sin_slot, features - low] = 1.0
        else:
            forward[sin_slot] = 1.0 - 2.0 * (index % 2)
            unpack[sin_slot, half] = 1.0
    return forward.astype(jnp.bfloat16), unpack.astype(jnp.bfloat16)


def seq_tables(period):
    index = np.arange(period)
    angles = (index[:, None] * index[None, :] % period).astype(np.float32)
    angles = angles * np.float32(2.0 * math.pi / period)
    return np.cos(angles).astype(jnp.bfloat16), np.sin(angles).astype(jnp.bfloat16)


MESH = pl.DeviceIdType.MESH
CHUNKS = 3
BF16, F32 = jnp.bfloat16, jnp.float32


def dot(left, right, left_dim, right_dim):
    return lax.dot_general(
        left, right, (((left_dim,), (right_dim,)), ((), ())), preferred_element_type=F32
    )


def row_mean(values):
    return jnp.mean(values, axis=-1, keepdims=True)


def layer_kernel(
    x_hbm, cot_hbm, win_hbm, wout_hbm, cin_ref, cout_ref, gmix_ref, bmix_ref, gout_ref, bout_ref,
    fwd_hbm, unp_hbm, cos_hbm, sin_hbm,
    out_hbm, gin_hbm, gmat_ref, gvec_ref,
    fwd_v, unp_v, cos_v, sin_v, prm_v, xbuf, cotb, win_v, wout_v, stage,
    ysend, yrecv, zsend, zrecv, actb, gpb, hb, gbb, dgb, acc, r1b, ostage, vacc,
    recv1, hop0, hop1, hop2, hop3, vsend, vrecv, vmid, vlast,
    ld_sem, x_sem, cot_sem, stg_sem, a_send, a_recv, b_send, b_recv, out_sem,
    core_send, core_recv, red_send, red_recv, gat_send, gat_recv, v_send, v_recv,
):
    chunks, rows, features = xbuf.shape
    per_chunk, share, period = yrecv.shape[2], yrecv.shape[3], yrecv.shape[4]
    own_len = period // 8
    half = share // 2
    unit_scale = 1.0 / math.sqrt(period * features)

    me, item = lax.axis_index("seq"), lax.axis_index("item")
    peers = [(lax.rem(me + k, 8), item) for k in range(1, 8)]
    z_lo, y_at = lax.rem(lax.div(me, 2), 2), lax.rem(me, 2)
    z_at, z_hi = lax.div(me, 2), lax.div(me, 4)
    core, x_at = lax.rem(item, 2), lax.div(item, 2)
    core_peer = (me, item + 1 - 2 * core)
    x_peer = (me, item + 2 - 4 * x_at)
    far_peer = (me, lax.rem(item + 2, 4) + 1 - 2 * core)
    y_peer = (me + 1 - 2 * y_at, item)
    za_peer = (me + 2 - 4 * z_lo, item)
    zb_peer = (me + 4 - 8 * z_hi, item)

    def remote(src, dst, send, recv, peer):
        return pltpu.make_async_remote_copy(
            src_ref=src, dst_ref=dst, send_sem=send, recv_sem=recv, device_id=peer, device_id_type=MESH
        )

    def wait_bytes(ref, sem):
        pltpu.make_async_copy(ref, ref, sem).wait()

    tables = [
        pltpu.make_async_copy(src, dst, ld_sem.at[i])
        for i, (src, dst) in enumerate(
            [(fwd_hbm, fwd_v), (cos_hbm, cos_v), (sin_hbm, sin_v), (unp_hbm, unp_v)]
        )
    ]
    x_loads = [pltpu.make_async_copy(x_hbm.at[c], xbuf.at[c], x_sem.at[c]) for c in range(chunks)]
    cot_loads = [pltpu.make_async_copy(cot_hbm.at[c], cotb.at[c], cot_sem.at[c]) for c in range(chunks)]
    x_loads[0].start()
    tables[0].start()
    for load in x_loads[1:] + tables[1:]:
        load.start()

    barrier = pltpu.get_barrier_semaphore()
    everyone = peers + [core_peer, x_peer, far_peer]
    for peer in everyone:
        pl.semaphore_signal(barrier, inc=1, device_id=peer, device_id_type=MESH)

    slots, piece = stage.shape[0], stage.shape[1]
    per_block = features // piece
    steps = 8 * per_block

    def weight_load(step, part, slot):
        block, at = lax.div(step, per_block), lax.rem(step, per_block) * piece
        if part == 0:
            cols = pl.ds(pl.multiple_of(block * features, features), features)
            src = win_hbm.at[pl.ds(pl.multiple_of(at, piece), piece), cols]
        else:
            src = wout_hbm.at[pl.ds(pl.multiple_of(block * features + at, piece), piece), :]
        return pltpu.make_async_copy(src, stage.at[slot], stg_sem.at[slot])

    def cast_weights(part):
        total = 4 * per_block
        groups = piece // share

        def one(step, carry):
            slot = lax.rem(step, slots)
            weight_load(step, part, slot).wait()
            block, at = lax.div(step, per_block), lax.rem(step, per_block) * groups
            value = stage[slot].astype(BF16)
            for g in range(groups):
                where = at + g
                rows_of = value[g * share : (g + 1) * share]
                if part == 0:
                    win_v[block, lax.div(where, 2), lax.rem(where, 2)] = rows_of
                else:
                    wout_v[block, lax.div(where, 4), lax.rem(lax.div(where, 2), 2), lax.rem(where, 2)] = rows_of

            @pl.when(step + slots < total)
            def _():
                weight_load(step + slots, part, slot).start()

            return carry

        lax.fori_loop(0, total, one, 0)

    def first_loads(part):
        for slot in range(slots):
            weight_load(jnp.int32(slot), part, jnp.int32(slot)).start()

    def in_block(j):
        return win_v[j].reshape(features, features)

    def out_block(j):
        return wout_v[j].reshape(features, features)

    def pack(c, low):
        packed = dot(fwd_v[...], low, 1, 1).astype(BF16)
        for s in range(per_chunk):
            ysend[c, s] = packed[:, s * own_len : (s + 1) * own_len]

    def send_owners(way, c):
        mine = pl.ds(pl.multiple_of(me * own_len, own_len), own_len)
        for peer in peers:
            to = pl.ds(pl.multiple_of(peer[0] * share, share), share)
            remote(
                ysend.at[c, :, to, :], yrecv.at[way, c, :, :, mine], a_send.at[way, c], a_recv.at[way, c], peer
            ).start()
        own = pl.ds(pl.multiple_of(me * share, share), share)
        pltpu.make_async_copy(ysend.at[c, :, own, :], yrecv.at[way, c, :, :, mine], a_recv.at[way, c]).start()

    def owners_sent(way, c):
        wait_bytes(ysend.at[c, :, pl.ds(0, 7 * share), :], a_send.at[way, c])

    def turn(way, c):
        wait_bytes(yrecv.at[way, c], a_recv.at[way, c])
        held = yrecv[way, c]
        cos_rows = held[:, :half].reshape(per_chunk * half, period)
        sin_rows = held[:, half:].reshape(per_chunk * half, period)
        mid_rows = held[:, half : half + 16].reshape(per_chunk * 16, period)
        by_cos = dot(cos_rows, cos_v[...], 1, 0) * unit_scale
        by_sin = dot(sin_rows, sin_v[...], 1, 0) * unit_scale
        by_mid = dot(mid_rows, cos_v[...], 1, 0) * unit_scale
        top = lax.broadcasted_iota(jnp.int32, (16, period), 0) == 0
        top = jnp.logical_and(top, me == 0)
        for s in range(per_chunk):
            zsend[c, s, :half] = by_cos[s * half : (s + 1) * half].astype(BF16)
            sin_part = by_sin[s * half : (s + 1) * half]
            zsend[c, s, half : half + 16] = jnp.where(
                top, by_mid[s * 16 : (s + 1) * 16], sin_part[:16]
            ).astype(BF16)
            zsend[c, s, half + 16 :] = sin_part[16:].astype(BF16)

    def send_back(way, c):
        mine = pl.ds(pl.multiple_of(me * share, share), share)
        for peer in peers:
            to = pl.ds(pl.multiple_of(peer[0] * own_len, own_len), own_len)
            remote(
                zsend.at[c, :, :, to], zrecv.at[c, :, mine, :], b_send.at[way, c], b_recv.at[way, c], peer
            ).start()
        own = pl.ds(pl.multiple_of(me * own_len, own_len), own_len)
        pltpu.make_async_copy(zsend.at[c, :, :, own], zrecv.at[c, :, mine, :], b_recv.at[way, c]).start()

    def return_sent(way, c):
        wait_bytes(zsend.at[c, :, :, pl.ds(0, 7 * own_len)], b_send.at[way, c])

    def mixed_of(c, way=0):
        wait_bytes(zrecv.at[c], b_recv.at[way, c])
        held = jnp.concatenate([zrecv[c, s] for s in range(per_chunk)], axis=1)
        return dot(held, unp_v[...], 0, 0)

    tables[0].wait()
    x_loads[0].wait()
    first_loads(0)
    pack(0, xbuf[0].astype(BF16))
    pl.semaphore_wait(barrier, len(everyone))
    send_owners(0, 0)
    x_loads[1].wait()
    pack(1, xbuf[1].astype(BF16))
    for load in cot_loads:
        load.start()
    vacc[...] = jnp.zeros_like(vacc)
    for j in range(4):
        prm_v[j : j + 1] = cin_ref[j * features : (j + 1) * features].reshape(1, features)
    for r, ref in enumerate((cout_ref, gmix_ref, bmix_ref, gout_ref, bout_ref)):
        prm_v[4 + r : 5 + r] = ref[...].reshape(1, features)
    cast_weights(0)
    first_loads(1)
    send_owners(0, 1)
    x_loads[2].wait()
    pack(2, xbuf[2].astype(BF16))
    cast_weights(1)
    for load in tables[1:]:
        load.wait()
    turn(0, 0)
    send_back(0, 0)
    owners_sent(0, 0)
    owners_sent(0, 1)
    send_owners(0, 2)
    turn(0, 1)

    gain_mix, bias_mix = prm_v[5:6], prm_v[6:7]
    gain_out, bias_out, c_out = prm_v[7:8], prm_v[8:9], prm_v[4:5]

    def out_copy(c):
        return pltpu.make_async_copy(ostage, out_hbm.at[c], out_sem.at[0])

    def feed_up(c, mixed=None):
        value = xbuf[c] + (mixed_of(c) if mixed is None else mixed)
        value = value - row_mean(value)
        scale = lax.rsqrt(row_mean(value * value) + 1e-05)
        normal = value * scale
        r1b[...] = jnp.broadcast_to(scale, r1b.shape)
        xbuf[c] = normal
        hidden = normal * gain_mix + bias_mix
        hb[c] = hidden.astype(BF16)
        acc[...] = hidden + c_out

        def up(j, carry):
            pre = dot(hb[c], in_block(j), 1, 0) + prm_v[pl.ds(j, 1)]
            prob = 0.5 + 0.5 * lax.erf(pre * math.sqrt(0.5))
            density = jnp.exp(-0.5 * pre * pre) * (1.0 / math.sqrt(2.0 * math.pi))
            act = (pre * prob).astype(BF16)
            dgb[j] = prob + pre * density
            actb[j, c] = act
            acc[...] += dot(act, out_block(j), 1, 0)
            return carry

        lax.fori_loop(0, 4, up, 0, unroll=True)

    def feed_mid(c):
        value = acc[...]
        value = value - row_mean(value)
        scale = lax.rsqrt(row_mean(value * value) + 1e-05)
        normal = value * scale

        if c > 0:
            out_copy(c - 1).wait()
        ostage[...] = (normal * gain_out + bias_out).astype(BF16)
        out_copy(c).start()
        cot_loads[c].wait()
        cot = cotb[c]
        vacc[7:8] += jnp.sum(cot * normal, axis=0, keepdims=True)
        vacc[8:9] += jnp.sum(cot, axis=0, keepdims=True)
        scaled = cot * gain_out
        g_sum2 = scale * (scaled - row_mean(scaled) - normal * row_mean(scaled * normal))
        low = g_sum2.astype(BF16)
        gbb[c] = low
        vacc[4:5] += jnp.sum(low.astype(F32), axis=0, keepdims=True)
        acc[...] = g_sum2

    def feed_down(c):
        for j in range(4):
            g_pre = (dot(gbb[c], out_block(j), 1, 1) * dgb[j]).astype(BF16)
            gpb[j, c] = g_pre
            vacc[j : j + 1] += jnp.sum(g_pre.astype(F32), axis=0, keepdims=True)

    def feed_end(c):
        for j in range(4):
            acc[...] += dot(gpb[j, c], in_block(j), 1, 1)
        g_hidden = acc[...]
        normal = xbuf[c]
        vacc[5:6] += jnp.sum(g_hidden * normal, axis=0, keepdims=True)
        vacc[6:7] += jnp.sum(g_hidden, axis=0, keepdims=True)
        scaled = g_hidden * gain_mix
        g_sum1 = r1b[:, :1] * (scaled - row_mean(scaled) - normal * row_mean(scaled * normal))
        xbuf[c] = g_sum1
        pack(c, g_sum1.astype(BF16))

    cut = hop3.shape[3]
    routes = ('xyz', 'xyz', 'yxz', 'xzy', 'yxz', 'xzy')
    z_pair = lax.rem(z_at + 2, 4)
    z_next = z_at + 1 - 2 * z_lo
    z_far = lax.rem(z_next + 2, 4)

    def part(p):
        return pl.ds((p % 3) * cut, cut)

    def add(*terms):
        total = terms[0].astype(F32)
        for term in terms[1:]:
            total = total + term.astype(F32)
        return total.astype(BF16)

    def product(p):
        kind, h, at = p // 3, p % 3, part(p)
        if kind == 0:
            for away in (1, 0):
                for x in range(2):
                    q = 2 * x + (1 - core if away else core)
                    grad = dot(hb[...].reshape(-1, features), gpb[q, :, :, at].reshape(-1, cut), 0, 0)
                    win_v[q, :, :, :, at] = grad.astype(BF16).reshape(4, 2, share, cut)
                    if away:
                        remote(
                            win_v.at[q, :, :, :, at], recv1.at[0, h, x], core_send.at[0, h], core_recv.at[0, h], core_peer
                        ).start()
        else:
            for j in range(4):
                grad = dot(actb[j].reshape(-1, features), gbb[:, :, at].reshape(-1, cut), 0, 0)
                wout_v[j, :, :, :, :, at] = grad.astype(BF16).reshape(2, 2, 2, share, cut)
            for x in range(2):
                remote(
                    wout_v.at[:, :, x, 1 - core, :, at], recv1.at[1, h, x], core_send.at[1, h], core_recv.at[1, h], core_peer
                ).start()

    def hop(p, step):
        kind, h, at = p // 3, p % 3, part(p)
        legs = routes[p].replace("z", "ab")
        past = legs[:step]
        grads = (win_v, wout_v)[kind]
        landing = (hop0, hop1, hop2, hop3)
        if step == 0:
            wait_bytes(recv1.at[kind, h], core_recv.at[kind, h])
        else:
            wait_bytes(landing[step - 1].at[p], red_recv.at[step - 1, p])

        def place(x, z, y):
            return (2 * x + core, z, y, slice(None), at) if kind == 0 else (z, y, x, core, slice(None), at)

        def arrived(x, z, y):
            if step == 0:
                return recv1[kind, h, x, z, y]
            count_z = 1 if "b" in past else 2 if "a" in past else 4
            count_y = 1 if "y" in past else 2
            slot = (0 if "x" in past else x * count_z) + zslot(z)
            if isinstance(y, slice):
                return landing[step - 1][p, pl.ds(slot * 2, 2)]
            return landing[step - 1][p, slot * count_y + (0 if count_y == 1 else y)]

        def zslot(z):
            if "a" not in past:
                return z
            return 0 if z is z_at else 1

        both_y = slice(None)
        xs = (x_at,) if "x" in past else (0, 1)
        ys = (y_at,) if "y" in past else (both_y,)
        zs = (z_at,) if "b" in past else (z_at, z_pair) if "a" in past else tuple(range(4))

        def put(x, z, y):
            where = place(x, z, y)
            grads[where] = add(grads[where], arrived(x, z, y))

        if step == 4:
            where = place(x_at, z_at, y_at)
            finish(p, add(grads[where], arrived(x_at, z_at, y_at)))
            return
        leg = legs[step]
        if leg == "x":
            away, keep, peer = [(1 - x_at, z, y) for z in zs for y in ys], [(x_at, z, y) for z in zs for y in ys], x_peer
        elif leg == "y":
            away, keep, peer = [(x, z, 1 - y_at) for x in xs for z in zs], [(x, z, y_at) for x in xs for z in zs], y_peer
        elif leg == "a":
            away = [(x, z, y) for x in xs for z in (z_next, z_far) for y in ys]
            keep, peer = [(x, z, y) for x in xs for z in (z_at, z_pair) for y in ys], za_peer
        else:
            away, keep, peer = [(x, z_pair, y) for x in xs for y in ys], [(x, z_at, y) for x in xs for y in ys], zb_peer
        for x, z, y in away:
            put(x, z, y)
        for count, (x, z, y) in enumerate(away):
            width = 2 if isinstance(y, slice) else 1
            dst = landing[step].at[p, pl.ds(count * 2, 2)] if width == 2 else landing[step].at[p, count]
            remote(grads.at[place(x, z, y)], dst, red_send.at[step, p], red_recv.at[step, p], peer).start()
        for x, z, y in keep:
            put(x, z, y)

    def finish(p, total):
        kind, at = p // 3, part(p)
        gmat_ref[kind, item, :, at] = total
        here = gmat_ref.at[kind, item, :, at]
        remote(here, here, gat_send.at[1, p], gat_recv.at[1, p], x_peer).start()
        remote(here, here, gat_send.at[0, p], gat_recv.at[0, p], core_peer).start()
        if p in (2, 3):
            remote(here, here, gat_send.at[2, p], gat_recv.at[2, p], far_peer).start()

    def forward_on(p):
        there = gmat_ref.at[p // 3, x_peer[1], :, part(p)]
        wait_bytes(there, gat_recv.at[1, p])
        if p not in (2, 3):
            remote(there, there, gat_send.at[2, p], gat_recv.at[2, p], core_peer).start()

    def final(c):
        hb[c] = (xbuf[c] + mixed_of(c, 1)).astype(BF16)
        pltpu.make_async_copy(hb.at[c], gin_hbm.at[c], out_sem.at[1]).start()

    def vectors_out():
        lanes = vsend.shape[2]
        vsend[...] = jnp.zeros_like(vsend)
        for d in range(8):
            at = d * (features // 2)
            for r in range(3):
                where = at + r * lanes
                vsend[d, r : r + 1, :] = vacc[where // features : where // features + 1, where % features : where % features + lanes]
            for r in range(5):
                vsend[d, 3 + r : 4 + r, :share] = vacc[4 + r : 5 + r, d * share : (d + 1) * share]
        for peer in peers:
            remote(vsend.at[peer[0]], vrecv.at[me], v_send.at[0], v_recv.at[0], peer).start()
        pltpu.make_async_copy(vsend.at[me], vrecv.at[me], v_recv.at[0]).start()

    def vectors_on():
        wait_bytes(vrecv, v_recv.at[0])
        vmid[...] = jnp.sum(vrecv[...], axis=0)
        remote(vmid, vlast.at[0], v_send.at[1], v_recv.at[1], core_peer).start()

    def vectors_over():
        wait_bytes(vlast.at[0], v_recv.at[1])
        vlast[1] = vmid[...] + vlast[0]
        remote(vlast.at[1], vlast.at[2], v_send.at[2], v_recv.at[2], x_peer).start()

    def vectors_end():
        wait_bytes(vlast.at[2], v_recv.at[2])
        gvec_ref[...] = vlast[1] + vlast[2]

    feed_up(0)
    send_back(0, 1)
    owners_sent(0, 2)
    feed_mid(0)
    turn(0, 2)
    send_back(0, 2)
    feed_down(0)
    feed_end(0)
    feed_up(1)
    send_owners(1, 0)
    feed_mid(1)
    feed_down(1)
    feed_end(1)
    send_owners(1, 1)
    feed_up(2)
    feed_mid(2)
    feed_down(2)
    product(3)
    return_sent(0, 0)
    turn(1, 0)
    send_back(1, 0)
    hop(3, 0)
    feed_end(2)
    send_owners(1, 2)
    product(4)
    product(5)
    hop(4, 0)
    hop(5, 0)
    return_sent(0, 1)
    turn(1, 1)
    send_back(1, 1)
    product(1)
    product(0)
    hop(3, 1)
    vectors_out()
    product(2)
    hop(0, 0)
    hop(2, 0)
    hop(5, 1)
    hop(1, 0)
    hop(3, 2)
    hop(0, 1)
    hop(5, 2)
    hop(4, 1)
    return_sent(0, 2)
    turn(1, 2)
    send_back(1, 2)
    final(0)
    hop(2, 1)
    hop(0, 2)
    vectors_on()
    hop(1, 1)
    hop(3, 3)
    hop(4, 2)
    hop(0, 3)
    vectors_over()
    hop(5, 3)
    final(1)
    hop(1, 2)
    hop(3, 4)
    hop(2, 2)
    hop(4, 3)
    hop(5, 4)
    hop(1, 3)
    hop(2, 3)
    hop(0, 4)
    hop(1, 4)
    final(2)
    hop(4, 4)
    hop(2, 4)
    forward_on(0)
    vectors_end()
    forward_on(4)
    forward_on(1)
    forward_on(5)
    forward_on(2)
    forward_on(3)

    out_copy(chunks - 1).wait()
    wait_bytes(hb, out_sem.at[1])
    for c in range(chunks):
        owners_sent(1, c)
        return_sent(1, c)
    for kind in range(2):
        for h in range(3):
            wait_bytes(recv1.at[kind, h], core_send.at[kind, h])
    for p in range(6):
        for step, ref in enumerate((hop0, hop1, hop2, hop3)):
            wait_bytes(ref.at[p], red_send.at[step, p])
        for leg in range(3):
            wait_bytes(hop3.at[p], gat_send.at[leg, p])
        wait_bytes(hop3.at[p], gat_recv.at[0, p])
        wait_bytes(hop3.at[p], gat_recv.at[2, p])
    wait_bytes(vrecv.at[pl.ds(0, 7)], v_send.at[0])
    wait_bytes(vlast.at[1], v_send.at[1])
    wait_bytes(vlast.at[1], v_send.at[2])


def exchange_body(inputs, w_in, c_in, w_out, c_out, gain_mix, bias_mix, gain_out, bias_out, cotangent):
    local_len, per_dev, features = inputs.shape
    parts = lax.axis_size("seq")
    period = local_len * parts
    share = features // parts
    per_chunk = per_dev // CHUNKS
    rows = per_chunk * local_len
    forward, unpack = packed_tables(features, parts)
    cos_seq, sin_seq = seq_tables(period)
    held = jnp.swapaxes(inputs, 0, 1).reshape(CHUNKS, rows, features)
    cot = jnp.swapaxes(cotangent, 0, 1).reshape(CHUNKS, rows, features)
    anywhere = pl.BlockSpec(memory_space=pl.ANY)
    whole = (CHUNKS, rows, features)
    vm, dma = pltpu.VMEM, pltpu.SemaphoreType.DMA
    inside = pl.BlockSpec(memory_space=pltpu.VMEM)
    out_low, gin_low, mats, vecs = pl.pallas_call(
        layer_kernel,
        out_shape=(
            jax.ShapeDtypeStruct(whole, BF16),
            jax.ShapeDtypeStruct(whole, BF16),
            jax.ShapeDtypeStruct((2, 4, share, features), BF16),
            jax.ShapeDtypeStruct((8, 128), F32),
        ),
        in_specs=[anywhere] * 4 + [inside] * 6 + [anywhere] * 4,
        out_specs=(anywhere, anywhere, inside, inside),
        scratch_shapes=[
            vm((features, features), BF16),
            vm((features, features), BF16),
            vm((period, period), BF16),
            vm((period, period), BF16),
            vm((16, features), F32),
            vm(whole, F32),
            vm(whole, F32),
            vm((4, 4, 2, share, features), BF16),
            vm((4, 2, 2, 2, share, features), BF16),
            vm((4, 192, features), F32),
            vm((CHUNKS, per_chunk, features, local_len), BF16),
            vm((2, CHUNKS, per_chunk, share, period), BF16),
            vm((CHUNKS, per_chunk, share, period), BF16),
            vm((CHUNKS, per_chunk, features, local_len), BF16),
            vm((4,) + whole, BF16),
            vm((4,) + whole, BF16),
            vm(whole, BF16),
            vm(whole, BF16),
            vm((4, rows, features), F32),
            vm((rows, features), F32),
            vm((rows, 128), F32),
            vm((rows, features), BF16),
            vm((16, features), F32),
            vm((2, 3, 2, 4, 2, share, features // 3), BF16),
            vm((6, 8, share, features // 3), BF16),
            vm((6, 4, share, features // 3), BF16),
            vm((6, 2, share, features // 3), BF16),
            vm((6, 1, share, features // 3), BF16),
            vm((8, 8, 128), F32),
            vm((8, 8, 128), F32),
            vm((8, 128), F32),
            vm((3, 8, 128), F32),
            dma((4,)),
            dma((CHUNKS,)),
            dma((CHUNKS,)),
            dma((4,)),
            dma((2, CHUNKS)),
            dma((2, CHUNKS)),
            dma((2, CHUNKS)),
            dma((2, CHUNKS)),
            dma((2,)),
            dma((2, 3)),
            dma((2, 3)),
            dma((4, 6)),
            dma((4, 6)),
            dma((3, 6)),
            dma((3, 6)),
            dma((3,)),
            dma((3,)),
        ],
        compiler_params=pltpu.CompilerParams(
            collective_id=0, has_side_effects=True, vmem_limit_bytes=62 * 1024 * 1024
        ),
    )(held, cot, w_in, w_out, c_in, c_out, gain_mix, bias_mix, gain_out, bias_out, forward, unpack, cos_seq, sin_seq)
    shape = (per_dev, local_len, features)
    grad_in = jnp.swapaxes(mats[0], 0, 1).reshape(share, 4 * features).astype(F32)
    grad_out = mats[1].reshape(4 * share, features).astype(F32)
    return (
        jnp.swapaxes(out_low.reshape(shape).astype(F32), 0, 1),
        jnp.swapaxes(gin_low.reshape(shape).astype(F32), 0, 1),
        grad_in,
        vecs[:3].reshape(-1),
        grad_out,
    ) + tuple(vecs[3 + r, :share] for r in range(5))


def body(inputs, *rest):
    if lax.axis_size("seq") != 8 or lax.axis_size("item") != 4:
        return gather_body(inputs, *rest)
    return exchange_body(inputs, *rest)


def solution(mesh):
    placed = (
        P("seq", "item", None),
        P(),
        P(),
        P(),
        P(),
        P(),
        P(),
        P(),
        P(),
        P("seq", "item", None),
    )
    return jax.shard_map(
        body,
        mesh=mesh,
        in_specs=placed,
        out_specs=(
            P("seq", "item", None),
            P("seq", "item", None),
            P("seq", None),
            P("seq"),
            P("seq", None),
            P("seq"),
            P("seq"),
            P("seq"),
            P("seq"),
            P("seq"),
        ),
        check_vma=False,
    )
```

```python
import math

import jax
import jax.numpy as jnp
import numpy as np
from jax import lax
from jax.experimental import pallas as pl
from jax.experimental.pallas import tpu as pltpu
from jax.sharding import PartitionSpec as P


def table_block(row_ids, col_ids, period):
    products = row_ids[:, None] * col_ids[None, :] % period
    angles = products.astype(jnp.float32) * (2.0 * math.pi / period)
    return (jnp.cos(angles).astype(jnp.bfloat16), jnp.sin(angles).astype(jnp.bfloat16))


def plain_dot(left, right):
    return jnp.dot(left, right, preferred_element_type=jnp.float32)


def rows_dot(left, right):
    return lax.dot_general(
        left, right, (((0,), (0,)), ((), ())), preferred_element_type=jnp.float32
    )


def cols_dot(left, right):
    return lax.dot_general(
        left, right, (((1,), (1,)), ((), ())), preferred_element_type=jnp.float32
    )


def layer_norm(values, scales, shifts):
    average = jnp.mean(values, axis=-1, keepdims=True)
    centered = values - average
    variance = jnp.mean(centered * centered, axis=-1, keepdims=True)
    return centered * lax.rsqrt(variance + 1e-05) * scales + shifts


def gelu_exact(values):
    return jax.nn.gelu(values, approximate=False)


def gather_body(inputs, w_in, c_in, w_out, c_out, gain_mix, bias_mix, gain_out, bias_out, cotangent):
    local_len, per_dev, features = inputs.shape
    merged = per_dev * features
    period = local_len * lax.axis_size("seq")
    unit_scale = 1.0 / math.sqrt(period * features)
    own_rows = lax.axis_index("seq") * local_len + jnp.arange(local_len, dtype=jnp.int32)
    feat_ids = jnp.arange(features, dtype=jnp.int32)
    cos_hid, sin_hid = table_block(feat_ids, feat_ids, features)
    tokens = inputs.reshape(-1, features)
    tokens_low = tokens.astype(jnp.bfloat16)
    cos_part = (
        plain_dot(tokens_low, cos_hid).astype(jnp.bfloat16).reshape(local_len, per_dev, features)
    )
    sin_part = (
        plain_dot(tokens_low, sin_hid).astype(jnp.bfloat16).reshape(local_len, per_dev, features)
    )
    pieces = (
        lax.all_gather(cos_part, "seq", axis=0, tiled=True),
        lax.all_gather(sin_part, "seq", axis=0, tiled=True),
    )
    col_ids = jnp.arange(pieces[0].shape[0], dtype=jnp.int32)
    cos_blk, sin_blk = table_block(own_rows, col_ids, period)
    mixed = plain_dot(cos_blk, pieces[0].reshape(pieces[0].shape[0], -1)) - plain_dot(
        sin_blk, pieces[1].reshape(pieces[1].shape[0], -1)
    )
    mixed = (mixed * unit_scale).reshape(-1, features)
    hidden, pull_mix = jax.vjp(layer_norm, tokens + mixed, gain_mix, bias_mix)
    hidden_low = hidden.astype(jnp.bfloat16)
    w_in_low = w_in.astype(jnp.bfloat16)
    w_out_low = w_out.astype(jnp.bfloat16)
    pre = plain_dot(hidden_low, w_in_low) + c_in
    act, pull_gelu = jax.vjp(gelu_exact, pre)
    act_low = act.astype(jnp.bfloat16)
    branch = plain_dot(act_low, w_out_low) + c_out
    output, pull_out = jax.vjp(layer_norm, hidden + branch, gain_out, bias_out)
    g_sum2, grad_gain_out, grad_bias_out = pull_out(cotangent.reshape(-1, features))
    g_branch = g_sum2.astype(jnp.bfloat16)
    grad_c_out = jnp.sum(g_branch.astype(jnp.float32), axis=0)
    grad_w_out = rows_dot(act_low, g_branch)
    (g_act,) = pull_gelu(cols_dot(g_branch, w_out_low))
    g_pre = g_act.astype(jnp.bfloat16)
    grad_c_in = jnp.sum(g_pre.astype(jnp.float32), axis=0)
    grad_w_in = rows_dot(hidden_low, g_pre)
    g_hidden = g_sum2 + cols_dot(g_pre, w_in_low)
    g_sum1, grad_gain_mix, grad_bias_mix = pull_mix(g_hidden)
    g_mixed = g_sum1.astype(jnp.bfloat16).reshape(local_len, per_dev, features)
    empty = jnp.zeros((local_len, merged), jnp.float32)
    piece = lax.all_gather(g_mixed, "seq", axis=0, tiled=True)
    row_ids = jnp.arange(piece.shape[0], dtype=jnp.int32)
    cos_blk, sin_blk = table_block(row_ids, own_rows, period)
    flat = piece.reshape(piece.shape[0], -1)
    cycle_gc = rows_dot(cos_blk, flat)
    cycle_gs = (empty, empty)[1] - rows_dot(sin_blk, flat)
    g_cos = (cycle_gc * unit_scale).astype(jnp.bfloat16).reshape(-1, features)
    g_sin = (cycle_gs * unit_scale).astype(jnp.bfloat16).reshape(-1, features)
    grad_inputs = g_sum1 + cols_dot(g_cos, cos_hid) + cols_dot(g_sin, sin_hid)
    shards = (
        lax.psum_scatter(
            grad_w_in.astype(jnp.bfloat16), "seq", scatter_dimension=0, tiled=True
        ).astype(jnp.float32),
        lax.psum_scatter(
            grad_c_in.astype(jnp.bfloat16), "seq", scatter_dimension=0, tiled=True
        ).astype(jnp.float32),
        lax.psum_scatter(
            grad_w_out.astype(jnp.bfloat16), "seq", scatter_dimension=0, tiled=True
        ).astype(jnp.float32),
        lax.psum_scatter(
            grad_c_out.astype(jnp.bfloat16), "seq", scatter_dimension=0, tiled=True
        ).astype(jnp.float32),
        lax.psum_scatter(
            grad_gain_mix.astype(jnp.bfloat16), "seq", scatter_dimension=0, tiled=True
        ).astype(jnp.float32),
        lax.psum_scatter(
            grad_bias_mix.astype(jnp.bfloat16), "seq", scatter_dimension=0, tiled=True
        ).astype(jnp.float32),
        lax.psum_scatter(
            grad_gain_out.astype(jnp.bfloat16), "seq", scatter_dimension=0, tiled=True
        ).astype(jnp.float32),
        lax.psum_scatter(
            grad_bias_out.astype(jnp.bfloat16), "seq", scatter_dimension=0, tiled=True
        ).astype(jnp.float32),
    )
    summed = (
        lax.psum(shards[0].astype(jnp.bfloat16), "item").astype(jnp.float32),
        lax.psum(shards[1].astype(jnp.bfloat16), "item").astype(jnp.float32),
        lax.psum(shards[2].astype(jnp.bfloat16), "item").astype(jnp.float32),
        lax.psum(shards[3].astype(jnp.bfloat16), "item").astype(jnp.float32),
        lax.psum(shards[4].astype(jnp.bfloat16), "item").astype(jnp.float32),
        lax.psum(shards[5].astype(jnp.bfloat16), "item").astype(jnp.float32),
        lax.psum(shards[6].astype(jnp.bfloat16), "item").astype(jnp.float32),
        lax.psum(shards[7].astype(jnp.bfloat16), "item").astype(jnp.float32),
    )
    return (
        output.reshape(inputs.shape),
        grad_inputs.reshape(inputs.shape),
        summed[0],
        summed[1],
        summed[2],
        summed[3],
        summed[4],
        summed[5],
        summed[6],
        summed[7],
    )


def packed_tables(features, parts):
    half = features // 2
    share = half // parts
    index = np.arange(features)
    forward = np.zeros((features, features), np.float32)
    unpack = np.zeros((features, features), np.float32)
    for low in range(half):
        block, place = divmod(low, share)
        cos_slot = block * 2 * share + place
        sin_slot = cos_slot + share
        angles = (index * low % features).astype(np.float32) * np.float32(2.0 * math.pi / features)
        forward[cos_slot] = np.cos(angles)
        unpack[cos_slot, low] = 1.0
        if low:
            unpack[cos_slot, features - low] = 1.0
            forward[sin_slot] = np.sin(angles)
            unpack[sin_slot, low] = -1.0
            unpack[sin_slot, features - low] = 1.0
        else:
            forward[sin_slot] = 1.0 - 2.0 * (index % 2)
            unpack[sin_slot, half] = 1.0
    return forward.astype(jnp.bfloat16), unpack.astype(jnp.bfloat16)


def seq_tables(period):
    index = np.arange(period)
    angles = (index[:, None] * index[None, :] % period).astype(np.float32)
    angles = angles * np.float32(2.0 * math.pi / period)
    return np.cos(angles).astype(jnp.bfloat16), np.sin(angles).astype(jnp.bfloat16)


MESH = pl.DeviceIdType.MESH
CHUNKS = 3
BF16, F32 = jnp.bfloat16, jnp.float32


def dot(left, right, left_dim, right_dim):
    return lax.dot_general(
        left, right, (((left_dim,), (right_dim,)), ((), ())), preferred_element_type=F32
    )


def row_mean(values):
    return jnp.mean(values, axis=-1, keepdims=True)


def layer_kernel(
    x_hbm, cot_hbm, win_hbm, wout_hbm, cin_ref, cout_ref, gmix_ref, bmix_ref, gout_ref, bout_ref,
    fwd_hbm, unp_hbm, cos_hbm, sin_hbm,
    out_hbm, gin_hbm, gmat_ref, gvec_ref,
    fwd_v, unp_v, cos_v, sin_v, prm_v, xbuf, cotb, win_v, wout_v, stage,
    ysend, yrecv, zsend, zrecv, actb, gpb, hb, gbb, dgb, acc, r1b, ostage, vacc,
    recv1, hop0, hop1, hop2, hop3, vsend, vrecv, vmid, vlast,
    ld_sem, x_sem, cot_sem, stg_sem, a_send, a_recv, b_send, b_recv, out_sem,
    core_send, core_recv, red_send, red_recv, gat_send, gat_recv, v_send, v_recv,
):
    chunks, rows, features = xbuf.shape
    per_chunk, share, period = yrecv.shape[2], yrecv.shape[3], yrecv.shape[4]
    own_len = period // 8
    half = share // 2
    unit_scale = 1.0 / math.sqrt(period * features)

    me, item = lax.axis_index("seq"), lax.axis_index("item")
    peers = [(lax.rem(me + k, 8), item) for k in range(1, 8)]
    z_lo, y_at = lax.rem(lax.div(me, 2), 2), lax.rem(me, 2)
    z_at, z_hi = lax.div(me, 2), lax.div(me, 4)
    core, x_at = lax.rem(item, 2), lax.div(item, 2)
    core_peer = (me, item + 1 - 2 * core)
    x_peer = (me, item + 2 - 4 * x_at)
    far_peer = (me, lax.rem(item + 2, 4) + 1 - 2 * core)
    y_peer = (me + 1 - 2 * y_at, item)
    za_peer = (me + 2 - 4 * z_lo, item)
    zb_peer = (me + 4 - 8 * z_hi, item)

    def remote(src, dst, send, recv, peer):
        return pltpu.make_async_remote_copy(
            src_ref=src, dst_ref=dst, send_sem=send, recv_sem=recv, device_id=peer, device_id_type=MESH
        )

    def wait_bytes(ref, sem):
        pltpu.make_async_copy(ref, ref, sem).wait()

    tables = [
        pltpu.make_async_copy(src, dst, ld_sem.at[i])
        for i, (src, dst) in enumerate(
            [(fwd_hbm, fwd_v), (cos_hbm, cos_v), (sin_hbm, sin_v), (unp_hbm, unp_v)]
        )
    ]
    x_loads = [pltpu.make_async_copy(x_hbm.at[c], xbuf.at[c], x_sem.at[c]) for c in range(chunks)]

    def cot_load(c):
        return pltpu.make_async_copy(cot_hbm.at[c], cotb.at[c], cot_sem.at[c])

    x_loads[0].start()
    tables[0].start()
    for load in x_loads[1:] + tables[1:]:
        load.start()

    barrier = pltpu.get_barrier_semaphore()
    everyone = peers + [core_peer, x_peer, far_peer]
    for peer in everyone:
        pl.semaphore_signal(barrier, inc=1, device_id=peer, device_id_type=MESH)

    slots, piece = stage.shape[0], stage.shape[1]
    per_block = features // piece
    steps = 8 * per_block

    def weight_load(step, part, slot):
        block, at = lax.div(step, per_block), lax.rem(step, per_block) * piece
        if part == 0:
            cols = pl.ds(pl.multiple_of(block * features, features), features)
            src = win_hbm.at[pl.ds(pl.multiple_of(at, piece), piece), cols]
        else:
            src = wout_hbm.at[pl.ds(pl.multiple_of(block * features + at, piece), piece), :]
        return pltpu.make_async_copy(src, stage.at[slot], stg_sem.at[slot])

    def cast_weights(part):
        total = 4 * per_block
        groups = piece // share

        def one(step, carry):
            slot = lax.rem(step, slots)
            weight_load(step, part, slot).wait()
            block, at = lax.div(step, per_block), lax.rem(step, per_block) * groups
            value = stage[slot].astype(BF16)
            for g in range(groups):
                where = at + g
                rows_of = value[g * share : (g + 1) * share]
                if part == 0:
                    win_v[block, lax.div(where, 2), lax.rem(where, 2)] = rows_of
                else:
                    wout_v[block, lax.div(where, 4), lax.rem(lax.div(where, 2), 2), lax.rem(where, 2)] = rows_of

            @pl.when(step + slots < total)
            def _():
                weight_load(step + slots, part, slot).start()

            return carry

        lax.fori_loop(0, total, one, 0)

    def first_loads(part):
        for slot in range(slots):
            weight_load(jnp.int32(slot), part, jnp.int32(slot)).start()

    def in_block(j):
        return win_v[j].reshape(features, features)

    def out_block(j):
        return wout_v[j].reshape(features, features)

    def pack(c, low):
        packed = dot(fwd_v[...], low, 1, 1).astype(BF16)
        for s in range(per_chunk):
            ysend[c, s] = packed[:, s * own_len : (s + 1) * own_len]

    def send_owners(way, c):
        mine = pl.ds(pl.multiple_of(me * own_len, own_len), own_len)
        for peer in peers:
            to = pl.ds(pl.multiple_of(peer[0] * share, share), share)
            remote(
                ysend.at[c, :, to, :], yrecv.at[way, c, :, :, mine], a_send.at[way, c], a_recv.at[way, c], peer
            ).start()
        own = pl.ds(pl.multiple_of(me * share, share), share)
        pltpu.make_async_copy(ysend.at[c, :, own, :], yrecv.at[way, c, :, :, mine], a_recv.at[way, c]).start()

    def owners_sent(way, c):
        wait_bytes(ysend.at[c, :, pl.ds(0, 7 * share), :], a_send.at[way, c])

    def turn(way, c):
        wait_bytes(yrecv.at[way, c], a_recv.at[way, c])
        held = yrecv[way, c]
        cos_rows = held[:, :half].reshape(per_chunk * half, period)
        sin_rows = held[:, half:].reshape(per_chunk * half, period)
        mid_rows = held[:, half : half + 16].reshape(per_chunk * 16, period)
        wide = period // 4
        top = lax.broadcasted_iota(jnp.int32, (16, wide), 0) == 0
        top = jnp.logical_and(top, me == 0)
        cos_rows = jnp.concatenate([cos_rows, mid_rows], axis=0)

        def one(n, carry):
            cols = pl.ds(pl.multiple_of(n * wide, wide), wide)
            by_cos = dot(cos_rows, cos_v[:, cols], 1, 0) * unit_scale
            by_sin = dot(sin_rows, sin_v[:, cols], 1, 0) * unit_scale
            for s in range(per_chunk):
                zsend[c, s, :half, cols] = by_cos[s * half : (s + 1) * half].astype(BF16)
                sin_part = by_sin[s * half : (s + 1) * half]
                at = per_chunk * half + s * 16
                zsend[c, s, half : half + 16, cols] = jnp.where(top, by_cos[at : at + 16], sin_part[:16]).astype(BF16)
                zsend[c, s, half + 16 :, cols] = sin_part[16:].astype(BF16)
            return carry

        lax.fori_loop(0, 4, one, 0)

    def send_back(way, c):
        mine = pl.ds(pl.multiple_of(me * share, share), share)
        for peer in peers:
            to = pl.ds(pl.multiple_of(peer[0] * own_len, own_len), own_len)
            remote(
                zsend.at[c, :, :, to], zrecv.at[c, :, mine, :], b_send.at[way, c], b_recv.at[way, c], peer
            ).start()
        own = pl.ds(pl.multiple_of(me * own_len, own_len), own_len)
        pltpu.make_async_copy(zsend.at[c, :, :, own], zrecv.at[c, :, mine, :], b_recv.at[way, c]).start()

    def return_sent(way, c):
        wait_bytes(zsend.at[c, :, :, pl.ds(0, 7 * own_len)], b_send.at[way, c])

    def mixed_of(c, way=0):
        wait_bytes(zrecv.at[c], b_recv.at[way, c])
        held = jnp.concatenate([zrecv[c, s] for s in range(per_chunk)], axis=1)
        return dot(held, unp_v[...], 0, 0)

    tables[0].wait()
    x_loads[0].wait()
    first_loads(0)
    pack(0, xbuf[0].astype(BF16))
    pl.semaphore_wait(barrier, len(everyone))
    send_owners(0, 0)
    x_loads[1].wait()
    pack(1, xbuf[1].astype(BF16))
    for c in range(chunks):
        cot_load(c).start()
    vacc[...] = jnp.zeros_like(vacc)
    for j in range(4):
        prm_v[j : j + 1] = cin_ref[j * features : (j + 1) * features].reshape(1, features)
    for r, ref in enumerate((cout_ref, gmix_ref, bmix_ref, gout_ref, bout_ref)):
        prm_v[4 + r : 5 + r] = ref[...].reshape(1, features)
    cast_weights(0)
    first_loads(1)
    send_owners(0, 1)
    x_loads[2].wait()
    pack(2, xbuf[2].astype(BF16))
    cast_weights(1)
    for load in tables[1:]:
        load.wait()
    turn(0, 0)
    send_back(0, 0)
    owners_sent(0, 0)
    owners_sent(0, 1)
    send_owners(0, 2)
    turn(0, 1)

    gain_mix, bias_mix = prm_v[5:6], prm_v[6:7]
    gain_out, bias_out, c_out = prm_v[7:8], prm_v[8:9], prm_v[4:5]

    def out_copy(c):
        return pltpu.make_async_copy(ostage, out_hbm.at[c], out_sem.at[0])

    def feed_up(c, mixed=None):
        value = xbuf[c] + (mixed_of(c) if mixed is None else mixed)
        value = value - row_mean(value)
        scale = lax.rsqrt(row_mean(value * value) + 1e-05)
        normal = value * scale
        r1b[...] = jnp.broadcast_to(scale, r1b.shape)
        xbuf[c] = normal
        hidden = normal * gain_mix + bias_mix
        hb[c] = hidden.astype(BF16)
        acc[...] = hidden + c_out

        def up(j, carry):
            pre = dot(hb[c], in_block(j), 1, 0) + prm_v[pl.ds(j, 1)]
            prob = 0.5 + 0.5 * lax.erf(pre * math.sqrt(0.5))
            density = jnp.exp(-0.5 * pre * pre) * (1.0 / math.sqrt(2.0 * math.pi))
            act = (pre * prob).astype(BF16)
            dgb[j] = prob + pre * density
            actb[j, c] = act
            acc[...] += dot(act, out_block(j), 1, 0)
            return carry

        lax.fori_loop(0, 4, up, 0, unroll=True)

    def feed_mid(c):
        value = acc[...]
        value = value - row_mean(value)
        scale = lax.rsqrt(row_mean(value * value) + 1e-05)
        normal = value * scale


        @pl.when(c > 0)
        def _():
            out_copy(c - 1).wait()

        ostage[...] = (normal * gain_out + bias_out).astype(BF16)
        out_copy(c).start()
        cot_load(c).wait()
        cot = cotb[c]
        vacc[7:8] += jnp.sum(cot * normal, axis=0, keepdims=True)
        vacc[8:9] += jnp.sum(cot, axis=0, keepdims=True)
        scaled = cot * gain_out
        g_sum2 = scale * (scaled - row_mean(scaled) - normal * row_mean(scaled * normal))
        low = g_sum2.astype(BF16)
        gbb[c] = low
        vacc[4:5] += jnp.sum(low.astype(F32), axis=0, keepdims=True)
        acc[...] = g_sum2

    def feed_down(c):
        for j in range(4):
            g_pre = (dot(gbb[c], out_block(j), 1, 1) * dgb[j]).astype(BF16)
            gpb[j, c] = g_pre
            vacc[j : j + 1] += jnp.sum(g_pre.astype(F32), axis=0, keepdims=True)

    def feed_end(c):
        for j in range(4):
            acc[...] += dot(gpb[j, c], in_block(j), 1, 1)
        g_hidden = acc[...]
        normal = xbuf[c]
        vacc[5:6] += jnp.sum(g_hidden * normal, axis=0, keepdims=True)
        vacc[6:7] += jnp.sum(g_hidden, axis=0, keepdims=True)
        scaled = g_hidden * gain_mix
        g_sum1 = r1b[:, :1] * (scaled - row_mean(scaled) - normal * row_mean(scaled * normal))
        xbuf[c] = g_sum1
        pack(c, g_sum1.astype(BF16))

    cut = hop3.shape[3]
    routes = ('xyz', 'xyz', 'yxz', 'xzy', 'yxz', 'xzy')
    z_pair = lax.rem(z_at + 2, 4)
    z_next = z_at + 1 - 2 * z_lo
    z_far = lax.rem(z_next + 2, 4)

    def part(p):
        return pl.ds((p % 3) * cut, cut)

    def add(*terms):
        total = terms[0].astype(F32)
        for term in terms[1:]:
            total = total + term.astype(F32)
        return total.astype(BF16)

    def product(p):
        kind, h, at = p // 3, p % 3, part(p)

        def one_in(i, carry):
            x = lax.rem(i, 2)
            q = jnp.where(i < 2, 2 * x + 1 - core, 2 * x + core)
            grad = dot(hb[...].reshape(-1, features), gpb[q, :, :, at].reshape(-1, cut), 0, 0)
            win_v[q, :, :, :, at] = grad.astype(BF16).reshape(4, 2, share, cut)

            @pl.when(i < 2)
            def _():
                remote(
                    win_v.at[2 * x + 1 - core, :, :, :, at], recv1.at[0, h, x],
                    core_send.at[0, h], core_recv.at[0, h], core_peer,
                ).start()

            return carry

        def one_out(j, carry):
            grad = dot(actb[j].reshape(-1, features), gbb[:, :, at].reshape(-1, cut), 0, 0)
            wout_v[j, :, :, :, :, at] = grad.astype(BF16).reshape(2, 2, 2, share, cut)
            return carry

        if kind == 0:
            lax.fori_loop(0, 4, one_in, 0)
        else:
            lax.fori_loop(0, 4, one_out, 0)
            for x in range(2):
                remote(
                    wout_v.at[:, :, x, 1 - core, :, at], recv1.at[1, h, x], core_send.at[1, h], core_recv.at[1, h], core_peer
                ).start()

    def hop(p, step):
        kind, h, at = p // 3, p % 3, part(p)
        legs = routes[p].replace("z", "ab")
        past = legs[:step]
        grads = (win_v, wout_v)[kind]
        landing = (hop0, hop1, hop2, hop3)
        if step == 0:
            wait_bytes(recv1.at[kind, h], core_recv.at[kind, h])
        else:
            wait_bytes(landing[step - 1].at[p], red_recv.at[step - 1, p])

        def place(x, z, y):
            return (2 * x + core, z, y, slice(None), at) if kind == 0 else (z, y, x, core, slice(None), at)

        def arrived(x, z, y, rows_at=slice(None)):
            if step == 0:
                return recv1[kind, h, x, z, y, rows_at]
            count_z = 1 if "b" in past else 2 if "a" in past else 4
            count_y = 1 if "y" in past else 2
            slot = (0 if "x" in past else x * count_z) + zslot(z)
            if isinstance(y, slice):
                return landing[step - 1][p, pl.ds(slot * 2, 2), rows_at]
            return landing[step - 1][p, slot * count_y + (0 if count_y == 1 else y), rows_at]

        def zslot(z):
            if "a" not in past:
                return z
            return 0 if z is z_at else 1

        both_y = slice(None)
        xs = (x_at,) if "x" in past else (0, 1)
        ys = (y_at,) if "y" in past else (both_y,)
        zs = (z_at,) if "b" in past else (z_at, z_pair) if "a" in past else tuple(range(4))

        def put(x, z, y):
            def rows_of(r, carry):
                rows_at = pl.ds(pl.multiple_of(r * 32, 32), 32)
                where = place(x, z, y)
                where = where[:-2] + (rows_at, at)
                grads[where] = add(grads[where], arrived(x, z, y, rows_at))
                return carry

            lax.fori_loop(0, share // 32, rows_of, 0)

        if step == 4:
            where = place(x_at, z_at, y_at)
            finish(p, add(grads[where], arrived(x_at, z_at, y_at)))
            return
        leg = legs[step]
        if leg == "x":
            away, keep, peer = [(1 - x_at, z, y) for z in zs for y in ys], [(x_at, z, y) for z in zs for y in ys], x_peer
        elif leg == "y":
            away, keep, peer = [(x, z, 1 - y_at) for x in xs for z in zs], [(x, z, y_at) for x in xs for z in zs], y_peer
        elif leg == "a":
            away = [(x, z, y) for x in xs for z in (z_next, z_far) for y in ys]
            keep, peer = [(x, z, y) for x in xs for z in (z_at, z_pair) for y in ys], za_peer
        else:
            away, keep, peer = [(x, z_pair, y) for x in xs for y in ys], [(x, z_at, y) for x in xs for y in ys], zb_peer
        for x, z, y in away:
            put(x, z, y)
        for count, (x, z, y) in enumerate(away):
            width = 2 if isinstance(y, slice) else 1
            dst = landing[step].at[p, pl.ds(count * 2, 2)] if width == 2 else landing[step].at[p, count]
            remote(grads.at[place(x, z, y)], dst, red_send.at[step, p], red_recv.at[step, p], peer).start()
        for x, z, y in keep:
            put(x, z, y)

    def finish(p, total):
        kind, at = p // 3, part(p)
        gmat_ref[kind, item, :, at] = total
        here = gmat_ref.at[kind, item, :, at]
        remote(here, here, gat_send.at[1, p], gat_recv.at[1, p], x_peer).start()
        remote(here, here, gat_send.at[0, p], gat_recv.at[0, p], core_peer).start()
        if p in (2, 3):
            remote(here, here, gat_send.at[2, p], gat_recv.at[2, p], far_peer).start()

    def forward_on(p):
        there = gmat_ref.at[p // 3, x_peer[1], :, part(p)]
        wait_bytes(there, gat_recv.at[1, p])
        if p not in (2, 3):
            remote(there, there, gat_send.at[2, p], gat_recv.at[2, p], core_peer).start()

    def final(c):
        hb[c] = (xbuf[c] + mixed_of(c, 1)).astype(BF16)
        pltpu.make_async_copy(hb.at[c], gin_hbm.at[c], out_sem.at[1]).start()

    def vectors_out():
        lanes = vsend.shape[2]
        vsend[...] = jnp.zeros_like(vsend)
        for d in range(8):
            at = d * (features // 2)
            for r in range(3):
                where = at + r * lanes
                vsend[d, r : r + 1, :] = vacc[where // features : where // features + 1, where % features : where % features + lanes]
            for r in range(5):
                vsend[d, 3 + r : 4 + r, :share] = vacc[4 + r : 5 + r, d * share : (d + 1) * share]
        for peer in peers:
            remote(vsend.at[peer[0]], vrecv.at[me], v_send.at[0], v_recv.at[0], peer).start()
        pltpu.make_async_copy(vsend.at[me], vrecv.at[me], v_recv.at[0]).start()

    def vectors_on():
        wait_bytes(vrecv, v_recv.at[0])
        vmid[...] = jnp.sum(vrecv[...], axis=0)
        remote(vmid, vlast.at[0], v_send.at[1], v_recv.at[1], core_peer).start()

    def vectors_over():
        wait_bytes(vlast.at[0], v_recv.at[1])
        vlast[1] = vmid[...] + vlast[0]
        remote(vlast.at[1], vlast.at[2], v_send.at[2], v_recv.at[2], x_peer).start()

    def vectors_end():
        wait_bytes(vlast.at[2], v_recv.at[2])
        gvec_ref[...] = vlast[1] + vlast[2]

    def feed(c, carry):
        feed_up(c)

        @pl.when(c == 0)
        def _():
            send_back(0, 1)
            owners_sent(0, 2)

        @pl.when(c == 1)
        def _():
            send_owners(1, 0)

        feed_mid(c)

        @pl.when(c == 0)
        def _():
            turn(0, 2)
            send_back(0, 2)

        feed_down(c)

        @pl.when(c == chunks - 1)
        def _():
            product(3)
            return_sent(0, 0)
            turn(1, 0)
            send_back(1, 0)
            hop(3, 0)

        feed_end(c)

        @pl.when(c == 1)
        def _():
            send_owners(1, 1)

        return carry

    lax.fori_loop(0, chunks, feed, 0)
    send_owners(1, 2)
    product(4)
    product(5)
    hop(4, 0)
    hop(5, 0)
    return_sent(0, 1)
    turn(1, 1)
    send_back(1, 1)
    product(1)
    product(0)
    hop(3, 1)
    vectors_out()
    product(2)
    hop(0, 0)
    hop(2, 0)
    hop(5, 1)
    hop(1, 0)
    hop(3, 2)
    hop(0, 1)
    hop(5, 2)
    hop(4, 1)
    return_sent(0, 2)
    turn(1, 2)
    send_back(1, 2)
    final(0)
    hop(2, 1)
    hop(0, 2)
    vectors_on()
    hop(1, 1)
    hop(3, 3)
    hop(4, 2)
    hop(0, 3)
    vectors_over()
    hop(5, 3)
    final(1)
    hop(1, 2)
    hop(3, 4)
    hop(2, 2)
    hop(4, 3)
    hop(5, 4)
    hop(1, 3)
    hop(2, 3)
    hop(0, 4)
    hop(1, 4)
    final(2)
    hop(4, 4)
    hop(2, 4)
    forward_on(0)
    vectors_end()
    forward_on(4)
    forward_on(1)
    forward_on(5)
    forward_on(2)
    forward_on(3)

    out_copy(chunks - 1).wait()
    wait_bytes(hb, out_sem.at[1])
    for c in range(chunks):
        owners_sent(1, c)
        return_sent(1, c)
    for kind in range(2):
        for h in range(3):
            wait_bytes(recv1.at[kind, h], core_send.at[kind, h])
    for p in range(6):
        for step, ref in enumerate((hop0, hop1, hop2, hop3)):
            wait_bytes(ref.at[p], red_send.at[step, p])
        for leg in range(3):
            wait_bytes(hop3.at[p], gat_send.at[leg, p])
        wait_bytes(hop3.at[p], gat_recv.at[0, p])
        wait_bytes(hop3.at[p], gat_recv.at[2, p])
    wait_bytes(vrecv.at[pl.ds(0, 7)], v_send.at[0])
    wait_bytes(vlast.at[1], v_send.at[1])
    wait_bytes(vlast.at[1], v_send.at[2])


def finish_kernel(
    out_in, gin_in, gmat_in, gvec_in,
    out_ref, gin_ref, gwi_ref, gwo_ref, gci_ref, gco_ref, ggm_ref, gbm_ref, ggo_ref, gbo_ref,
    low, mv, res, wi, wo, sem_in, sem_out,
):
    chunks, features, share = low.shape[1], low.shape[3], mv.shape[2]
    loads = [pltpu.make_async_copy(gmat_in, mv, sem_in.at[0])]
    for k, src in enumerate((out_in, gin_in)):
        for c in range(chunks):
            loads.append(pltpu.make_async_copy(src.at[c], low.at[k, c], sem_in.at[len(loads)]))
    for load in loads:
        load.start()
    stores = []

    def put(src, dst):
        copy = pltpu.make_async_copy(src, dst, sem_out.at[len(stores)])
        copy.start()
        stores.append(copy)

    loads[0].wait()
    for q in range(4):
        wi[:, q * features : (q + 1) * features] = mv[0, q].astype(F32)
        wo[q * share : (q + 1) * share] = mv[1, q].astype(F32)
    put(wi, gwi_ref)
    put(wo, gwo_ref)
    for k, dst in enumerate((out_ref, gin_ref)):
        for c in range(chunks):
            loads[1 + k * chunks + c].wait()
            res[k, c] = low[k, c].astype(F32)
            put(res.at[k, c], dst.at[c])
    lanes = gvec_in.shape[1]
    for r in range(3):
        gci_ref[r * lanes : (r + 1) * lanes] = gvec_in[r]
    for r, ref in enumerate((gco_ref, ggm_ref, gbm_ref, ggo_ref, gbo_ref)):
        ref[...] = gvec_in[3 + r, :share]
    for copy in stores:
        copy.wait()


def exchange_body(inputs, w_in, c_in, w_out, c_out, gain_mix, bias_mix, gain_out, bias_out, cotangent):
    local_len, per_dev, features = inputs.shape
    parts = lax.axis_size("seq")
    period = local_len * parts
    share = features // parts
    per_chunk = per_dev // CHUNKS
    rows = per_chunk * local_len
    forward, unpack = packed_tables(features, parts)
    cos_seq, sin_seq = seq_tables(period)
    held = jnp.swapaxes(inputs, 0, 1).reshape(CHUNKS, rows, features)
    cot = jnp.swapaxes(cotangent, 0, 1).reshape(CHUNKS, rows, features)
    anywhere = pl.BlockSpec(memory_space=pl.ANY)
    whole = (CHUNKS, rows, features)
    vm, dma = pltpu.VMEM, pltpu.SemaphoreType.DMA
    inside = pl.BlockSpec(memory_space=pltpu.VMEM)
    out_low, gin_low, mats, vecs = pl.pallas_call(
        layer_kernel,
        out_shape=(
            jax.ShapeDtypeStruct(whole, BF16),
            jax.ShapeDtypeStruct(whole, BF16),
            jax.ShapeDtypeStruct((2, 4, share, features), BF16),
            jax.ShapeDtypeStruct((8, 128), F32),
        ),
        in_specs=[anywhere] * 4 + [inside] * 6 + [anywhere] * 4,
        out_specs=(anywhere, anywhere, inside, inside),
        scratch_shapes=[
            vm((features, features), BF16),
            vm((features, features), BF16),
            vm((period, period), BF16),
            vm((period, period), BF16),
            vm((16, features), F32),
            vm(whole, F32),
            vm(whole, F32),
            vm((4, 4, 2, share, features), BF16),
            vm((4, 2, 2, 2, share, features), BF16),
            vm((4, 192, features), F32),
            vm((CHUNKS, per_chunk, features, local_len), BF16),
            vm((2, CHUNKS, per_chunk, share, period), BF16),
            vm((CHUNKS, per_chunk, share, period), BF16),
            vm((CHUNKS, per_chunk, features, local_len), BF16),
            vm((4,) + whole, BF16),
            vm((4,) + whole, BF16),
            vm(whole, BF16),
            vm(whole, BF16),
            vm((4, rows, features), F32),
            vm((rows, features), F32),
            vm((rows, 128), F32),
            vm((rows, features), BF16),
            vm((16, features), F32),
            vm((2, 3, 2, 4, 2, share, features // 3), BF16),
            vm((6, 8, share, features // 3), BF16),
            vm((6, 4, share, features // 3), BF16),
            vm((6, 2, share, features // 3), BF16),
            vm((6, 1, share, features // 3), BF16),
            vm((8, 8, 128), F32),
            vm((8, 8, 128), F32),
            vm((8, 128), F32),
            vm((3, 8, 128), F32),
            dma((4,)),
            dma((CHUNKS,)),
            dma((CHUNKS,)),
            dma((4,)),
            dma((2, CHUNKS)),
            dma((2, CHUNKS)),
            dma((2, CHUNKS)),
            dma((2, CHUNKS)),
            dma((2,)),
            dma((2, 3)),
            dma((2, 3)),
            dma((4, 6)),
            dma((4, 6)),
            dma((3, 6)),
            dma((3, 6)),
            dma((3,)),
            dma((3,)),
        ],
        compiler_params=pltpu.CompilerParams(
            collective_id=0, has_side_effects=True, vmem_limit_bytes=62 * 1024 * 1024
        ),
    )(held, cot, w_in, w_out, c_in, c_out, gain_mix, bias_mix, gain_out, bias_out, forward, unpack, cos_seq, sin_seq)
    shape = (per_dev, local_len, features)
    vec = lambda n: jax.ShapeDtypeStruct((n,), F32)
    output, grad_inputs, grad_in, grad_out, grad_c_in, *others = pl.pallas_call(
        finish_kernel,
        in_specs=[anywhere] * 3 + [inside],
        out_specs=(anywhere,) * 4 + (inside,) * 6,
        out_shape=(
            jax.ShapeDtypeStruct(whole, F32),
            jax.ShapeDtypeStruct(whole, F32),
            jax.ShapeDtypeStruct((share, 4 * features), F32),
            jax.ShapeDtypeStruct((4 * share, features), F32),
            vec(4 * share),
        )
        + (vec(share),) * 5,
        scratch_shapes=[
            vm((2,) + whole, BF16),
            vm((2, 4, share, features), BF16),
            vm((2,) + whole, F32),
            vm((share, 4 * features), F32),
            vm((4 * share, features), F32),
            dma((1 + 2 * CHUNKS,)),
            dma((2 + 2 * CHUNKS,)),
        ],
        compiler_params=pltpu.CompilerParams(vmem_limit_bytes=60 * 1024 * 1024),
    )(out_low, gin_low, mats, vecs)
    output = jnp.swapaxes(output.reshape(shape), 0, 1)
    grad_inputs = jnp.swapaxes(grad_inputs.reshape(shape), 0, 1)
    return (output, grad_inputs, grad_in, grad_c_in, grad_out, *others)


def body(inputs, *rest):
    if lax.axis_size("seq") != 8 or lax.axis_size("item") != 4:
        return gather_body(inputs, *rest)
    return exchange_body(inputs, *rest)


def solution(mesh):
    placed = (
        P("seq", "item", None),
        P(),
        P(),
        P(),
        P(),
        P(),
        P(),
        P(),
        P(),
        P("seq", "item", None),
    )
    return jax.shard_map(
        body,
        mesh=mesh,
        in_specs=placed,
        out_specs=(
            P("seq", "item", None),
            P("seq", "item", None),
            P("seq", None),
            P("seq"),
            P("seq", None),
            P("seq"),
            P("seq"),
            P("seq"),
            P("seq"),
            P("seq"),
        ),
        check_vma=False,
    )
```

```python
import math

import jax
import jax.numpy as jnp
import numpy as np
from jax import lax
from jax.experimental import pallas as pl
from jax.experimental.pallas import tpu as pltpu
from jax.sharding import PartitionSpec as P


def table_block(row_ids, col_ids, period):
    products = row_ids[:, None] * col_ids[None, :] % period
    angles = products.astype(jnp.float32) * (2.0 * math.pi / period)
    return (jnp.cos(angles).astype(jnp.bfloat16), jnp.sin(angles).astype(jnp.bfloat16))


def plain_dot(left, right):
    return jnp.dot(left, right, preferred_element_type=jnp.float32)


def rows_dot(left, right):
    return lax.dot_general(
        left, right, (((0,), (0,)), ((), ())), preferred_element_type=jnp.float32
    )


def cols_dot(left, right):
    return lax.dot_general(
        left, right, (((1,), (1,)), ((), ())), preferred_element_type=jnp.float32
    )


def layer_norm(values, scales, shifts):
    average = jnp.mean(values, axis=-1, keepdims=True)
    centered = values - average
    variance = jnp.mean(centered * centered, axis=-1, keepdims=True)
    return centered * lax.rsqrt(variance + 1e-05) * scales + shifts


def gelu_exact(values):
    return jax.nn.gelu(values, approximate=False)


def gather_body(inputs, w_in, c_in, w_out, c_out, gain_mix, bias_mix, gain_out, bias_out, cotangent):
    local_len, per_dev, features = inputs.shape
    merged = per_dev * features
    period = local_len * lax.axis_size("seq")
    unit_scale = 1.0 / math.sqrt(period * features)
    own_rows = lax.axis_index("seq") * local_len + jnp.arange(local_len, dtype=jnp.int32)
    feat_ids = jnp.arange(features, dtype=jnp.int32)
    cos_hid, sin_hid = table_block(feat_ids, feat_ids, features)
    tokens = inputs.reshape(-1, features)
    tokens_low = tokens.astype(jnp.bfloat16)
    cos_part = (
        plain_dot(tokens_low, cos_hid).astype(jnp.bfloat16).reshape(local_len, per_dev, features)
    )
    sin_part = (
        plain_dot(tokens_low, sin_hid).astype(jnp.bfloat16).reshape(local_len, per_dev, features)
    )
    pieces = (
        lax.all_gather(cos_part, "seq", axis=0, tiled=True),
        lax.all_gather(sin_part, "seq", axis=0, tiled=True),
    )
    col_ids = jnp.arange(pieces[0].shape[0], dtype=jnp.int32)
    cos_blk, sin_blk = table_block(own_rows, col_ids, period)
    mixed = plain_dot(cos_blk, pieces[0].reshape(pieces[0].shape[0], -1)) - plain_dot(
        sin_blk, pieces[1].reshape(pieces[1].shape[0], -1)
    )
    mixed = (mixed * unit_scale).reshape(-1, features)
    hidden, pull_mix = jax.vjp(layer_norm, tokens + mixed, gain_mix, bias_mix)
    hidden_low = hidden.astype(jnp.bfloat16)
    w_in_low = w_in.astype(jnp.bfloat16)
    w_out_low = w_out.astype(jnp.bfloat16)
    pre = plain_dot(hidden_low, w_in_low) + c_in
    act, pull_gelu = jax.vjp(gelu_exact, pre)
    act_low = act.astype(jnp.bfloat16)
    branch = plain_dot(act_low, w_out_low) + c_out
    output, pull_out = jax.vjp(layer_norm, hidden + branch, gain_out, bias_out)
    g_sum2, grad_gain_out, grad_bias_out = pull_out(cotangent.reshape(-1, features))
    g_branch = g_sum2.astype(jnp.bfloat16)
    grad_c_out = jnp.sum(g_branch.astype(jnp.float32), axis=0)
    grad_w_out = rows_dot(act_low, g_branch)
    (g_act,) = pull_gelu(cols_dot(g_branch, w_out_low))
    g_pre = g_act.astype(jnp.bfloat16)
    grad_c_in = jnp.sum(g_pre.astype(jnp.float32), axis=0)
    grad_w_in = rows_dot(hidden_low, g_pre)
    g_hidden = g_sum2 + cols_dot(g_pre, w_in_low)
    g_sum1, grad_gain_mix, grad_bias_mix = pull_mix(g_hidden)
    g_mixed = g_sum1.astype(jnp.bfloat16).reshape(local_len, per_dev, features)
    empty = jnp.zeros((local_len, merged), jnp.float32)
    piece = lax.all_gather(g_mixed, "seq", axis=0, tiled=True)
    row_ids = jnp.arange(piece.shape[0], dtype=jnp.int32)
    cos_blk, sin_blk = table_block(row_ids, own_rows, period)
    flat = piece.reshape(piece.shape[0], -1)
    cycle_gc = rows_dot(cos_blk, flat)
    cycle_gs = (empty, empty)[1] - rows_dot(sin_blk, flat)
    g_cos = (cycle_gc * unit_scale).astype(jnp.bfloat16).reshape(-1, features)
    g_sin = (cycle_gs * unit_scale).astype(jnp.bfloat16).reshape(-1, features)
    grad_inputs = g_sum1 + cols_dot(g_cos, cos_hid) + cols_dot(g_sin, sin_hid)
    shards = (
        lax.psum_scatter(
            grad_w_in.astype(jnp.bfloat16), "seq", scatter_dimension=0, tiled=True
        ).astype(jnp.float32),
        lax.psum_scatter(
            grad_c_in.astype(jnp.bfloat16), "seq", scatter_dimension=0, tiled=True
        ).astype(jnp.float32),
        lax.psum_scatter(
            grad_w_out.astype(jnp.bfloat16), "seq", scatter_dimension=0, tiled=True
        ).astype(jnp.float32),
        lax.psum_scatter(
            grad_c_out.astype(jnp.bfloat16), "seq", scatter_dimension=0, tiled=True
        ).astype(jnp.float32),
        lax.psum_scatter(
            grad_gain_mix.astype(jnp.bfloat16), "seq", scatter_dimension=0, tiled=True
        ).astype(jnp.float32),
        lax.psum_scatter(
            grad_bias_mix.astype(jnp.bfloat16), "seq", scatter_dimension=0, tiled=True
        ).astype(jnp.float32),
        lax.psum_scatter(
            grad_gain_out.astype(jnp.bfloat16), "seq", scatter_dimension=0, tiled=True
        ).astype(jnp.float32),
        lax.psum_scatter(
            grad_bias_out.astype(jnp.bfloat16), "seq", scatter_dimension=0, tiled=True
        ).astype(jnp.float32),
    )
    summed = (
        lax.psum(shards[0].astype(jnp.bfloat16), "item").astype(jnp.float32),
        lax.psum(shards[1].astype(jnp.bfloat16), "item").astype(jnp.float32),
        lax.psum(shards[2].astype(jnp.bfloat16), "item").astype(jnp.float32),
        lax.psum(shards[3].astype(jnp.bfloat16), "item").astype(jnp.float32),
        lax.psum(shards[4].astype(jnp.bfloat16), "item").astype(jnp.float32),
        lax.psum(shards[5].astype(jnp.bfloat16), "item").astype(jnp.float32),
        lax.psum(shards[6].astype(jnp.bfloat16), "item").astype(jnp.float32),
        lax.psum(shards[7].astype(jnp.bfloat16), "item").astype(jnp.float32),
    )
    return (
        output.reshape(inputs.shape),
        grad_inputs.reshape(inputs.shape),
        summed[0],
        summed[1],
        summed[2],
        summed[3],
        summed[4],
        summed[5],
        summed[6],
        summed[7],
    )


def packed_tables(features, parts):
    half = features // 2
    share = half // parts
    index = np.arange(features)
    forward = np.zeros((features, features), np.float32)
    unpack = np.zeros((features, features), np.float32)
    for low in range(half):
        block, place = divmod(low, share)
        cos_slot = block * 2 * share + place
        sin_slot = cos_slot + share
        angles = (index * low % features).astype(np.float32) * np.float32(2.0 * math.pi / features)
        forward[cos_slot] = np.cos(angles)
        unpack[cos_slot, low] = 1.0
        if low:
            unpack[cos_slot, features - low] = 1.0
            forward[sin_slot] = np.sin(angles)
            unpack[sin_slot, low] = -1.0
            unpack[sin_slot, features - low] = 1.0
        else:
            forward[sin_slot] = 1.0 - 2.0 * (index % 2)
            unpack[sin_slot, half] = 1.0
    return forward.astype(jnp.bfloat16), unpack.astype(jnp.bfloat16)


def seq_tables(period):
    index = np.arange(period)
    angles = (index[:, None] * index[None, :] % period).astype(np.float32)
    angles = angles * np.float32(2.0 * math.pi / period)
    return np.cos(angles).astype(jnp.bfloat16), np.sin(angles).astype(jnp.bfloat16)


MESH = pl.DeviceIdType.MESH
CHUNKS = 3
BF16, F32 = jnp.bfloat16, jnp.float32


def dot(left, right, left_dim, right_dim):
    return lax.dot_general(
        left, right, (((left_dim,), (right_dim,)), ((), ())), preferred_element_type=F32
    )


def row_mean(values):
    return jnp.mean(values, axis=-1, keepdims=True)


def layer_kernel(
    x_hbm, cot_hbm, win_hbm, wout_hbm, cin_hbm, cout_hbm, gmix_hbm, bmix_hbm, gout_hbm, bout_hbm,
    fwd_hbm, unp_hbm, cos_hbm, sin_hbm,
    out_hbm, gin_hbm, gmat_ref, gvec_ref,
    cin_ref, cout_ref, gmix_ref, bmix_ref, gout_ref, bout_ref,
    fwd_v, unp_v, cos_v, sin_v, prm_v, xbuf, cotb, win_v, wout_v, stage,
    ysend, yrecv, zsend, zrecv, actb, gpb, hb, gbb, dgb, acc, r1b, ostage, vacc,
    recv1, hop0, hop1, hop2, hop3, vsend, vrecv, vmid, vlast,
    ld_sem, x_sem, cot_sem, stg_sem, a_send, a_recv, b_send, b_recv, out_sem,
    core_send, core_recv, red_send, red_recv, gat_send, gat_recv, v_send, v_recv,
):
    chunks, rows, features = xbuf.shape
    per_chunk, share, period = yrecv.shape[2], yrecv.shape[3], yrecv.shape[4]
    own_len = period // 8
    half = share // 2
    unit_scale = 1.0 / math.sqrt(period * features)

    me, item = lax.axis_index("seq"), lax.axis_index("item")
    peers = [(lax.rem(me + k, 8), item) for k in range(1, 8)]
    z_lo, y_at = lax.rem(lax.div(me, 2), 2), lax.rem(me, 2)
    z_at, z_hi = lax.div(me, 2), lax.div(me, 4)
    core, x_at = lax.rem(item, 2), lax.div(item, 2)
    core_peer = (me, item + 1 - 2 * core)
    x_peer = (me, item + 2 - 4 * x_at)
    far_peer = (me, lax.rem(item + 2, 4) + 1 - 2 * core)
    y_peer = (me + 1 - 2 * y_at, item)
    za_peer = (me + 2 - 4 * z_lo, item)
    zb_peer = (me + 4 - 8 * z_hi, item)

    def remote(src, dst, send, recv, peer):
        return pltpu.make_async_remote_copy(
            src_ref=src, dst_ref=dst, send_sem=send, recv_sem=recv, device_id=peer, device_id_type=MESH
        )

    def wait_bytes(ref, sem):
        pltpu.make_async_copy(ref, ref, sem).wait()

    tables = [
        pltpu.make_async_copy(src, dst, ld_sem.at[i])
        for i, (src, dst) in enumerate(
            [
                (fwd_hbm, fwd_v), (cos_hbm, cos_v), (sin_hbm, sin_v), (unp_hbm, unp_v),
                (cin_hbm, cin_ref), (cout_hbm, cout_ref), (gmix_hbm, gmix_ref),
                (bmix_hbm, bmix_ref), (gout_hbm, gout_ref), (bout_hbm, bout_ref),
            ]
        )
    ]
    x_loads = [pltpu.make_async_copy(x_hbm.at[c], xbuf.at[c], x_sem.at[c]) for c in range(chunks)]

    def cot_load(c):
        return pltpu.make_async_copy(cot_hbm.at[c], cotb.at[c], cot_sem.at[c])

    x_loads[0].start()
    tables[0].start()
    for load in x_loads[1:] + tables[1:]:
        load.start()

    barrier = pltpu.get_barrier_semaphore()
    everyone = peers + [core_peer, x_peer, far_peer]
    for peer in everyone:
        pl.semaphore_signal(barrier, inc=1, device_id=peer, device_id_type=MESH)

    slots, piece = stage.shape[0], stage.shape[1]
    per_block = features // piece
    steps = 8 * per_block

    def weight_load(step, part, slot):
        block, at = lax.div(step, per_block), lax.rem(step, per_block) * piece
        if part == 0:
            cols = pl.ds(pl.multiple_of(block * features, features), features)
            src = win_hbm.at[pl.ds(pl.multiple_of(at, piece), piece), cols]
        else:
            src = wout_hbm.at[pl.ds(pl.multiple_of(block * features + at, piece), piece), :]
        return pltpu.make_async_copy(src, stage.at[slot], stg_sem.at[slot])

    def cast_weights(part):
        total = 4 * per_block
        groups = piece // share

        def one(step, carry):
            slot = lax.rem(step, slots)
            weight_load(step, part, slot).wait()
            block, at = lax.div(step, per_block), lax.rem(step, per_block) * groups
            value = stage[slot].astype(BF16)
            for g in range(groups):
                where = at + g
                rows_of = value[g * share : (g + 1) * share]
                if part == 0:
                    win_v[block, lax.div(where, 2), lax.rem(where, 2)] = rows_of
                else:
                    wout_v[block, lax.div(where, 4), lax.rem(lax.div(where, 2), 2), lax.rem(where, 2)] = rows_of

            @pl.when(step + slots < total)
            def _():
                weight_load(step + slots, part, slot).start()

            return carry

        lax.fori_loop(0, total, one, 0)

    def first_loads(part):
        for slot in range(slots):
            weight_load(jnp.int32(slot), part, jnp.int32(slot)).start()

    def in_block(j):
        return win_v[j].reshape(features, features)

    def out_block(j):
        return wout_v[j].reshape(features, features)

    def pack(c, low):
        packed = dot(fwd_v[...], low, 1, 1).astype(BF16)
        for s in range(per_chunk):
            ysend[c, s] = packed[:, s * own_len : (s + 1) * own_len]

    def send_owners(way, c):
        mine = pl.ds(pl.multiple_of(me * own_len, own_len), own_len)
        for peer in peers:
            to = pl.ds(pl.multiple_of(peer[0] * share, share), share)
            remote(
                ysend.at[c, :, to, :], yrecv.at[way, c, :, :, mine], a_send.at[way, c], a_recv.at[way, c], peer
            ).start()
        own = pl.ds(pl.multiple_of(me * share, share), share)
        pltpu.make_async_copy(ysend.at[c, :, own, :], yrecv.at[way, c, :, :, mine], a_recv.at[way, c]).start()

    def owners_sent(way, c):
        wait_bytes(ysend.at[c, :, pl.ds(0, 7 * share), :], a_send.at[way, c])

    def turn(way, c):
        wait_bytes(yrecv.at[way, c], a_recv.at[way, c])
        held = yrecv[way, c]
        cos_rows = held[:, :half].reshape(per_chunk * half, period)
        sin_rows = held[:, half:].reshape(per_chunk * half, period)
        mid_rows = held[:, half : half + 16].reshape(per_chunk * 16, period)
        wide = period // 4
        top = lax.broadcasted_iota(jnp.int32, (16, wide), 0) == 0
        top = jnp.logical_and(top, me == 0)
        cos_rows = jnp.concatenate([cos_rows, mid_rows], axis=0)

        def one(n, carry):
            cols = pl.ds(pl.multiple_of(n * wide, wide), wide)
            by_cos = dot(cos_rows, cos_v[:, cols], 1, 0) * unit_scale
            by_sin = dot(sin_rows, sin_v[:, cols], 1, 0) * unit_scale
            for s in range(per_chunk):
                zsend[c, s, :half, cols] = by_cos[s * half : (s + 1) * half].astype(BF16)
                sin_part = by_sin[s * half : (s + 1) * half]
                at = per_chunk * half + s * 16
                zsend[c, s, half : half + 16, cols] = jnp.where(top, by_cos[at : at + 16], sin_part[:16]).astype(BF16)
                zsend[c, s, half + 16 :, cols] = sin_part[16:].astype(BF16)
            return carry

        lax.fori_loop(0, 4, one, 0)

    def send_back(way, c):
        mine = pl.ds(pl.multiple_of(me * share, share), share)
        for peer in peers:
            to = pl.ds(pl.multiple_of(peer[0] * own_len, own_len), own_len)
            remote(
                zsend.at[c, :, :, to], zrecv.at[c, :, mine, :], b_send.at[way, c], b_recv.at[way, c], peer
            ).start()
        own = pl.ds(pl.multiple_of(me * own_len, own_len), own_len)
        pltpu.make_async_copy(zsend.at[c, :, :, own], zrecv.at[c, :, mine, :], b_recv.at[way, c]).start()

    def return_sent(way, c):
        wait_bytes(zsend.at[c, :, :, pl.ds(0, 7 * own_len)], b_send.at[way, c])

    def mixed_of(c, way=0):
        wait_bytes(zrecv.at[c], b_recv.at[way, c])
        held = jnp.concatenate([zrecv[c, s] for s in range(per_chunk)], axis=1)
        return dot(held, unp_v[...], 0, 0)

    tables[0].wait()
    x_loads[0].wait()
    first_loads(0)
    pack(0, xbuf[0].astype(BF16))
    pl.semaphore_wait(barrier, len(everyone))
    send_owners(0, 0)
    x_loads[1].wait()
    pack(1, xbuf[1].astype(BF16))
    for c in range(chunks):
        cot_load(c).start()
    vacc[...] = jnp.zeros_like(vacc)
    for load in tables[4:]:
        load.wait()
    for j in range(4):
        prm_v[j : j + 1] = cin_ref[j * features : (j + 1) * features].reshape(1, features)
    for r, ref in enumerate((cout_ref, gmix_ref, bmix_ref, gout_ref, bout_ref)):
        prm_v[4 + r : 5 + r] = ref[...].reshape(1, features)
    cast_weights(0)
    first_loads(1)
    send_owners(0, 1)
    x_loads[2].wait()
    pack(2, xbuf[2].astype(BF16))
    cast_weights(1)
    for load in tables[1:4]:
        load.wait()
    turn(0, 0)
    send_back(0, 0)
    owners_sent(0, 0)
    owners_sent(0, 1)
    send_owners(0, 2)
    turn(0, 1)

    gain_mix, bias_mix = prm_v[5:6], prm_v[6:7]
    gain_out, bias_out, c_out = prm_v[7:8], prm_v[8:9], prm_v[4:5]

    def out_copy(c):
        return pltpu.make_async_copy(ostage, out_hbm.at[c], out_sem.at[0])

    def feed_up(c, mixed=None):
        value = xbuf[c] + (mixed_of(c) if mixed is None else mixed)
        value = value - row_mean(value)
        scale = lax.rsqrt(row_mean(value * value) + 1e-05)
        normal = value * scale
        r1b[...] = jnp.broadcast_to(scale, r1b.shape)
        xbuf[c] = normal
        hidden = normal * gain_mix + bias_mix
        hb[c] = hidden.astype(BF16)
        acc[...] = hidden + c_out

        def up(j, carry):
            pre = dot(hb[c], in_block(j), 1, 0) + prm_v[pl.ds(j, 1)]
            prob = 0.5 + 0.5 * lax.erf(pre * math.sqrt(0.5))
            density = jnp.exp(-0.5 * pre * pre) * (1.0 / math.sqrt(2.0 * math.pi))
            act = (pre * prob).astype(BF16)
            dgb[j] = prob + pre * density
            actb[j, c] = act
            acc[...] += dot(act, out_block(j), 1, 0)
            return carry

        lax.fori_loop(0, 4, up, 0, unroll=True)

    def feed_mid(c):
        value = acc[...]
        value = value - row_mean(value)
        scale = lax.rsqrt(row_mean(value * value) + 1e-05)
        normal = value * scale


        @pl.when(c > 0)
        def _():
            out_copy(c - 1).wait()

        ostage[...] = (normal * gain_out + bias_out).astype(BF16)
        out_copy(c).start()
        cot_load(c).wait()
        cot = cotb[c]
        vacc[7:8] += jnp.sum(cot * normal, axis=0, keepdims=True)
        vacc[8:9] += jnp.sum(cot, axis=0, keepdims=True)
        scaled = cot * gain_out
        g_sum2 = scale * (scaled - row_mean(scaled) - normal * row_mean(scaled * normal))
        low = g_sum2.astype(BF16)
        gbb[c] = low
        vacc[4:5] += jnp.sum(low.astype(F32), axis=0, keepdims=True)
        acc[...] = g_sum2

    def feed_down(c):
        for j in range(4):
            g_pre = (dot(gbb[c], out_block(j), 1, 1) * dgb[j]).astype(BF16)
            gpb[j, c] = g_pre
            vacc[j : j + 1] += jnp.sum(g_pre.astype(F32), axis=0, keepdims=True)

    def feed_end(c):
        for j in range(4):
            acc[...] += dot(gpb[j, c], in_block(j), 1, 1)
        g_hidden = acc[...]
        normal = xbuf[c]
        vacc[5:6] += jnp.sum(g_hidden * normal, axis=0, keepdims=True)
        vacc[6:7] += jnp.sum(g_hidden, axis=0, keepdims=True)
        scaled = g_hidden * gain_mix
        g_sum1 = r1b[:, :1] * (scaled - row_mean(scaled) - normal * row_mean(scaled * normal))
        xbuf[c] = g_sum1
        pack(c, g_sum1.astype(BF16))

    cut = hop3.shape[3]
    routes = ('xyz', 'xzy', 'xyz', 'xzy', 'yxz', 'yxz')
    z_pair = lax.rem(z_at + 2, 4)
    z_next = z_at + 1 - 2 * z_lo
    z_far = lax.rem(z_next + 2, 4)

    def part(p):
        return pl.ds((p % 3) * cut, cut)

    def add(*terms):
        total = terms[0].astype(F32)
        for term in terms[1:]:
            total = total + term.astype(F32)
        return total.astype(BF16)

    def product(p):
        kind, h, at = p // 3, p % 3, part(p)

        def one_in(i, carry):
            x = lax.rem(i, 2)
            q = jnp.where(i < 2, 2 * x + 1 - core, 2 * x + core)
            grad = dot(hb[...].reshape(-1, features), gpb[q, :, :, at].reshape(-1, cut), 0, 0)
            win_v[q, :, :, :, at] = grad.astype(BF16).reshape(4, 2, share, cut)

            @pl.when(i < 2)
            def _():
                remote(
                    win_v.at[2 * x + 1 - core, :, :, :, at], recv1.at[0, h, x],
                    core_send.at[0, h], core_recv.at[0, h], core_peer,
                ).start()

            return carry

        def one_out(j, carry):
            grad = dot(actb[j].reshape(-1, features), gbb[:, :, at].reshape(-1, cut), 0, 0)
            wout_v[j, :, :, :, :, at] = grad.astype(BF16).reshape(2, 2, 2, share, cut)
            return carry

        if kind == 0:
            lax.fori_loop(0, 4, one_in, 0)
        else:
            lax.fori_loop(0, 4, one_out, 0)
            for x in range(2):
                remote(
                    wout_v.at[:, :, x, 1 - core, :, at], recv1.at[1, h, x], core_send.at[1, h], core_recv.at[1, h], core_peer
                ).start()

    def hop(p, step):
        kind, h, at = p // 3, p % 3, part(p)
        legs = routes[p].replace("z", "ab")
        past = legs[:step]
        grads = (win_v, wout_v)[kind]
        landing = (hop0, hop1, hop2, hop3)
        if step == 0:
            wait_bytes(recv1.at[kind, h], core_recv.at[kind, h])
        else:
            wait_bytes(landing[step - 1].at[p], red_recv.at[step - 1, p])

        def place(x, z, y):
            return (2 * x + core, z, y, slice(None), at) if kind == 0 else (z, y, x, core, slice(None), at)

        def arrived(x, z, y, rows_at=slice(None)):
            if step == 0:
                return recv1[kind, h, x, z, y, rows_at]
            count_z = 1 if "b" in past else 2 if "a" in past else 4
            count_y = 1 if "y" in past else 2
            slot = (0 if "x" in past else x * count_z) + zslot(z)
            if isinstance(y, slice):
                return landing[step - 1][p, pl.ds(slot * 2, 2), rows_at]
            return landing[step - 1][p, slot * count_y + (0 if count_y == 1 else y), rows_at]

        def zslot(z):
            if "a" not in past:
                return z
            return 0 if z is z_at else 1

        both_y = slice(None)
        xs = (x_at,) if "x" in past else (0, 1)
        ys = (y_at,) if "y" in past else (both_y,)
        zs = (z_at,) if "b" in past else (z_at, z_pair) if "a" in past else tuple(range(4))

        def put(x, z, y):
            def rows_of(r, carry):
                rows_at = pl.ds(pl.multiple_of(r * 32, 32), 32)
                where = place(x, z, y)
                where = where[:-2] + (rows_at, at)
                grads[where] = add(grads[where], arrived(x, z, y, rows_at))
                return carry

            lax.fori_loop(0, share // 32, rows_of, 0)

        if step == 4:
            where = place(x_at, z_at, y_at)
            finish(p, add(grads[where], arrived(x_at, z_at, y_at)))
            return
        leg = legs[step]
        if leg == "x":
            away, keep, peer = [(1 - x_at, z, y) for z in zs for y in ys], [(x_at, z, y) for z in zs for y in ys], x_peer
        elif leg == "y":
            away, keep, peer = [(x, z, 1 - y_at) for x in xs for z in zs], [(x, z, y_at) for x in xs for z in zs], y_peer
        elif leg == "a":
            away = [(x, z, y) for x in xs for z in (z_next, z_far) for y in ys]
            keep, peer = [(x, z, y) for x in xs for z in (z_at, z_pair) for y in ys], za_peer
        else:
            away, keep, peer = [(x, z_pair, y) for x in xs for y in ys], [(x, z_at, y) for x in xs for y in ys], zb_peer
        for x, z, y in away:
            put(x, z, y)
        for count, (x, z, y) in enumerate(away):
            width = 2 if isinstance(y, slice) else 1
            dst = landing[step].at[p, pl.ds(count * 2, 2)] if width == 2 else landing[step].at[p, count]
            remote(grads.at[place(x, z, y)], dst, red_send.at[step, p], red_recv.at[step, p], peer).start()
        for x, z, y in keep:
            put(x, z, y)

    def finish(p, total):
        kind, at = p // 3, part(p)
        gmat_ref[kind, item, :, at] = total
        here = gmat_ref.at[kind, item, :, at]
        remote(here, here, gat_send.at[1, p], gat_recv.at[1, p], x_peer).start()
        remote(here, here, gat_send.at[0, p], gat_recv.at[0, p], core_peer).start()
        if p in (1, 4, 5):
            remote(here, here, gat_send.at[2, p], gat_recv.at[2, p], far_peer).start()

    def forward_on(p):
        there = gmat_ref.at[p // 3, x_peer[1], :, part(p)]
        wait_bytes(there, gat_recv.at[1, p])
        if p not in (1, 4, 5):
            remote(there, there, gat_send.at[2, p], gat_recv.at[2, p], core_peer).start()

    def final(c):
        hb[c] = (xbuf[c] + mixed_of(c, 1)).astype(BF16)
        pltpu.make_async_copy(hb.at[c], gin_hbm.at[c], out_sem.at[1]).start()

    def vectors_out():
        lanes = vsend.shape[2]
        vsend[...] = jnp.zeros_like(vsend)
        for d in range(8):
            at = d * (features // 2)
            for r in range(3):
                where = at + r * lanes
                vsend[d, r : r + 1, :] = vacc[where // features : where // features + 1, where % features : where % features + lanes]
            for r in range(5):
                vsend[d, 3 + r : 4 + r, :share] = vacc[4 + r : 5 + r, d * share : (d + 1) * share]
        for peer in peers:
            remote(vsend.at[peer[0]], vrecv.at[me], v_send.at[0], v_recv.at[0], peer).start()
        pltpu.make_async_copy(vsend.at[me], vrecv.at[me], v_recv.at[0]).start()

    def vectors_on():
        wait_bytes(vrecv, v_recv.at[0])
        vmid[...] = jnp.sum(vrecv[...], axis=0)
        remote(vmid, vlast.at[0], v_send.at[1], v_recv.at[1], core_peer).start()

    def vectors_over():
        wait_bytes(vlast.at[0], v_recv.at[1])
        vlast[1] = vmid[...] + vlast[0]
        remote(vlast.at[1], vlast.at[2], v_send.at[2], v_recv.at[2], x_peer).start()

    def vectors_end():
        wait_bytes(vlast.at[2], v_recv.at[2])
        gvec_ref[...] = vlast[1] + vlast[2]

    def feed(c, carry):
        feed_up(c)

        @pl.when(c == 0)
        def _():
            send_back(0, 1)
            owners_sent(0, 2)

        @pl.when(c == 1)
        def _():
            send_owners(1, 0)

        feed_mid(c)

        @pl.when(c == 0)
        def _():
            turn(0, 2)
            send_back(0, 2)

        feed_down(c)

        @pl.when(c == chunks - 1)
        def _():
            product(3)
            return_sent(0, 0)
            turn(1, 0)
            send_back(1, 0)
            product(4)
            hop(3, 0)

        feed_end(c)

        @pl.when(c == 1)
        def _():
            send_owners(1, 1)

        return carry

    lax.fori_loop(0, chunks, feed, 0)
    vectors_out()
    hop(4, 0)
    send_owners(1, 2)
    product(0)
    product(1)
    hop(0, 0)
    hop(1, 0)
    hop(3, 1)
    return_sent(0, 1)
    turn(1, 1)
    send_back(1, 1)
    product(2)
    product(5)
    hop(3, 2)
    hop(0, 1)
    vectors_on()
    vectors_over()
    hop(5, 0)
    return_sent(0, 2)
    turn(1, 2)
    send_back(1, 2)
    final(0)
    hop(2, 0)
    hop(4, 1)
    hop(1, 1)
    hop(0, 2)
    hop(5, 1)
    hop(2, 1)
    hop(3, 3)
    hop(1, 2)
    hop(4, 2)
    hop(0, 3)
    hop(2, 2)
    hop(3, 4)
    hop(5, 2)
    hop(4, 3)
    final(1)
    hop(1, 3)
    hop(2, 3)
    forward_on(3)
    hop(0, 4)
    hop(5, 3)
    hop(1, 4)
    hop(4, 4)
    hop(2, 4)
    hop(5, 4)
    vectors_end()
    final(2)
    forward_on(2)
    forward_on(0)
    forward_on(1)
    forward_on(4)
    forward_on(5)

    out_copy(chunks - 1).wait()
    wait_bytes(hb, out_sem.at[1])
    for c in range(chunks):
        owners_sent(1, c)
        return_sent(1, c)
    for kind in range(2):
        for h in range(3):
            wait_bytes(recv1.at[kind, h], core_send.at[kind, h])
    for p in range(6):
        for step, ref in enumerate((hop0, hop1, hop2, hop3)):
            wait_bytes(ref.at[p], red_send.at[step, p])
        for leg in range(3):
            wait_bytes(hop3.at[p], gat_send.at[leg, p])
        wait_bytes(hop3.at[p], gat_recv.at[0, p])
        wait_bytes(hop3.at[p], gat_recv.at[2, p])
    wait_bytes(vrecv.at[pl.ds(0, 7)], v_send.at[0])
    wait_bytes(vlast.at[1], v_send.at[1])
    wait_bytes(vlast.at[1], v_send.at[2])


def finish_kernel(
    out_in, gin_in, gmat_in, gvec_in,
    out_ref, gin_ref, gwi_ref, gwo_ref, gci_ref, gco_ref, ggm_ref, gbm_ref, ggo_ref, gbo_ref,
    low, mv, res, wi, wo, sem_in, sem_out,
):
    chunks, features, share = low.shape[1], low.shape[3], mv.shape[2]
    loads = [pltpu.make_async_copy(gmat_in, mv, sem_in.at[0])]
    for k, src in enumerate((out_in, gin_in)):
        for c in range(chunks):
            loads.append(pltpu.make_async_copy(src.at[c], low.at[k, c], sem_in.at[len(loads)]))
    for load in loads[1:] + loads[:1]:
        load.start()
    stores = []

    def put(src, dst):
        copy = pltpu.make_async_copy(src, dst, sem_out.at[len(stores)])
        copy.start()
        stores.append(copy)

    for k, dst in enumerate((out_ref, gin_ref)):
        for c in range(chunks):
            loads[1 + k * chunks + c].wait()
            res[k, c] = low[k, c].astype(F32)
            put(res.at[k, c], dst.at[c])
    loads[0].wait()
    for q in range(4):
        wi[:, q * features : (q + 1) * features] = mv[0, q].astype(F32)
        wo[q * share : (q + 1) * share] = mv[1, q].astype(F32)
    put(wi, gwi_ref)
    put(wo, gwo_ref)
    lanes = gvec_in.shape[1]
    for r in range(3):
        gci_ref[r * lanes : (r + 1) * lanes] = gvec_in[r]
    for r, ref in enumerate((gco_ref, ggm_ref, gbm_ref, ggo_ref, gbo_ref)):
        ref[...] = gvec_in[3 + r, :share]
    for copy in stores:
        copy.wait()


def exchange_body(inputs, w_in, c_in, w_out, c_out, gain_mix, bias_mix, gain_out, bias_out, cotangent):
    local_len, per_dev, features = inputs.shape
    parts = lax.axis_size("seq")
    period = local_len * parts
    share = features // parts
    per_chunk = per_dev // CHUNKS
    rows = per_chunk * local_len
    forward, unpack = packed_tables(features, parts)
    cos_seq, sin_seq = seq_tables(period)
    held = jnp.swapaxes(inputs, 0, 1).reshape(CHUNKS, rows, features)
    cot = jnp.swapaxes(cotangent, 0, 1).reshape(CHUNKS, rows, features)
    anywhere = pl.BlockSpec(memory_space=pl.ANY)
    whole = (CHUNKS, rows, features)
    vm, dma = pltpu.VMEM, pltpu.SemaphoreType.DMA
    inside = pl.BlockSpec(memory_space=pltpu.VMEM)
    out_low, gin_low, mats, vecs = pl.pallas_call(
        layer_kernel,
        out_shape=(
            jax.ShapeDtypeStruct(whole, BF16),
            jax.ShapeDtypeStruct(whole, BF16),
            jax.ShapeDtypeStruct((2, 4, share, features), BF16),
            jax.ShapeDtypeStruct((8, 128), F32),
        ),
        in_specs=[anywhere] * 14,
        out_specs=(anywhere, anywhere, inside, inside),
        scratch_shapes=[
            vm((4 * features,), F32),
            vm((features,), F32),
            vm((features,), F32),
            vm((features,), F32),
            vm((features,), F32),
            vm((features,), F32),
            vm((features, features), BF16),
            vm((features, features), BF16),
            vm((period, period), BF16),
            vm((period, period), BF16),
            vm((16, features), F32),
            vm(whole, F32),
            vm(whole, F32),
            vm((4, 4, 2, share, features), BF16),
            vm((4, 2, 2, 2, share, features), BF16),
            vm((4, 192, features), F32),
            vm((CHUNKS, per_chunk, features, local_len), BF16),
            vm((2, CHUNKS, per_chunk, share, period), BF16),
            vm((CHUNKS, per_chunk, share, period), BF16),
            vm((CHUNKS, per_chunk, features, local_len), BF16),
            vm((4,) + whole, BF16),
            vm((4,) + whole, BF16),
            vm(whole, BF16),
            vm(whole, BF16),
            vm((4, rows, features), F32),
            vm((rows, features), F32),
            vm((rows, 128), F32),
            vm((rows, features), BF16),
            vm((16, features), F32),
            vm((2, 3, 2, 4, 2, share, features // 3), BF16),
            vm((6, 8, share, features // 3), BF16),
            vm((6, 4, share, features // 3), BF16),
            vm((6, 2, share, features // 3), BF16),
            vm((6, 1, share, features // 3), BF16),
            vm((8, 8, 128), F32),
            vm((8, 8, 128), F32),
            vm((8, 128), F32),
            vm((3, 8, 128), F32),
            dma((10,)),
            dma((CHUNKS,)),
            dma((CHUNKS,)),
            dma((4,)),
            dma((2, CHUNKS)),
            dma((2, CHUNKS)),
            dma((2, CHUNKS)),
            dma((2, CHUNKS)),
            dma((2,)),
            dma((2, 3)),
            dma((2, 3)),
            dma((4, 6)),
            dma((4, 6)),
            dma((3, 6)),
            dma((3, 6)),
            dma((3,)),
            dma((3,)),
        ],
        compiler_params=pltpu.CompilerParams(
            collective_id=0, has_side_effects=True, vmem_limit_bytes=62 * 1024 * 1024
        ),
    )(held, cot, w_in, w_out, c_in, c_out, gain_mix, bias_mix, gain_out, bias_out, forward, unpack, cos_seq, sin_seq)
    shape = (per_dev, local_len, features)
    vec = lambda n: jax.ShapeDtypeStruct((n,), F32)
    output, grad_inputs, grad_in, grad_out, grad_c_in, *others = pl.pallas_call(
        finish_kernel,
        in_specs=[anywhere] * 3 + [inside],
        out_specs=(anywhere,) * 4 + (inside,) * 6,
        out_shape=(
            jax.ShapeDtypeStruct(whole, F32),
            jax.ShapeDtypeStruct(whole, F32),
            jax.ShapeDtypeStruct((share, 4 * features), F32),
            jax.ShapeDtypeStruct((4 * share, features), F32),
            vec(4 * share),
        )
        + (vec(share),) * 5,
        scratch_shapes=[
            vm((2,) + whole, BF16),
            vm((2, 4, share, features), BF16),
            vm((2,) + whole, F32),
            vm((share, 4 * features), F32),
            vm((4 * share, features), F32),
            dma((1 + 2 * CHUNKS,)),
            dma((2 + 2 * CHUNKS,)),
        ],
        compiler_params=pltpu.CompilerParams(vmem_limit_bytes=60 * 1024 * 1024),
    )(out_low, gin_low, mats, vecs)
    output = jnp.swapaxes(output.reshape(shape), 0, 1)
    grad_inputs = jnp.swapaxes(grad_inputs.reshape(shape), 0, 1)
    return (output, grad_inputs, grad_in, grad_c_in, grad_out, *others)


def body(inputs, *rest):
    if lax.axis_size("seq") != 8 or lax.axis_size("item") != 4:
        return gather_body(inputs, *rest)
    return exchange_body(inputs, *rest)


def solution(mesh):
    placed = (
        P("seq", "item", None),
        P(),
        P(),
        P(),
        P(),
        P(),
        P(),
        P(),
        P(),
        P("seq", "item", None),
    )
    return jax.shard_map(
        body,
        mesh=mesh,
        in_specs=placed,
        out_specs=(
            P("seq", "item", None),
            P("seq", "item", None),
            P("seq", None),
            P("seq"),
            P("seq", None),
            P("seq"),
            P("seq"),
            P("seq"),
            P("seq"),
            P("seq"),
        ),
        check_vma=False,
    )
```

```python
import math

import jax
import jax.numpy as jnp
import numpy as np
from jax import lax
from jax.experimental import pallas as pl
from jax.experimental.pallas import tpu as pltpu
from jax.sharding import PartitionSpec as P


def table_block(row_ids, col_ids, period):
    products = row_ids[:, None] * col_ids[None, :] % period
    angles = products.astype(jnp.float32) * (2.0 * math.pi / period)
    return (jnp.cos(angles).astype(jnp.bfloat16), jnp.sin(angles).astype(jnp.bfloat16))


def plain_dot(left, right):
    return jnp.dot(left, right, preferred_element_type=jnp.float32)


def rows_dot(left, right):
    return lax.dot_general(
        left, right, (((0,), (0,)), ((), ())), preferred_element_type=jnp.float32
    )


def cols_dot(left, right):
    return lax.dot_general(
        left, right, (((1,), (1,)), ((), ())), preferred_element_type=jnp.float32
    )


def layer_norm(values, scales, shifts):
    average = jnp.mean(values, axis=-1, keepdims=True)
    centered = values - average
    variance = jnp.mean(centered * centered, axis=-1, keepdims=True)
    return centered * lax.rsqrt(variance + 1e-05) * scales + shifts


def gelu_exact(values):
    return jax.nn.gelu(values, approximate=False)


def gather_body(inputs, w_in, c_in, w_out, c_out, gain_mix, bias_mix, gain_out, bias_out, cotangent):
    local_len, per_dev, features = inputs.shape
    merged = per_dev * features
    period = local_len * lax.axis_size("seq")
    unit_scale = 1.0 / math.sqrt(period * features)
    own_rows = lax.axis_index("seq") * local_len + jnp.arange(local_len, dtype=jnp.int32)
    feat_ids = jnp.arange(features, dtype=jnp.int32)
    cos_hid, sin_hid = table_block(feat_ids, feat_ids, features)
    tokens = inputs.reshape(-1, features)
    tokens_low = tokens.astype(jnp.bfloat16)
    cos_part = (
        plain_dot(tokens_low, cos_hid).astype(jnp.bfloat16).reshape(local_len, per_dev, features)
    )
    sin_part = (
        plain_dot(tokens_low, sin_hid).astype(jnp.bfloat16).reshape(local_len, per_dev, features)
    )
    pieces = (
        lax.all_gather(cos_part, "seq", axis=0, tiled=True),
        lax.all_gather(sin_part, "seq", axis=0, tiled=True),
    )
    col_ids = jnp.arange(pieces[0].shape[0], dtype=jnp.int32)
    cos_blk, sin_blk = table_block(own_rows, col_ids, period)
    mixed = plain_dot(cos_blk, pieces[0].reshape(pieces[0].shape[0], -1)) - plain_dot(
        sin_blk, pieces[1].reshape(pieces[1].shape[0], -1)
    )
    mixed = (mixed * unit_scale).reshape(-1, features)
    hidden, pull_mix = jax.vjp(layer_norm, tokens + mixed, gain_mix, bias_mix)
    hidden_low = hidden.astype(jnp.bfloat16)
    w_in_low = w_in.astype(jnp.bfloat16)
    w_out_low = w_out.astype(jnp.bfloat16)
    pre = plain_dot(hidden_low, w_in_low) + c_in
    act, pull_gelu = jax.vjp(gelu_exact, pre)
    act_low = act.astype(jnp.bfloat16)
    branch = plain_dot(act_low, w_out_low) + c_out
    output, pull_out = jax.vjp(layer_norm, hidden + branch, gain_out, bias_out)
    g_sum2, grad_gain_out, grad_bias_out = pull_out(cotangent.reshape(-1, features))
    g_branch = g_sum2.astype(jnp.bfloat16)
    grad_c_out = jnp.sum(g_branch.astype(jnp.float32), axis=0)
    grad_w_out = rows_dot(act_low, g_branch)
    (g_act,) = pull_gelu(cols_dot(g_branch, w_out_low))
    g_pre = g_act.astype(jnp.bfloat16)
    grad_c_in = jnp.sum(g_pre.astype(jnp.float32), axis=0)
    grad_w_in = rows_dot(hidden_low, g_pre)
    g_hidden = g_sum2 + cols_dot(g_pre, w_in_low)
    g_sum1, grad_gain_mix, grad_bias_mix = pull_mix(g_hidden)
    g_mixed = g_sum1.astype(jnp.bfloat16).reshape(local_len, per_dev, features)
    empty = jnp.zeros((local_len, merged), jnp.float32)
    piece = lax.all_gather(g_mixed, "seq", axis=0, tiled=True)
    row_ids = jnp.arange(piece.shape[0], dtype=jnp.int32)
    cos_blk, sin_blk = table_block(row_ids, own_rows, period)
    flat = piece.reshape(piece.shape[0], -1)
    cycle_gc = rows_dot(cos_blk, flat)
    cycle_gs = (empty, empty)[1] - rows_dot(sin_blk, flat)
    g_cos = (cycle_gc * unit_scale).astype(jnp.bfloat16).reshape(-1, features)
    g_sin = (cycle_gs * unit_scale).astype(jnp.bfloat16).reshape(-1, features)
    grad_inputs = g_sum1 + cols_dot(g_cos, cos_hid) + cols_dot(g_sin, sin_hid)
    shards = (
        lax.psum_scatter(
            grad_w_in.astype(jnp.bfloat16), "seq", scatter_dimension=0, tiled=True
        ).astype(jnp.float32),
        lax.psum_scatter(
            grad_c_in.astype(jnp.bfloat16), "seq", scatter_dimension=0, tiled=True
        ).astype(jnp.float32),
        lax.psum_scatter(
            grad_w_out.astype(jnp.bfloat16), "seq", scatter_dimension=0, tiled=True
        ).astype(jnp.float32),
        lax.psum_scatter(
            grad_c_out.astype(jnp.bfloat16), "seq", scatter_dimension=0, tiled=True
        ).astype(jnp.float32),
        lax.psum_scatter(
            grad_gain_mix.astype(jnp.bfloat16), "seq", scatter_dimension=0, tiled=True
        ).astype(jnp.float32),
        lax.psum_scatter(
            grad_bias_mix.astype(jnp.bfloat16), "seq", scatter_dimension=0, tiled=True
        ).astype(jnp.float32),
        lax.psum_scatter(
            grad_gain_out.astype(jnp.bfloat16), "seq", scatter_dimension=0, tiled=True
        ).astype(jnp.float32),
        lax.psum_scatter(
            grad_bias_out.astype(jnp.bfloat16), "seq", scatter_dimension=0, tiled=True
        ).astype(jnp.float32),
    )
    summed = (
        lax.psum(shards[0].astype(jnp.bfloat16), "item").astype(jnp.float32),
        lax.psum(shards[1].astype(jnp.bfloat16), "item").astype(jnp.float32),
        lax.psum(shards[2].astype(jnp.bfloat16), "item").astype(jnp.float32),
        lax.psum(shards[3].astype(jnp.bfloat16), "item").astype(jnp.float32),
        lax.psum(shards[4].astype(jnp.bfloat16), "item").astype(jnp.float32),
        lax.psum(shards[5].astype(jnp.bfloat16), "item").astype(jnp.float32),
        lax.psum(shards[6].astype(jnp.bfloat16), "item").astype(jnp.float32),
        lax.psum(shards[7].astype(jnp.bfloat16), "item").astype(jnp.float32),
    )
    return (
        output.reshape(inputs.shape),
        grad_inputs.reshape(inputs.shape),
        summed[0],
        summed[1],
        summed[2],
        summed[3],
        summed[4],
        summed[5],
        summed[6],
        summed[7],
    )


def packed_tables(features, parts):
    half = features // 2
    share = half // parts
    index = np.arange(features)
    forward = np.zeros((features, features), np.float32)
    unpack = np.zeros((features, features), np.float32)
    for low in range(half):
        block, place = divmod(low, share)
        cos_slot = block * 2 * share + place
        sin_slot = cos_slot + share
        angles = (index * low % features).astype(np.float32) * np.float32(2.0 * math.pi / features)
        forward[cos_slot] = np.cos(angles)
        unpack[cos_slot, low] = 1.0
        if low:
            unpack[cos_slot, features - low] = 1.0
            forward[sin_slot] = np.sin(angles)
            unpack[sin_slot, low] = -1.0
            unpack[sin_slot, features - low] = 1.0
        else:
            forward[sin_slot] = 1.0 - 2.0 * (index % 2)
            unpack[sin_slot, half] = 1.0
    return forward.astype(jnp.bfloat16), unpack.astype(jnp.bfloat16)


def seq_tables(period):
    index = np.arange(period)
    angles = (index[:, None] * index[None, :] % period).astype(np.float32)
    angles = angles * np.float32(2.0 * math.pi / period)
    return np.cos(angles).astype(jnp.bfloat16), np.sin(angles).astype(jnp.bfloat16)


MESH = pl.DeviceIdType.MESH
CHUNKS = 3
BF16, F32 = jnp.bfloat16, jnp.float32


def dot(left, right, left_dim, right_dim):
    return lax.dot_general(
        left, right, (((left_dim,), (right_dim,)), ((), ())), preferred_element_type=F32
    )


def row_mean(values):
    return jnp.mean(values, axis=-1, keepdims=True)


def layer_kernel(
    x_hbm, cot_hbm, win_hbm, wout_hbm, cin_hbm, cout_hbm, gmix_hbm, bmix_hbm, gout_hbm, bout_hbm,
    fwd_hbm, unp_hbm, cos_hbm, sin_hbm,
    out_hbm, gin_hbm, gmat_ref, gvec_ref,
    cin_ref, cout_ref, gmix_ref, bmix_ref, gout_ref, bout_ref,
    fwd_v, unp_v, cos_v, sin_v, prm_v, xbuf, cotb, win_v, wout_v, stage,
    ysend, yrecv, zsend, zrecv, actb, gpb, hb, gbb, dgb, acc, r1b, ostage, vacc,
    recv1, hop0, hop1, hop2, hop3, vsend, vrecv, vmid, vlast,
    ld_sem, x_sem, cot_sem, stg_sem, a_send, a_recv, b_send, b_recv, out_sem,
    core_send, core_recv, red_send, red_recv, gat_send, gat_recv, v_send, v_recv,
):
    chunks, rows, features = xbuf.shape
    per_chunk, share, period = yrecv.shape[2], yrecv.shape[3], yrecv.shape[4]
    own_len = period // 8
    half = share // 2
    unit_scale = 1.0 / math.sqrt(period * features)

    me, item = lax.axis_index("seq"), lax.axis_index("item")
    peers = [(lax.rem(me + k, 8), item) for k in range(1, 8)]
    z_lo, y_at = lax.rem(lax.div(me, 2), 2), lax.rem(me, 2)
    z_at, z_hi = lax.div(me, 2), lax.div(me, 4)
    core, x_at = lax.rem(item, 2), lax.div(item, 2)
    core_peer = (me, item + 1 - 2 * core)
    x_peer = (me, item + 2 - 4 * x_at)
    far_peer = (me, lax.rem(item + 2, 4) + 1 - 2 * core)
    y_peer = (me + 1 - 2 * y_at, item)
    za_peer = (me + 2 - 4 * z_lo, item)
    zb_peer = (me + 4 - 8 * z_hi, item)

    def remote(src, dst, send, recv, peer):
        return pltpu.make_async_remote_copy(
            src_ref=src, dst_ref=dst, send_sem=send, recv_sem=recv, device_id=peer, device_id_type=MESH
        )

    def wait_bytes(ref, sem):
        pltpu.make_async_copy(ref, ref, sem).wait()

    tables = [
        pltpu.make_async_copy(src, dst, ld_sem.at[i])
        for i, (src, dst) in enumerate(
            [
                (fwd_hbm, fwd_v), (cos_hbm, cos_v), (sin_hbm, sin_v), (unp_hbm, unp_v),
                (cin_hbm, cin_ref), (cout_hbm, cout_ref), (gmix_hbm, gmix_ref),
                (bmix_hbm, bmix_ref), (gout_hbm, gout_ref), (bout_hbm, bout_ref),
            ]
        )
    ]
    x_loads = [pltpu.make_async_copy(x_hbm.at[c], xbuf.at[c], x_sem.at[c]) for c in range(chunks)]

    def cot_load(c):
        return pltpu.make_async_copy(cot_hbm.at[c], cotb.at[c], cot_sem.at[c])

    x_loads[0].start()
    tables[0].start()
    for load in x_loads[1:] + tables[1:]:
        load.start()

    barrier = pltpu.get_barrier_semaphore()
    everyone = peers + [core_peer, x_peer, far_peer]
    for peer in everyone:
        pl.semaphore_signal(barrier, inc=1, device_id=peer, device_id_type=MESH)

    slots, piece = stage.shape[0], stage.shape[1]
    per_block = features // piece
    steps = 8 * per_block

    def weight_load(step, part, slot):
        block, at = lax.div(step, per_block), lax.rem(step, per_block) * piece
        if part == 0:
            cols = pl.ds(pl.multiple_of(block * features, features), features)
            src = win_hbm.at[pl.ds(pl.multiple_of(at, piece), piece), cols]
        else:
            src = wout_hbm.at[pl.ds(pl.multiple_of(block * features + at, piece), piece), :]
        return pltpu.make_async_copy(src, stage.at[slot], stg_sem.at[slot])

    def cast_weights(part):
        total = 4 * per_block
        groups = piece // share

        def one(step, carry):
            slot = lax.rem(step, slots)
            weight_load(step, part, slot).wait()
            block, at = lax.div(step, per_block), lax.rem(step, per_block) * groups
            value = stage[slot].astype(BF16)
            for g in range(groups):
                where = at + g
                rows_of = value[g * share : (g + 1) * share]
                if part == 0:
                    win_v[block, lax.div(where, 2), lax.rem(where, 2)] = rows_of
                else:
                    wout_v[block, lax.div(where, 4), lax.rem(lax.div(where, 2), 2), lax.rem(where, 2)] = rows_of

            @pl.when(step + slots < total)
            def _():
                weight_load(step + slots, part, slot).start()

            return carry

        lax.fori_loop(0, total, one, 0)

    def first_loads(part):
        for slot in range(slots):
            weight_load(jnp.int32(slot), part, jnp.int32(slot)).start()

    def in_block(j):
        return win_v[j].reshape(features, features)

    def out_block(j):
        return wout_v[j].reshape(features, features)

    def pack(c, low):
        packed = dot(fwd_v[...], low, 1, 1).astype(BF16)
        for s in range(per_chunk):
            ysend[c, s] = packed[:, s * own_len : (s + 1) * own_len]

    def send_owners(way, c):
        mine = pl.ds(pl.multiple_of(me * own_len, own_len), own_len)
        for peer in peers:
            to = pl.ds(pl.multiple_of(peer[0] * share, share), share)
            remote(
                ysend.at[c, :, to, :], yrecv.at[way, c, :, :, mine], a_send.at[way, c], a_recv.at[way, c], peer
            ).start()
        own = pl.ds(pl.multiple_of(me * share, share), share)
        pltpu.make_async_copy(ysend.at[c, :, own, :], yrecv.at[way, c, :, :, mine], a_recv.at[way, c]).start()

    def owners_sent(way, c):
        wait_bytes(ysend.at[c, :, pl.ds(0, 7 * share), :], a_send.at[way, c])

    def turn(way, c):
        wait_bytes(yrecv.at[way, c], a_recv.at[way, c])
        held = yrecv[way, c]
        cos_rows = held[:, :half].reshape(per_chunk * half, period)
        sin_rows = held[:, half:].reshape(per_chunk * half, period)
        mid_rows = held[:, half : half + 16].reshape(per_chunk * 16, period)
        wide = period // 4
        top = lax.broadcasted_iota(jnp.int32, (16, wide), 0) == 0
        top = jnp.logical_and(top, me == 0)
        cos_rows = jnp.concatenate([cos_rows, mid_rows], axis=0)

        def one(n, carry):
            cols = pl.ds(pl.multiple_of(n * wide, wide), wide)
            by_cos = dot(cos_rows, cos_v[:, cols], 1, 0) * unit_scale
            by_sin = dot(sin_rows, sin_v[:, cols], 1, 0) * unit_scale
            for s in range(per_chunk):
                zsend[c, s, :half, cols] = by_cos[s * half : (s + 1) * half].astype(BF16)
                sin_part = by_sin[s * half : (s + 1) * half]
                at = per_chunk * half + s * 16
                zsend[c, s, half : half + 16, cols] = jnp.where(top, by_cos[at : at + 16], sin_part[:16]).astype(BF16)
                zsend[c, s, half + 16 :, cols] = sin_part[16:].astype(BF16)
            return carry

        lax.fori_loop(0, 4, one, 0)

    def send_back(way, c):
        mine = pl.ds(pl.multiple_of(me * share, share), share)
        for peer in peers:
            to = pl.ds(pl.multiple_of(peer[0] * own_len, own_len), own_len)
            remote(
                zsend.at[c, :, :, to], zrecv.at[c, :, mine, :], b_send.at[way, c], b_recv.at[way, c], peer
            ).start()
        own = pl.ds(pl.multiple_of(me * own_len, own_len), own_len)
        pltpu.make_async_copy(zsend.at[c, :, :, own], zrecv.at[c, :, mine, :], b_recv.at[way, c]).start()

    def return_sent(way, c):
        wait_bytes(zsend.at[c, :, :, pl.ds(0, 7 * own_len)], b_send.at[way, c])

    def mixed_of(c, way=0):
        wait_bytes(zrecv.at[c], b_recv.at[way, c])
        held = jnp.concatenate([zrecv[c, s] for s in range(per_chunk)], axis=1)
        return dot(held, unp_v[...], 0, 0)

    tables[0].wait()
    x_loads[0].wait()
    first_loads(0)
    pack(0, xbuf[0].astype(BF16))
    pl.semaphore_wait(barrier, len(everyone))
    send_owners(0, 0)
    x_loads[1].wait()
    pack(1, xbuf[1].astype(BF16))
    for c in range(chunks):
        cot_load(c).start()
    vacc[...] = jnp.zeros_like(vacc)
    for load in tables[4:]:
        load.wait()
    for j in range(4):
        prm_v[j : j + 1] = cin_ref[j * features : (j + 1) * features].reshape(1, features)
    for r, ref in enumerate((cout_ref, gmix_ref, bmix_ref, gout_ref, bout_ref)):
        prm_v[4 + r : 5 + r] = ref[...].reshape(1, features)
    cast_weights(0)
    first_loads(1)
    send_owners(0, 1)
    x_loads[2].wait()
    pack(2, xbuf[2].astype(BF16))
    cast_weights(1)
    for load in tables[1:4]:
        load.wait()
    turn(0, 0)
    send_back(0, 0)
    owners_sent(0, 0)
    owners_sent(0, 1)
    send_owners(0, 2)
    turn(0, 1)

    gain_mix, bias_mix = prm_v[5:6], prm_v[6:7]
    gain_out, bias_out, c_out = prm_v[7:8], prm_v[8:9], prm_v[4:5]

    def out_copy(c):
        return pltpu.make_async_copy(ostage, out_hbm.at[c], out_sem.at[0])

    def feed_up(c, mixed=None):
        value = xbuf[c] + (mixed_of(c) if mixed is None else mixed)
        value = value - row_mean(value)
        scale = lax.rsqrt(row_mean(value * value) + 1e-05)
        normal = value * scale
        r1b[...] = jnp.broadcast_to(scale, r1b.shape)
        xbuf[c] = normal
        hidden = normal * gain_mix + bias_mix
        hb[c] = hidden.astype(BF16)
        acc[...] = hidden + c_out

        def up(j, carry):
            pre = dot(hb[c], in_block(j), 1, 0) + prm_v[pl.ds(j, 1)]
            prob = 0.5 + 0.5 * lax.erf(pre * math.sqrt(0.5))
            density = jnp.exp(-0.5 * pre * pre) * (1.0 / math.sqrt(2.0 * math.pi))
            act = (pre * prob).astype(BF16)
            dgb[j] = prob + pre * density
            actb[j, c] = act
            acc[...] += dot(act, out_block(j), 1, 0)
            return carry

        lax.fori_loop(0, 4, up, 0, unroll=True)

    def feed_mid(c):
        value = acc[...]
        value = value - row_mean(value)
        scale = lax.rsqrt(row_mean(value * value) + 1e-05)
        normal = value * scale


        @pl.when(c > 0)
        def _():
            out_copy(c - 1).wait()

        ostage[...] = (normal * gain_out + bias_out).astype(BF16)
        out_copy(c).start()
        cot_load(c).wait()
        cot = cotb[c]
        vacc[7:8] += jnp.sum(cot * normal, axis=0, keepdims=True)
        vacc[8:9] += jnp.sum(cot, axis=0, keepdims=True)
        scaled = cot * gain_out
        g_sum2 = scale * (scaled - row_mean(scaled) - normal * row_mean(scaled * normal))
        low = g_sum2.astype(BF16)
        gbb[c] = low
        vacc[4:5] += jnp.sum(low.astype(F32), axis=0, keepdims=True)
        acc[...] = g_sum2

    def feed_down(c):
        for j in range(4):
            g_pre = (dot(gbb[c], out_block(j), 1, 1) * dgb[j]).astype(BF16)
            gpb[j, c] = g_pre
            vacc[j : j + 1] += jnp.sum(g_pre.astype(F32), axis=0, keepdims=True)

    def feed_end(c):
        for j in range(4):
            acc[...] += dot(gpb[j, c], in_block(j), 1, 1)
        g_hidden = acc[...]
        normal = xbuf[c]
        vacc[5:6] += jnp.sum(g_hidden * normal, axis=0, keepdims=True)
        vacc[6:7] += jnp.sum(g_hidden, axis=0, keepdims=True)
        scaled = g_hidden * gain_mix
        g_sum1 = r1b[:, :1] * (scaled - row_mean(scaled) - normal * row_mean(scaled * normal))
        xbuf[c] = g_sum1
        pack(c, g_sum1.astype(BF16))

    cut = hop3.shape[3]
    routes = ('xyz', 'xzy', 'xyz', 'xzy', 'yxz', 'yxz')
    z_pair = lax.rem(z_at + 2, 4)
    z_next = z_at + 1 - 2 * z_lo
    z_far = lax.rem(z_next + 2, 4)

    def part(p):
        return pl.ds((p % 3) * cut, cut)

    def add(*terms):
        total = terms[0].astype(F32)
        for term in terms[1:]:
            total = total + term.astype(F32)
        return total.astype(BF16)

    def product(p):
        kind, h, at = p // 3, p % 3, part(p)

        def one_in(i, carry):
            x = lax.rem(i, 2)
            q = jnp.where(i < 2, 2 * x + 1 - core, 2 * x + core)
            grad = dot(hb[...].reshape(-1, features), gpb[q, :, :, at].reshape(-1, cut), 0, 0)
            win_v[q, :, :, :, at] = grad.astype(BF16).reshape(4, 2, share, cut)

            @pl.when(i < 2)
            def _():
                remote(
                    win_v.at[2 * x + 1 - core, :, :, :, at], recv1.at[0, h, x],
                    core_send.at[0, h], core_recv.at[0, h], core_peer,
                ).start()

            return carry

        def one_out(j, carry):
            grad = dot(actb[j].reshape(-1, features), gbb[:, :, at].reshape(-1, cut), 0, 0)
            wout_v[j, :, :, :, :, at] = grad.astype(BF16).reshape(2, 2, 2, share, cut)
            return carry

        if kind == 0:
            lax.fori_loop(0, 4, one_in, 0)
        else:
            lax.fori_loop(0, 4, one_out, 0)
            for x in range(2):
                remote(
                    wout_v.at[:, :, x, 1 - core, :, at], recv1.at[1, h, x], core_send.at[1, h], core_recv.at[1, h], core_peer
                ).start()

    def hop(p, step):
        kind, h, at = p // 3, p % 3, part(p)
        legs = routes[p].replace("z", "ab")
        past = legs[:step]
        grads = (win_v, wout_v)[kind]
        landing = (hop0, hop1, hop2, hop3)
        if step == 0:
            wait_bytes(recv1.at[kind, h], core_recv.at[kind, h])
        else:
            wait_bytes(landing[step - 1].at[p], red_recv.at[step - 1, p])

        def place(x, z, y):
            return (2 * x + core, z, y, slice(None), at) if kind == 0 else (z, y, x, core, slice(None), at)

        def arrived(x, z, y, rows_at=slice(None)):
            if step == 0:
                return recv1[kind, h, x, z, y, rows_at]
            count_z = 1 if "b" in past else 2 if "a" in past else 4
            count_y = 1 if "y" in past else 2
            slot = (0 if "x" in past else x * count_z) + zslot(z)
            if isinstance(y, slice):
                return landing[step - 1][p, pl.ds(slot * 2, 2), rows_at]
            return landing[step - 1][p, slot * count_y + (0 if count_y == 1 else y), rows_at]

        def zslot(z):
            if "a" not in past:
                return z
            return 0 if z is z_at else 1

        both_y = slice(None)
        xs = (x_at,) if "x" in past else (0, 1)
        ys = (y_at,) if "y" in past else (both_y,)
        zs = (z_at,) if "b" in past else (z_at, z_pair) if "a" in past else tuple(range(4))

        def put(x, z, y):
            def rows_of(r, carry):
                rows_at = pl.ds(pl.multiple_of(r * 32, 32), 32)
                where = place(x, z, y)
                where = where[:-2] + (rows_at, at)
                grads[where] = add(grads[where], arrived(x, z, y, rows_at))
                return carry

            lax.fori_loop(0, share // 32, rows_of, 0)

        if step == 4:
            where = place(x_at, z_at, y_at)
            finish(p, add(grads[where], arrived(x_at, z_at, y_at)))
            return
        leg = legs[step]
        if leg == "x":
            away, keep, peer = [(1 - x_at, z, y) for z in zs for y in ys], [(x_at, z, y) for z in zs for y in ys], x_peer
        elif leg == "y":
            away, keep, peer = [(x, z, 1 - y_at) for x in xs for z in zs], [(x, z, y_at) for x in xs for z in zs], y_peer
        elif leg == "a":
            away = [(x, z, y) for x in xs for z in (z_next, z_far) for y in ys]
            keep, peer = [(x, z, y) for x in xs for z in (z_at, z_pair) for y in ys], za_peer
        else:
            away, keep, peer = [(x, z_pair, y) for x in xs for y in ys], [(x, z_at, y) for x in xs for y in ys], zb_peer
        for x, z, y in away:
            put(x, z, y)
        for count, (x, z, y) in enumerate(away):
            width = 2 if isinstance(y, slice) else 1
            dst = landing[step].at[p, pl.ds(count * 2, 2)] if width == 2 else landing[step].at[p, count]
            remote(grads.at[place(x, z, y)], dst, red_send.at[step, p], red_recv.at[step, p], peer).start()
        for x, z, y in keep:
            put(x, z, y)

    def finish(p, total):
        kind, at = p // 3, part(p)
        gmat_ref[kind, item, :, at] = total
        here = gmat_ref.at[kind, item, :, at]
        remote(here, here, gat_send.at[1, p], gat_recv.at[1, p], x_peer).start()
        remote(here, here, gat_send.at[0, p], gat_recv.at[0, p], core_peer).start()
        if p in (1, 4, 5):
            remote(here, here, gat_send.at[2, p], gat_recv.at[2, p], far_peer).start()

    def forward_on(p):
        there = gmat_ref.at[p // 3, x_peer[1], :, part(p)]
        wait_bytes(there, gat_recv.at[1, p])
        if p not in (1, 4, 5):
            remote(there, there, gat_send.at[2, p], gat_recv.at[2, p], core_peer).start()

    def final(c):
        hb[c] = (xbuf[c] + mixed_of(c, 1)).astype(BF16)
        pltpu.make_async_copy(hb.at[c], gin_hbm.at[c], out_sem.at[1]).start()

    def vectors_out():
        lanes = vsend.shape[2]
        vsend[...] = jnp.zeros_like(vsend)
        for d in range(8):
            at = d * (features // 2)
            for r in range(3):
                where = at + r * lanes
                vsend[d, r : r + 1, :] = vacc[where // features : where // features + 1, where % features : where % features + lanes]
            for r in range(5):
                vsend[d, 3 + r : 4 + r, :share] = vacc[4 + r : 5 + r, d * share : (d + 1) * share]
        for peer in peers:
            remote(vsend.at[peer[0]], vrecv.at[me], v_send.at[0], v_recv.at[0], peer).start()
        pltpu.make_async_copy(vsend.at[me], vrecv.at[me], v_recv.at[0]).start()

    def vectors_on():
        wait_bytes(vrecv, v_recv.at[0])
        vmid[...] = jnp.sum(vrecv[...], axis=0)
        remote(vmid, vlast.at[0], v_send.at[1], v_recv.at[1], core_peer).start()

    def vectors_over():
        wait_bytes(vlast.at[0], v_recv.at[1])
        vlast[1] = vmid[...] + vlast[0]
        remote(vlast.at[1], vlast.at[2], v_send.at[2], v_recv.at[2], x_peer).start()

    def vectors_end():
        wait_bytes(vlast.at[2], v_recv.at[2])
        gvec_ref[...] = vlast[1] + vlast[2]

    def feed(c, carry):
        feed_up(c)

        @pl.when(c == 0)
        def _():
            send_back(0, 1)
            owners_sent(0, 2)

        feed_mid(c)

        @pl.when(c == 0)
        def _():
            turn(0, 2)
            send_back(0, 2)

        feed_down(c)

        @pl.when(c == chunks - 1)
        def _():
            product(3)
            return_sent(0, 0)
            turn(1, 0)
            send_back(1, 0)
            product(4)
            hop(3, 0)

        feed_end(c)

        @pl.when(c == 0)
        def _():
            send_owners(1, 0)

        @pl.when(c == 1)
        def _():
            send_owners(1, 1)

        return carry

    lax.fori_loop(0, chunks, feed, 0)
    vectors_out()
    hop(4, 0)
    send_owners(1, 2)
    product(0)
    product(1)
    hop(0, 0)
    hop(1, 0)
    hop(3, 1)
    return_sent(0, 1)
    turn(1, 1)
    send_back(1, 1)
    product(2)
    product(5)
    hop(3, 2)
    hop(0, 1)
    vectors_on()
    vectors_over()
    hop(5, 0)
    return_sent(0, 2)
    turn(1, 2)
    send_back(1, 2)
    final(0)
    hop(2, 0)
    hop(4, 1)
    hop(1, 1)
    hop(0, 2)
    hop(5, 1)
    hop(2, 1)
    hop(3, 3)
    hop(1, 2)
    hop(4, 2)
    hop(0, 3)
    hop(2, 2)
    hop(3, 4)
    hop(5, 2)
    hop(4, 3)
    final(1)
    hop(1, 3)
    hop(2, 3)
    forward_on(3)
    hop(0, 4)
    hop(5, 3)
    hop(1, 4)
    hop(4, 4)
    hop(2, 4)
    hop(5, 4)
    vectors_end()
    final(2)
    forward_on(2)
    forward_on(0)
    forward_on(1)
    forward_on(4)
    forward_on(5)

    out_copy(chunks - 1).wait()
    wait_bytes(hb, out_sem.at[1])
    for c in range(chunks):
        owners_sent(1, c)
        return_sent(1, c)
    for kind in range(2):
        for h in range(3):
            wait_bytes(recv1.at[kind, h], core_send.at[kind, h])
    for p in range(6):
        for step, ref in enumerate((hop0, hop1, hop2, hop3)):
            wait_bytes(ref.at[p], red_send.at[step, p])
        for leg in range(3):
            wait_bytes(hop3.at[p], gat_send.at[leg, p])
        wait_bytes(hop3.at[p], gat_recv.at[0, p])
        wait_bytes(hop3.at[p], gat_recv.at[2, p])
    wait_bytes(vrecv.at[pl.ds(0, 7)], v_send.at[0])
    wait_bytes(vlast.at[1], v_send.at[1])
    wait_bytes(vlast.at[1], v_send.at[2])


def finish_kernel(
    out_in, gin_in, gmat_in, gvec_in,
    out_ref, gin_ref, gwi_ref, gwo_ref, gci_ref, gco_ref, ggm_ref, gbm_ref, ggo_ref, gbo_ref,
    low, mv, res, wi, wo, sem_in, sem_out,
):
    chunks, features, share = low.shape[1], low.shape[3], mv.shape[2]
    loads = [pltpu.make_async_copy(gmat_in, mv, sem_in.at[0])]
    for k, src in enumerate((out_in, gin_in)):
        for c in range(chunks):
            loads.append(pltpu.make_async_copy(src.at[c], low.at[k, c], sem_in.at[len(loads)]))
    for load in loads[1:] + loads[:1]:
        load.start()
    stores = []

    def put(src, dst):
        copy = pltpu.make_async_copy(src, dst, sem_out.at[len(stores)])
        copy.start()
        stores.append(copy)

    for k, dst in enumerate((out_ref, gin_ref)):
        for c in range(chunks):
            loads[1 + k * chunks + c].wait()
            res[k, c] = low[k, c].astype(F32)
            put(res.at[k, c], dst.at[c])
    loads[0].wait()
    for q in range(4):
        wi[:, q * features : (q + 1) * features] = mv[0, q].astype(F32)
        wo[q * share : (q + 1) * share] = mv[1, q].astype(F32)
    put(wi, gwi_ref)
    put(wo, gwo_ref)
    lanes = gvec_in.shape[1]
    for r in range(3):
        gci_ref[r * lanes : (r + 1) * lanes] = gvec_in[r]
    for r, ref in enumerate((gco_ref, ggm_ref, gbm_ref, ggo_ref, gbo_ref)):
        ref[...] = gvec_in[3 + r, :share]
    for copy in stores:
        copy.wait()


def exchange_body(inputs, w_in, c_in, w_out, c_out, gain_mix, bias_mix, gain_out, bias_out, cotangent):
    local_len, per_dev, features = inputs.shape
    parts = lax.axis_size("seq")
    period = local_len * parts
    share = features // parts
    per_chunk = per_dev // CHUNKS
    rows = per_chunk * local_len
    forward, unpack = packed_tables(features, parts)
    cos_seq, sin_seq = seq_tables(period)
    held = jnp.swapaxes(inputs, 0, 1).reshape(CHUNKS, rows, features)
    cot = jnp.swapaxes(cotangent, 0, 1).reshape(CHUNKS, rows, features)
    anywhere = pl.BlockSpec(memory_space=pl.ANY)
    whole = (CHUNKS, rows, features)
    vm, dma = pltpu.VMEM, pltpu.SemaphoreType.DMA
    inside = pl.BlockSpec(memory_space=pltpu.VMEM)
    out_low, gin_low, mats, vecs = pl.pallas_call(
        layer_kernel,
        out_shape=(
            jax.ShapeDtypeStruct(whole, BF16),
            jax.ShapeDtypeStruct(whole, BF16),
            jax.ShapeDtypeStruct((2, 4, share, features), BF16),
            jax.ShapeDtypeStruct((8, 128), F32),
        ),
        in_specs=[anywhere] * 14,
        out_specs=(anywhere, anywhere, inside, inside),
        scratch_shapes=[
            vm((4 * features,), F32),
            vm((features,), F32),
            vm((features,), F32),
            vm((features,), F32),
            vm((features,), F32),
            vm((features,), F32),
            vm((features, features), BF16),
            vm((features, features), BF16),
            vm((period, period), BF16),
            vm((period, period), BF16),
            vm((16, features), F32),
            vm(whole, F32),
            vm(whole, F32),
            vm((4, 4, 2, share, features), BF16),
            vm((4, 2, 2, 2, share, features), BF16),
            vm((4, 192, features), F32),
            vm((CHUNKS, per_chunk, features, local_len), BF16),
            vm((2, CHUNKS, per_chunk, share, period), BF16),
            vm((CHUNKS, per_chunk, share, period), BF16),
            vm((CHUNKS, per_chunk, features, local_len), BF16),
            vm((4,) + whole, BF16),
            vm((4,) + whole, BF16),
            vm(whole, BF16),
            vm(whole, BF16),
            vm((4, rows, features), F32),
            vm((rows, features), F32),
            vm((rows, 128), F32),
            vm((rows, features), BF16),
            vm((16, features), F32),
            vm((2, 3, 2, 4, 2, share, features // 3), BF16),
            vm((6, 8, share, features // 3), BF16),
            vm((6, 4, share, features // 3), BF16),
            vm((6, 2, share, features // 3), BF16),
            vm((6, 1, share, features // 3), BF16),
            vm((8, 8, 128), F32),
            vm((8, 8, 128), F32),
            vm((8, 128), F32),
            vm((3, 8, 128), F32),
            dma((10,)),
            dma((CHUNKS,)),
            dma((CHUNKS,)),
            dma((4,)),
            dma((2, CHUNKS)),
            dma((2, CHUNKS)),
            dma((2, CHUNKS)),
            dma((2, CHUNKS)),
            dma((2,)),
            dma((2, 3)),
            dma((2, 3)),
            dma((4, 6)),
            dma((4, 6)),
            dma((3, 6)),
            dma((3, 6)),
            dma((3,)),
            dma((3,)),
        ],
        compiler_params=pltpu.CompilerParams(
            collective_id=0, has_side_effects=True, vmem_limit_bytes=62 * 1024 * 1024
        ),
    )(held, cot, w_in, w_out, c_in, c_out, gain_mix, bias_mix, gain_out, bias_out, forward, unpack, cos_seq, sin_seq)
    shape = (per_dev, local_len, features)
    vec = lambda n: jax.ShapeDtypeStruct((n,), F32)
    output, grad_inputs, grad_in, grad_out, grad_c_in, *others = pl.pallas_call(
        finish_kernel,
        in_specs=[anywhere] * 3 + [inside],
        out_specs=(anywhere,) * 4 + (inside,) * 6,
        out_shape=(
            jax.ShapeDtypeStruct(whole, F32),
            jax.ShapeDtypeStruct(whole, F32),
            jax.ShapeDtypeStruct((share, 4 * features), F32),
            jax.ShapeDtypeStruct((4 * share, features), F32),
            vec(4 * share),
        )
        + (vec(share),) * 5,
        scratch_shapes=[
            vm((2,) + whole, BF16),
            vm((2, 4, share, features), BF16),
            vm((2,) + whole, F32),
            vm((share, 4 * features), F32),
            vm((4 * share, features), F32),
            dma((1 + 2 * CHUNKS,)),
            dma((2 + 2 * CHUNKS,)),
        ],
        compiler_params=pltpu.CompilerParams(vmem_limit_bytes=60 * 1024 * 1024),
    )(out_low, gin_low, mats, vecs)
    output = jnp.swapaxes(output.reshape(shape), 0, 1)
    grad_inputs = jnp.swapaxes(grad_inputs.reshape(shape), 0, 1)
    return (output, grad_inputs, grad_in, grad_c_in, grad_out, *others)


def body(inputs, *rest):
    if lax.axis_size("seq") != 8 or lax.axis_size("item") != 4:
        return gather_body(inputs, *rest)
    return exchange_body(inputs, *rest)


def solution(mesh):
    placed = (
        P("seq", "item", None),
        P(),
        P(),
        P(),
        P(),
        P(),
        P(),
        P(),
        P(),
        P("seq", "item", None),
    )
    return jax.shard_map(
        body,
        mesh=mesh,
        in_specs=placed,
        out_specs=(
            P("seq", "item", None),
            P("seq", "item", None),
            P("seq", None),
            P("seq"),
            P("seq", None),
            P("seq"),
            P("seq"),
            P("seq"),
            P("seq"),
            P("seq"),
        ),
        check_vma=False,
    )
```
